32 devices in a mesh: shard: 4 (over z), dp: 4 (over y, x), mp: 2 (over core).
Axes of the slice: x: 2, y: 2, z: 4, core: 2. Of those that a mesh axis runs over, the one named last changes fastest.
Arguments:
- tokens_in: bfloat16 [2048, 2560], P(('shard', 'dp')), may hold values from -6 to 6
- segment_ids: int32 [2048], P(('shard', 'dp')), may hold values from 0 to 3, never falling along the last dimension, each value on 1 to 1024 neighbouring positions
- block_cotangent: bfloat16 [2048, 2560], P(('shard', 'dp')), may hold values from -6 to 6
- query_weight: bfloat16 [2560, 2560], P(('shard', 'dp'), 'mp'), may hold values from -0.125 to 0.125
- keyval_weight: bfloat16 [2560, 512], P(('shard', 'dp')), may hold values from -0.125 to 0.125
- outproj_weight: bfloat16 [2560, 2560], P('mp', ('shard', 'dp')), may hold values from -2 to 2
- gateup_weight: bfloat16 [2560, 2, 7680], P(('shard', 'dp'), None, 'mp'), may hold values from -0.125 to 0.125
- down_weight: bfloat16 [7680, 2560], P('mp', ('shard', 'dp')), may hold values from -0.0625 to 0.0625
- norm_gains: bfloat16 [2, 2560], P(None, ('shard', 'dp')), may hold values from 0.5 to 1.5
- query_first: float32 [2560, 2560], P(('shard', 'dp'), 'mp'), may hold values from -40 to 40
- keyval_first: float32 [2560, 512], P(('shard', 'dp')), may hold values from -96 to 96
- outproj_first: float32 [2560, 2560], P('mp', ('shard', 'dp')), may hold values from -3 to 3
- gateup_first: float32 [2560, 2, 7680], P(('shard', 'dp'), None, 'mp'), may hold values from -12 to 12
- down_first: float32 [7680, 2560], P('mp', ('shard', 'dp')), may hold values from -20 to 20
- gains_first: float32 [2, 2560], P(None, ('shard', 'dp')), may hold values from -40 to 40
- query_second: float32 [2560, 2560], P(('shard', 'dp'), 'mp'), may hold values from 65.536 to 491.52
- keyval_second: float32 [2560, 512], P(('shard', 'dp')), may hold values from 409.6 to 3072
- outproj_second: float32 [2560, 2560], P('mp', ('shard', 'dp')), may hold values from 0.4096 to 3.072
- gateup_second: float32 [2560, 2, 7680], P(('shard', 'dp'), None, 'mp'), may hold values from 6.144 to 45.056
- down_second: float32 [7680, 2560], P('mp', ('shard', 'dp')), may hold values from 16.384 to 122.88
- gains_second: float32 [2, 2560], P(None, ('shard', 'dp')), may hold values from 65.536 to 491.52
- step_count: int32 [1], replicated, may hold values from 1 to 20
Outputs:
- block_out: bfloat16 [2048, 2560], P(('shard', 'dp'))
- input_grad: float32 [2048, 2560], P(('shard', 'dp'))
- query_grad: float32 [2560, 2560], P(('shard', 'dp'), 'mp')
- keyval_grad: float32 [2560, 512], P(('shard', 'dp'))
- outproj_grad: float32 [2560, 2560], P('mp', ('shard', 'dp'))
- gateup_grad: float32 [2560, 2, 7680], P(('shard', 'dp'), None, 'mp')
- down_grad: float32 [7680, 2560], P('mp', ('shard', 'dp'))
- gains_grad: float32 [2, 2560], P(None, ('shard', 'dp'))
- query_first_new: float32 [2560, 2560], P(('shard', 'dp'), 'mp')
- keyval_first_new: float32 [2560, 512], P(('shard', 'dp'))
- outproj_first_new: float32 [2560, 2560], P('mp', ('shard', 'dp'))
- gateup_first_new: float32 [2560, 2, 7680], P(('shard', 'dp'), None, 'mp')
- down_first_new: float32 [7680, 2560], P('mp', ('shard', 'dp'))
- gains_first_new: float32 [2, 2560], P(None, ('shard', 'dp'))
- query_second_new: float32 [2560, 2560], P(('shard', 'dp'), 'mp')
- keyval_second_new: float32 [2560, 512], P(('shard', 'dp'))
- outproj_second_new: float32 [2560, 2560], P('mp', ('shard', 'dp'))
- gateup_second_new: float32 [2560, 2, 7680], P(('shard', 'dp'), None, 'mp')
- down_second_new: float32 [7680, 2560], P('mp', ('shard', 'dp'))
- gains_second_new: float32 [2, 2560], P(None, ('shard', 'dp'))
- query_update: float32 [2560, 2560], P(('shard', 'dp'), 'mp')
- keyval_update: float32 [2560, 512], P(('shard', 'dp'))
- outproj_update: float32 [2560, 2560], P('mp', ('shard', 'dp'))
- gateup_update: float32 [2560, 2, 7680], P(('shard', 'dp'), None, 'mp')
- down_update: float32 [7680, 2560], P('mp', ('shard', 'dp'))
- gains_update: float32 [2, 2560], P(None, ('shard', 'dp'))
The draws below stay inside these ranges and needn't reach their ends.
Inputs may be any that keep to these rules, and one draw needn't show every extreme that they name: `segment_ids`: segment ids never fall along the tokens; every document has 1 to 1024 tokens and one has exactly 1024.
All inputs are finite; a program needn't handle non-finite values.
Results may differ from the reference program's by a relative error of at most 0.028.
Values may be sent and summed in bfloat16 or wider, within the bound.
A program may use at most 576 MiB of HBM per device.

```python
import math
import jax
import jax.numpy as jnp
import numpy as np
from jax import lax

D = 2560
HEADS = 10
HEAD_DIM = 256
FF = 7680
TOK_DEV = 128
SEQ = 1024
TOKENS = 2048
SEGS = 4
KV_BLOCKS = 8


def strengthened(drawn, stream_key, source, target, parts, factor):
    owner, partner = [(jnp.arange(drawn.shape[axis_at]) // (drawn.shape[axis_at] // parts)).reshape([-1 if axis == axis_at else 1 for axis in range(drawn.ndim)]) for axis_at in (source, target)]
    chosen = jax.random.permutation(stream_key, parts)[partner]
    strong = (owner == chosen) | (owner == (partner + parts // 2) % parts)
    return jnp.where(strong, factor * drawn, drawn)


def level_of(own_key, dims, shards, low, high):
    def one(dim, blocks):
        draws = jax.random.uniform(jax.random.fold_in(jax.random.fold_in(own_key, 6), dim), (blocks,), jnp.float32, low / len(shards), high / len(shards))
        return jnp.repeat(jnp.exp(draws), dims[dim] // blocks).reshape((-1,) + (1,) * (len(dims) - dim - 1))

    factor_of = one(*shards[0])
    for cut in shards[1:]:
        factor_of = factor_of * one(*cut)
    return factor_of


def split_up(amount, total, bound, lean):
    loads = [(1 << 20) // math.isqrt(grade ** lean) + 1 for grade in range(2, amount + 1)]
    rest, holding = total - bound - (amount - 1), [1] * (amount - 1)
    while rest > 0:
        free = [i for i in range(amount - 1) if holding[i] < bound]
        whole, left = sum([loads[i] for i in free]), rest
        for i in free:
            extra = min(bound - holding[i], max(1, left * loads[i] // whole), rest)
            holding[i] = holding[i] + extra
            rest = rest - extra
    return np.array([bound] + holding)


def ragged(rng, count, total, bound, slope):
    if count == 2:
        one = jax.random.randint(rng, (), max(1, total - bound), min(bound, total - 1) + 1)
        return jnp.stack([one, total - one])
    tallies = jnp.asarray(split_up(count, total, bound, slope), jnp.int32)
    twos = (count - 1) // 2
    source_of, receiver = tallies[1:1 + 2 * twos:2], tallies[2:2 + 2 * twos:2]
    room = jnp.minimum(source_of - 1, bound - receiver)
    moved = jax.random.randint(jax.random.fold_in(rng, 1), (twos,), 0, 1 << 20) % (room + 1)
    tallies = tallies.at[1:1 + 2 * twos:2].set(source_of - moved).at[2:2 + 2 * twos:2].set(receiver + moved)
    return tallies[jax.random.permutation(jax.random.fold_in(rng, 2), count)]


def normal_values(own_key, dims, spread, bound, split=(), held_as=jnp.bfloat16):
    gain = level_of(own_key, dims, split, -0.22, 0.18) if split else 1.0
    drawn = jax.random.normal(own_key, dims, jnp.float32) * spread * gain
    return jnp.minimum(jnp.maximum(drawn, -bound), bound).astype(held_as)


def bell_draw_with(own_key, dims, width, limit, split, heavy, kind=jnp.bfloat16):
    values = width * jax.random.normal(own_key, dims, jnp.float32)
    if split:
        values = values * level_of(own_key, dims, split, -0.22, 0.18)
    return jnp.clip(strengthened(values, jax.random.fold_in(own_key, 3), *heavy), -limit, limit).astype(kind)


def setup_inputs(seed: int = 0) -> dict:
    keys = jax.random.split(jax.random.key(seed), 23)
    tokens_in = bell_draw_with(keys[0], (TOKENS, D), 1.0, 6.0, ((0, 16),), (0, 1, 16, 2.0))
    segment_ids = jnp.searchsorted(jnp.cumsum(ragged(keys[1], SEGS, TOKENS, SEQ, 2)), jnp.arange(TOKENS), side="right").astype(jnp.int32)
    block_cotangent = bell_draw_with(keys[2], (TOKENS, D), 1.0, 6.0, ((0, 16),), (0, 1, 16, 2.0))
    query_weight = normal_values(keys[3], (D, HEADS * HEAD_DIM), D ** -0.5, 0.125, ((0, 16), (1, 2)))
    keyval_weight = normal_values(keys[4], (D, 2 * HEAD_DIM), D ** -0.5, 0.125, ((0, 16),))
    outproj_weight = normal_values(keys[5], (HEADS * HEAD_DIM, D), (max(4, HEADS * HEAD_DIM // 256)) ** -0.5, 2.0, ((0, 2), (1, 16)))
    gateup_weight = normal_values(keys[6], (D, 2, FF), D ** -0.5, 0.125, ((0, 16), (2, 2)))
    down_weight = normal_values(keys[7], (FF, D), FF ** -0.5, 0.0625, ((0, 2), (1, 16)))
    norm_gains = jnp.clip(1.0 + 0.1 * jax.random.normal(keys[8], (2, D), jnp.float32), 0.5, 1.5).astype(jnp.bfloat16)
    query_first = normal_values(keys[9], (D, HEADS * HEAD_DIM), (0.14 * TOKENS ** 0.5), 40.0, ((0, 16), (1, 2)), jnp.float32)
    keyval_first = normal_values(keys[10], (D, 2 * HEAD_DIM), (0.35 * TOKENS ** 0.5), 96.0, ((0, 16),), jnp.float32)
    outproj_first = normal_values(keys[11], (HEADS * HEAD_DIM, D), (0.011 * TOKENS ** 0.5), 3.0, ((0, 2), (1, 16)), jnp.float32)
    gateup_first = normal_values(keys[12], (D, 2, FF), (0.042 * TOKENS ** 0.5), 12.0, ((0, 16), (2, 2)), jnp.float32)
    down_first = normal_values(keys[13], (FF, D), (0.07 * TOKENS ** 0.5), 20.0, ((0, 2), (1, 16)), jnp.float32)
    gains_first = normal_values(keys[14], (2, D), (0.14 * TOKENS ** 0.5), 40.0, ((1, 16),), jnp.float32)
    query_second = jnp.clip(jnp.exp(math.log(491.52) - 2.014903 * jax.random.uniform(keys[15], (D, HEADS * HEAD_DIM), jnp.float32) ** level_of(keys[15], (D, HEADS * HEAD_DIM), ((0, 16), (1, 2)), -0.2, 0.2)), 65.536, 491.52)
    keyval_second = jnp.clip(jnp.exp(math.log(3072.0) - 2.014903 * jax.random.uniform(keys[16], (D, 2 * HEAD_DIM), jnp.float32) ** level_of(keys[16], (D, 2 * HEAD_DIM), ((0, 16),), -0.2, 0.2)), 409.6, 3072.0)
    outproj_second = jnp.clip(jnp.exp(math.log(3.072) - 2.014903 * jax.random.uniform(keys[17], (HEADS * HEAD_DIM, D), jnp.float32) ** level_of(keys[17], (HEADS * HEAD_DIM, D), ((0, 2), (1, 16)), -0.2, 0.2)), 0.4096, 3.072)
    gateup_second = jnp.clip(jnp.exp(math.log(45.056) - 1.9924302 * jax.random.uniform(keys[18], (D, 2, FF), jnp.float32) ** level_of(keys[18], (D, 2, FF), ((0, 16), (2, 2)), -0.2, 0.2)), 6.144, 45.056)
    down_second = jnp.clip(jnp.exp(math.log(122.88) - 2.014903 * jax.random.uniform(keys[19], (FF, D), jnp.float32) ** level_of(keys[19], (FF, D), ((0, 2), (1, 16)), -0.2, 0.2)), 16.384, 122.88)
    gains_second = jnp.clip(jnp.exp(math.log(491.52) - 2.014903 * jax.random.uniform(keys[20], (2, D), jnp.float32) ** level_of(keys[20], (2, D), ((1, 16),), -0.2, 0.2)), 65.536, 491.52)
    step_count = jax.random.randint(keys[21], (1,), 1, 21).astype(jnp.int32)
    return dict(tokens_in=tokens_in, segment_ids=segment_ids, block_cotangent=block_cotangent, query_weight=query_weight, keyval_weight=keyval_weight, outproj_weight=outproj_weight, gateup_weight=gateup_weight, down_weight=down_weight, norm_gains=norm_gains, query_first=query_first, keyval_first=keyval_first, outproj_first=outproj_first, gateup_first=gateup_first, down_first=down_first, gains_first=gains_first, query_second=query_second, keyval_second=keyval_second, outproj_second=outproj_second, gateup_second=gateup_second, down_second=down_second, gains_second=gains_second, step_count=step_count)


EPS_NORM = 1e-06
BETA_ONE = 0.9
BETA_TWO = 0.95
ADAM_EPS = 1e-08
LEARN_RATE = 0.01
DECAY_RATE = 0.1
ROPE_BASE = 10000.0

@jax.custom_vjp
def low(v):
    return lax.optimization_barrier(v.astype(jnp.bfloat16)).astype(jnp.float32)

@jax.custom_vjp
def low_back(v):
    return v

def low_keep(v):
    return (low(v), None)

def low_pass(kept, grad):
    return (grad,)

def back_keep(v):
    return (v, None)

def back_low(kept, grad):
    return (low(grad),)
low.defvjp(low_keep, low_pass)
low_back.defvjp(back_keep, back_low)

def matmul(left_side, right_side):
    return jnp.dot(left_side, right_side, precision=lax.Precision.HIGHEST, preferred_element_type=jnp.float32)

def rms_scale(values, gain_row):
    inverse = lax.rsqrt(lax.optimization_barrier(jnp.mean(values * values, axis=1, keepdims=True)) + EPS_NORM)
    return values * inverse * gain_row

def rope_tables(positions):
    half_dim = HEAD_DIM // 2
    exponent = jnp.arange(half_dim, dtype=jnp.float32) * (-2.0 / HEAD_DIM)
    angles = positions.astype(jnp.float32)[:, None] * jnp.power(ROPE_BASE, exponent)[None, :]
    return (jnp.cos(angles), jnp.sin(angles))

def rotate(values, cosine, sine_rows):
    half_dim = values.shape[-1] // 2
    front_half = values[..., :half_dim]
    back_half = values[..., half_dim:]
    cos_heads = cosine[:, None, :]
    sin_heads = sine_rows[:, None, :]
    return jnp.concatenate([front_half * cos_heads - back_half * sin_heads, back_half * cos_heads + front_half * sin_heads], axis=-1)

def segment_positions(segment_ids):
    index_rows = jnp.arange(segment_ids.shape[0], dtype=jnp.int32)
    boundary = jnp.concatenate([jnp.ones((1,), dtype=jnp.bool_), segment_ids[1:] != segment_ids[:-1]])
    starts = jnp.where(boundary, index_rows, 0).astype(jnp.int32)
    return (index_rows - lax.cummax(starts, axis=0)).astype(jnp.int32)

def attend(queries, key_rows, value_rows, seg_tags):
    count_rows = queries.shape[0]
    pad_rows = KV_BLOCKS * TOK_DEV
    key_pad = jnp.concatenate([jnp.zeros((pad_rows, HEAD_DIM), jnp.float32), key_rows], axis=0)
    value_pad = jnp.concatenate([jnp.zeros((pad_rows, HEAD_DIM), jnp.float32), value_rows], axis=0)
    tag_pad = jnp.concatenate([jnp.zeros((pad_rows,), jnp.int32), seg_tags.astype(jnp.int32)], axis=0)
    block_count = count_rows // TOK_DEV
    query_blocks = queries.reshape(block_count, TOK_DEV, HEADS, HEAD_DIM)
    tag_blocks = seg_tags.reshape(block_count, TOK_DEV)
    block_starts = (jnp.arange(block_count, dtype=jnp.int32) * TOK_DEV).astype(jnp.int32)
    query_index = jnp.arange(TOK_DEV, dtype=jnp.int32) + pad_rows
    key_index = jnp.arange(pad_rows + TOK_DEV, dtype=jnp.int32)

    @jax.checkpoint
    def one_block(operands):
        query_block, tag_block, start_row = operands
        key_block = lax.dynamic_slice_in_dim(key_pad, start_row, pad_rows + TOK_DEV, 0)
        value_block = lax.dynamic_slice_in_dim(value_pad, start_row, pad_rows + TOK_DEV, 0)
        key_tags = lax.dynamic_slice_in_dim(tag_pad, start_row, pad_rows + TOK_DEV, 0)
        allowed = (key_tags[None, :] == tag_block[:, None]) & (key_index[None, :] <= query_index[:, None])
        raw_scores = jnp.einsum('thd,kd->htk', query_block, key_block, precision=lax.Precision.HIGHEST)
        scores = low_back(raw_scores) * HEAD_DIM ** (-0.5)
        scores = jnp.where(allowed[None], scores, -jnp.inf)
        probs = low(jax.nn.softmax(scores, axis=-1))
        return jnp.einsum('htk,kd->thd', probs, value_block, precision=lax.Precision.HIGHEST)
    mixed = lax.map(one_block, (query_blocks, tag_blocks, block_starts))
    return mixed.reshape(count_rows, HEADS, HEAD_DIM)

def forward(input_rows, norm_gains, query_weight, keyval_weight, outproj_weight, gateup_weight, down_weight, seg_tags, cosine, sine_rows):
    count_rows = input_rows.shape[0]
    model_width = input_rows.shape[1]
    hidden_one = low(rms_scale(input_rows, norm_gains[0]))
    query_raw = low_back(matmul(hidden_one, query_weight)).reshape(count_rows, HEADS, HEAD_DIM)
    keyval_raw = low_back(matmul(hidden_one, keyval_weight))
    queries = low(rotate(query_raw, cosine, sine_rows))
    key_rows = low(rotate(keyval_raw[:, None, :HEAD_DIM], cosine, sine_rows)[:, 0])
    value_rows = low(keyval_raw[:, HEAD_DIM:])
    mixed = attend(queries, key_rows, value_rows, seg_tags)
    mixed_low = low(low_back(mixed.reshape(count_rows, HEADS * HEAD_DIM)))
    residual = input_rows + low_back(matmul(mixed_low, outproj_weight))
    gateup_flat = gateup_weight.reshape(model_width, 2 * FF)

    @jax.checkpoint
    def ffn_block(rows_block):
        hidden_two = low(rms_scale(rows_block, norm_gains[1]))
        gateup_pre = low_back(matmul(hidden_two, gateup_flat))
        act_low = low(jax.nn.gelu(gateup_pre[:, :FF], approximate=True) * gateup_pre[:, FF:])
        return rows_block + low_back(matmul(act_low, down_weight))
    blocks = residual.reshape(count_rows // TOK_DEV, TOK_DEV, model_width)
    return lax.map(ffn_block, blocks).reshape(count_rows, model_width)

def adam_update(grad_own, weight, first_old, second_old, bias_first, bias_second, decay):
    first_new = BETA_ONE * first_old + (1.0 - BETA_ONE) * grad_own
    second_new = BETA_TWO * second_old + (1.0 - BETA_TWO) * grad_own * grad_own
    direction = first_new / bias_first / (jnp.sqrt(second_new / bias_second) + ADAM_EPS)
    return (first_new, second_new, -LEARN_RATE * (direction + decay * weight.astype(jnp.float32)))

def reference(tokens_in, segment_ids, block_cotangent, query_weight, keyval_weight, outproj_weight, gateup_weight, down_weight, norm_gains, query_first, keyval_first, outproj_first, gateup_first, down_first, gains_first, query_second, keyval_second, outproj_second, gateup_second, down_second, gains_second, step_count):
    seg_tags = (segment_ids + 1).astype(jnp.int32)
    cosine, sine_rows = rope_tables(segment_positions(segment_ids))

    def run(input_rows, gains_val, query_val, keyval_val, outproj_val, gateup_val, down_val):
        return forward(input_rows, gains_val, query_val, keyval_val, outproj_val, gateup_val, down_val, seg_tags, cosine, sine_rows)
    block_value, pull_back = jax.vjp(run, tokens_in.astype(jnp.float32), norm_gains.astype(jnp.float32), query_weight.astype(jnp.float32), keyval_weight.astype(jnp.float32), outproj_weight.astype(jnp.float32), gateup_weight.astype(jnp.float32), down_weight.astype(jnp.float32))
    input_grad, gains_grad, query_grad, keyval_grad, outproj_grad, gateup_grad, down_grad = pull_back(block_cotangent.astype(jnp.float32))
    step_value = step_count[0].astype(jnp.float32)
    bias_first = 1.0 - jnp.power(BETA_ONE, step_value)
    bias_second = 1.0 - jnp.power(BETA_TWO, step_value)
    query_new = adam_update(query_grad, query_weight, query_first, query_second, bias_first, bias_second, DECAY_RATE)
    keyval_new = adam_update(keyval_grad, keyval_weight, keyval_first, keyval_second, bias_first, bias_second, DECAY_RATE)
    outproj_new = adam_update(outproj_grad, outproj_weight, outproj_first, outproj_second, bias_first, bias_second, DECAY_RATE)
    gateup_new = adam_update(gateup_grad, gateup_weight, gateup_first, gateup_second, bias_first, bias_second, DECAY_RATE)
    down_new = adam_update(down_grad, down_weight, down_first, down_second, bias_first, bias_second, DECAY_RATE)
    gains_new = adam_update(gains_grad, norm_gains, gains_first, gains_second, bias_first, bias_second, 0.0)
    return (block_value.astype(jnp.bfloat16), input_grad, query_grad, keyval_grad, outproj_grad, gateup_grad, down_grad, gains_grad, query_new[0], keyval_new[0], outproj_new[0], gateup_new[0], down_new[0], gains_new[0], query_new[1], keyval_new[1], outproj_new[1], gateup_new[1], down_new[1], gains_new[1], query_new[2], keyval_new[2], outproj_new[2], gateup_new[2], down_new[2], gains_new[2])
```

```python
from functools import partial

import jax
import jax.numpy as jnp
from jax import lax
from jax.experimental import pallas as pl
from jax.experimental.pallas import tpu as pltpu
from jax.sharding import PartitionSpec as P

HEAD_DIM = 256
KV_BLOCKS = 8

EPS_NORM = 1e-06
BETA_ONE = 0.9
BETA_TWO = 0.95
ADAM_EPS = 1e-08
LEARN_RATE = 0.01
DECAY_RATE = 0.1
ROPE_BASE = 10000.0

MESH = pl.DeviceIdType.MESH
TOK = ("shard", "dp")
VMEM_LIMIT = 56 << 20
F32 = jnp.float32
BF16 = jnp.bfloat16


def when(cond, fn):
    if cond is True:
        fn()
    else:
        pl.when(cond)(fn)


def planes(s, ns, far_first=False):
    steps = [(s, 0, 0, True)]
    for t in range(1, ns):
        steps.append((s - t, t, 1, s - t >= 0))
        steps.append((s + t, t, -1, s + t < ns))
    return steps[::-1] if far_first else steps


def greet(ns, nd, use_z, use_plane, use_core, z_all=False):
    s, d, m = (lax.axis_index(a) for a in ("shard", "dp", "mp"))
    bar = pltpu.get_barrier_semaphore()

    def hello(dev):
        pl.semaphore_signal(bar, 1, device_id=dev, device_id_type=MESH)

    count = 0
    if use_z and z_all:
        for k in range(1, ns):
            hello({"shard": lax.rem(s + k, ns)})
        count += ns - 1
    elif use_z:
        when(s < ns - 1, lambda: hello({"shard": s + 1}))
        when(s > 0, lambda: hello({"shard": s - 1}))
        count = (s < ns - 1).astype(jnp.int32) + (s > 0).astype(jnp.int32)
    if use_plane:
        for k in range(1, nd):
            hello({"dp": lax.rem(d + k, nd)})
        count += nd - 1
    if use_core:
        hello({"mp": 1 - m})
        count += 1
    pl.semaphore_wait(bar, count)


def square(d):
    low = lax.rem(d, 2)
    x = d + 1 - 2 * low
    y = lax.rem(d + 2, 4)
    return x, y, lax.rem(x + 2, 4)


def gather_kernel(ns, nd, modes, *refs):
    n = len(modes)
    ins, outs, sems = refs[:n], refs[n : 2 * n], refs[2 * n :]
    s, d, m = (lax.axis_index(a) for a in ("shard", "dp", "mp"))
    use_z = any(k in ("z", "all") for k in modes)
    use_plane = any(k in ("plane", "all", "swap") for k in modes)
    greet(ns, nd, use_z, use_plane, "all" in modes)
    peers = [lax.rem(d + k, nd) for k in range(1, nd)]
    relay = [
        nd == 4 and modes[i] in ("all", "plane") and ins[i].shape[0] % 32 == 0 for i in range(n)]
    if nd == 4:
        x, y, across = square(d)

    def place(i, b, e, core):
        if modes[i] == "z":
            return outs[i].at[b]
        if modes[i] in ("plane", "swap"):
            return outs[i].at[e]
        return outs[i].at[b, e, core]

    def part(i, ref, k):
        if k is None:
            return ref
        rows = ins[i].shape[0] // 2
        return ref.at[pl.ds(k * rows, rows)]

    def zcopy(i, b, way, first):
        src = ins[i] if first else place(i, b, d, m)
        return pltpu.make_async_remote_copy(
            src, place(i, b, d, m), sems[7 * i].at[(way + 1) // 2, b], sems[7 * i + 1].at[b],
            device_id={"shard": s + way}, device_id_type=MESH)

    def pcopy(i, b, to, slot, first, e=None, k=None):
        e = d if e is None else e
        src = (ins[i].at[to] if modes[i] == "swap" else ins[i]) if first else place(i, b, e, m)
        return pltpu.make_async_remote_copy(
            part(i, src, k), part(i, place(i, b, e, m), k),
            sems[7 * i + 2].at[b, slot], sems[7 * i + 3].at[b, e, k or 0],
            device_id={"dp": to}, device_id_type=MESH)

    def precv(i, b, e, k=None):
        ref = place(i, b, e, m)
        return pltpu.make_async_remote_copy(
            part(i, ref, k), part(i, ref, k), sems[7 * i + 2].at[b, 0], sems[7 * i + 3].at[b, e, k or 0],
            device_id={"dp": peers[0]}, device_id_type=MESH)

    def own_copies(i, b, first):
        if relay[i]:
            return [pcopy(i, b, x, 0, first, k=0), pcopy(i, b, y, 1, first, k=1),
                    pcopy(i, b, x, 2, first, k=1), pcopy(i, b, y, 3, first, k=0)]
        return [pcopy(i, b, e, j, first) for j, e in enumerate(peers)]

    def pass_copies(i, b):
        return [(precv(i, b, x, 0), pcopy(i, b, y, 4, False, x, 0)),
                (precv(i, b, y, 1), pcopy(i, b, x, 5, False, y, 1))]

    def ccopy(i, b, e, first):
        src = ins[i] if first else place(i, b, e, m)
        return pltpu.make_async_remote_copy(
            src, place(i, b, e, m), sems[7 * i + 4].at[b, e], sems[7 * i + 5].at[b, e],
            device_id={"mp": 1 - m}, device_id_type=MESH)

    def crecv(i, b, e):
        ref = place(i, b, e, 1 - m)
        return pltpu.make_async_remote_copy(
            ref, ref, sems[7 * i + 4].at[b, e], sems[7 * i + 5].at[b, e],
            device_id={"mp": 1 - m}, device_id_type=MESH)

    def lcopy(i):
        src = ins[i].at[d] if modes[i] == "swap" else ins[i]
        return pltpu.make_async_copy(src, place(i, s, d, m), sems[7 * i + 6])

    def in_z(i):
        return modes[i] in ("z", "all")

    def in_plane(i, t):
        return modes[i] == "all" or (modes[i] in ("plane", "swap") and t == 0)

    def onward(i, b, t, way):
        first = t == 0
        if in_z(i):
            if way >= 0:
                when(s < ns - 1, lambda: zcopy(i, b, 1, first).start())
            if way <= 0:
                when(s > 0, lambda: zcopy(i, b, -1, first).start())
        if in_plane(i, t):
            for c in own_copies(i, b, first):
                c.start()
        if modes[i] == "all":
            ccopy(i, b, d, first).start()
        if first:
            lcopy(i).start()

    def arrive(i, b, t, way):
        zcopy(i, b, -way, False).wait_recv()
        onward(i, b, t, way)

    def pass_on(i, b):
        for got, on in pass_copies(i, b):
            got.wait_recv()
            on.start()

    def settle(i, b):
        if relay[i]:
            waits = [(x, [precv(i, b, x, 1)]), (y, [precv(i, b, y, 0)]),
                     (across, [precv(i, b, across, 0), precv(i, b, across, 1)])]
        else:
            waits = [(e, [precv(i, b, e)]) for e in peers]
        for e, got in waits:
            for w in got:
                w.wait_recv()
            if modes[i] == "all":
                ccopy(i, b, e, False).start()

    def finish(i, b, t, way):
        first = t == 0
        if in_z(i):
            if way >= 0:
                when(s < ns - 1, lambda: zcopy(i, b, 1, first).wait_send())
            if way <= 0:
                when(s > 0, lambda: zcopy(i, b, -1, first).wait_send())
        if in_plane(i, t):
            for c in own_copies(i, b, first):
                c.wait_send()
            if relay[i]:
                for _, on in pass_copies(i, b):
                    on.wait_send()
        if modes[i] == "all":
            for e in [d] + peers:
                crecv(i, b, e).wait_recv()
                ccopy(i, b, e, False).wait_send()
        if first:
            lcopy(i).wait()

    def each(steps, chosen, fn):
        for b, t, way, ok in steps:
            for i in range(n):
                if chosen(i, t):
                    when(ok, partial(fn, i, b, t, way))

    steps = planes(s, ns)
    levels = [[q for q in steps if q[1] == t] for t in range(ns)]
    each(levels[0], lambda i, t: True, onward)
    for t in range(1, ns + 1):
        if t < ns:
            each(levels[t], lambda i, t: in_z(i), arrive)
        each(levels[t - 1], lambda i, t: relay[i] and in_plane(i, t), lambda i, b, t, way: pass_on(i, b))
    each(steps, in_plane, lambda i, b, t, way: settle(i, b))
    each(steps, lambda i, t: t == 0 or in_z(i), finish)


def gather(collective, mesh_shape, items):
    ns, nd = mesh_shape["shard"], mesh_shape["dp"]
    modes = tuple(mode for _, mode in items)
    lead = {"z": (ns,), "plane": (nd,), "all": (ns, nd, 2), "swap": ()}
    shapes = [jax.ShapeDtypeStruct(lead[mode] + a.shape, a.dtype) for a, mode in items]
    sems = []
    dma = pltpu.SemaphoreType.DMA
    for _ in items:
        sems += [dma((2, ns)), dma((ns,)), dma((ns, max(nd, 6))), dma((ns, nd, 2)), dma((ns, nd)), dma((ns, nd)),
                 dma(())]
    return pl.pallas_call(
        partial(gather_kernel, ns, nd, modes),
        out_shape=shapes,
        in_specs=[pl.BlockSpec(memory_space=pl.ANY)] * len(items),
        out_specs=[pl.BlockSpec(memory_space=pl.ANY)] * len(items),
        scratch_shapes=sems,
        compiler_params=pltpu.CompilerParams(
            collective_id=collective, has_side_effects=True, vmem_limit_bytes=VMEM_LIMIT),
        cost_estimate=pl.CostEstimate(flops=0, bytes_accessed=1 << 20, transcendentals=0),
    )(*[a for a, _ in items])


def reduce_kernel(ns, nd, share, p, out, own, sib, got, mid, zgot, fin,
                  lsem, ss, sr, ps, pr, zs, zr, fs, fr, ls2):
    s, d, m = (lax.axis_index(a) for a in ("shard", "dp", "mp"))
    h, c = fin.shape
    tile = 16
    greet(ns, nd, True, True, True, z_all=True)
    peers = [lax.rem(d + k, nd) for k in range(1, nd)]
    relay = nd == 4 and h % 32 == 0
    if relay:
        x, y, across = square(d)
        peers = [across, x, y]
    order = [lax.rem(s + k, ns) for k in sorted(range(1, ns), key=lambda k: abs(k - ns // 2))] + [s]

    def score(b):
        return pltpu.make_async_remote_copy(
            p.at[b, :, 1 - m], sib.at[b], ss.at[b], sr.at[b], device_id={"mp": 1 - m}, device_id_type=MESH)

    def load(b):
        return pltpu.make_async_copy(p.at[b, :, m], own.at[b], lsem.at[b])

    def pcopy(b, src, slot, to):
        return pltpu.make_async_remote_copy(
            src, slot[0], ps.at[b, slot[1]], pr.at[b, slot[1]], device_id={"dp": to}, device_id_type=MESH)

    def sends(b):
        if not relay:
            return [pltpu.make_async_remote_copy(
                own.at[b, e], got.at[b, d], ps.at[b, e], pr.at[b, d], device_id={"dp": e}, device_id_type=MESH)
                for e in peers]
        half = h // 2
        first, last = pl.ds(0, half), pl.ds(half, half)
        return [
            pcopy(b, own.at[b, across, first], (got.at[b, 0, first], 0), x),
            pcopy(b, own.at[b, across, last], (got.at[b, 0, last], 1), y),
            pcopy(b, own.at[b, x], (got.at[b, 1], 2), x),
            pcopy(b, own.at[b, y], (got.at[b, 2], 3), y),
        ]

    def zcopy(b, to):
        return pltpu.make_async_remote_copy(
            mid.at[b], zgot.at[to], zs.at[b], zr.at[to], device_id={"shard": b}, device_id_type=MESH)

    def rows(r):
        return pl.ds(pl.multiple_of(r * tile, tile), tile)

    def sum_rows(lo, hi, terms, store):
        @pl.loop(lo // tile, hi // tile)
        def _(r):
            at = rows(r)
            v = terms[0](at).astype(F32)
            for f in terms[1:]:
                v = v + f(at).astype(F32)
            store(at, v)

    def to_own(b, e):
        def store(at, v):
            own[b, e, at] = v.astype(BF16)
        return store

    def one(b):
        score(b).wait_recv()
        load(b).wait()
        out_now = sends(b)
        for j, e in enumerate(peers + [d]):
            sum_rows(0, h, [lambda at, e=e: own[b, e, at], lambda at, e=e: sib[b, e, at]], to_own(b, e))
            if relay and j == 0:
                out_now[0].start()
                out_now[1].start()
            elif not relay and j < len(peers):
                out_now[j].start()

    def two(b):
        if not relay:
            return
        half = h // 2
        c0, c1, c2, c3 = sends(b)
        c0.wait_recv()
        sum_rows(0, half, [lambda at: own[b, y, at], lambda at: got[b, 0, at]], to_own(b, y))
        c3.start()
        c1.wait_recv()
        sum_rows(half, h, [lambda at: own[b, x, at], lambda at: got[b, 0, at]], to_own(b, x))
        c2.start()

    def plane_terms(b):
        slots = [1, 2] if relay else peers
        return [lambda at: own[b, d, at]] + [lambda at, e=e: got[b, e, at] for e in slots]

    def three(b, last):
        if relay:
            for w in sends(b)[2:]:
                w.wait_recv()
        else:
            for e in peers:
                pltpu.make_async_remote_copy(
                    own.at[b, e], got.at[b, e], ps.at[b, e], pr.at[b, e],
                    device_id={"dp": e}, device_id_type=MESH).wait_recv()
        if not last:
            def store(at, v):
                mid[b, at] = v.astype(BF16)
            sum_rows(0, h, plane_terms(b), store)
            zcopy(b, s).start()

    for b in order:
        score(b).start()
        load(b).start()
    for k in range(ns + 2):
        if k < ns:
            one(order[k])
        if 0 <= k - 1 < ns:
            two(order[k - 1])
        if 0 <= k - 2 < ns:
            three(order[k - 2], k - 2 == ns - 1)
    others = order[:-1]
    for b in others:
        zcopy(b, b).wait_recv()

    def store(at, v):
        fin[at] = v.astype(fin.dtype)

    sum_rows(0, h, plane_terms(s) + [lambda at, b=b: zgot[b, at] for b in others], store)
    if share:
        give = pltpu.make_async_remote_copy(
            fin, out.at[m], fs, fr, device_id={"mp": 1 - m}, device_id_type=MESH)
        take = pltpu.make_async_remote_copy(
            fin, out.at[1 - m], fs, fr, device_id={"mp": 1 - m}, device_id_type=MESH)
        give.start()
        keep = pltpu.make_async_copy(fin, out.at[m], ls2)
        keep.start()
        take.wait_recv()
        give.wait_send()
        keep.wait()
    else:
        keep = pltpu.make_async_copy(fin, out, ls2)
        keep.start()
        keep.wait()
    for b in order:
        score(b).wait_send()
        for w in sends(b):
            w.wait_send()
    for b in others:
        zcopy(b, s).wait_send()


def reduce_scatter(collective, mesh_shape, p, share):
    ns, nd = mesh_shape["shard"], mesh_shape["dp"]
    h, c = p.shape[3:]
    if 3 * (p.size // 2) * 2 > (40 << 20):
        total = lax.psum_scatter(p.reshape(ns * nd, 2, h, c), TOK, scatter_dimension=0, tiled=True)[0]
        total = lax.psum(total, "mp")
        return total if share else lax.dynamic_index_in_dim(total, lax.axis_index("mp"), 0, False)
    dma = pltpu.SemaphoreType.DMA
    return pl.pallas_call(
        partial(reduce_kernel, ns, nd, share),
        out_shape=jax.ShapeDtypeStruct((2, h, c) if share else (h, c), BF16),
        in_specs=[pl.BlockSpec(memory_space=pl.ANY)],
        out_specs=pl.BlockSpec(memory_space=pl.ANY),
        scratch_shapes=[
            pltpu.VMEM((ns, nd, h, c), BF16),
            pltpu.VMEM((ns, nd, h, c), BF16),
            pltpu.VMEM((ns, nd, h, c), BF16),
            pltpu.VMEM((ns, h, c), BF16),
            pltpu.VMEM((ns, h, c), BF16),
            pltpu.VMEM((h, c), BF16),
            dma((ns,)), dma((ns,)), dma((ns,)),
            dma((ns, nd)), dma((ns, nd)),
            dma((ns,)), dma((ns,)), dma(()), dma(()), dma(()),
        ],
        compiler_params=pltpu.CompilerParams(
            collective_id=collective, has_side_effects=True, vmem_limit_bytes=VMEM_LIMIT),
        cost_estimate=pl.CostEstimate(flops=0, bytes_accessed=1 << 20, transcendentals=0),
    )(p)


def rope_tables(positions):
    half_dim = HEAD_DIM // 2
    exponent = jnp.arange(half_dim, dtype=F32) * (-2.0 / HEAD_DIM)
    angles = positions.astype(F32)[:, None] * jnp.power(ROPE_BASE, exponent)[None, :]
    return (jnp.cos(angles), jnp.sin(angles))


def rotate(values, cosine, sine_rows):
    half_dim = values.shape[-1] // 2
    front_half = values[..., :half_dim]
    back_half = values[..., half_dim:]
    return jnp.concatenate(
        [front_half * cosine - back_half * sine_rows, back_half * cosine + front_half * sine_rows], axis=-1)


def rows_product(left_side, right_side):
    return lax.dot_general(
        left_side, right_side, (((0,), (0,)), ((), ())), preferred_element_type=F32)


def cols_product(left_side, right_side):
    return lax.dot_general(
        left_side, right_side, (((1,), (1,)), ((), ())), preferred_element_type=F32)


def product(left_side, right_side):
    return jnp.dot(left_side, right_side, preferred_element_type=F32)


def adam_update(grad_own, weight, first_old, second_old, bias_first, bias_second, decay):
    first_new = BETA_ONE * first_old + (1.0 - BETA_ONE) * grad_own
    second_new = BETA_TWO * second_old + (1.0 - BETA_TWO) * grad_own * grad_own
    direction = first_new / bias_first / (jnp.sqrt(second_new / bias_second) + ADAM_EPS)
    return (first_new, second_new, -LEARN_RATE * (direction + decay * weight.astype(F32)))


def swap_add(value):
    other = lax.ppermute(value, "mp", [(0, 1), (1, 0)])
    return value.astype(F32) + other.astype(F32)


def shards(
    mesh_shape,
    tokens_in,
    segment_ids,
    block_cotangent,
    query_weight,
    keyval_weight,
    outproj_weight,
    gateup_weight,
    down_weight,
    norm_gains,
    query_first,
    keyval_first,
    outproj_first,
    gateup_first,
    down_first,
    gains_first,
    query_second,
    keyval_second,
    outproj_second,
    gateup_second,
    down_second,
    gains_second,
    step_count,
):
    ns, nd = mesh_shape["shard"], mesh_shape["dp"]
    n = ns * nd
    s, d, m = (lax.axis_index(a) for a in ("shard", "dp", "mp"))
    me = s * nd + d
    tok, width = tokens_in.shape
    own_d = query_weight.shape[0]
    q_cols = query_weight.shape[1]
    heads_local = q_cols // HEAD_DIM
    ff_local = gateup_weight.shape[2]
    units = -(-(-(-ff_local // n)) // 128) * 128
    ff_pad = units * n - ff_local
    half = tok // 2
    plane_tok = nd * tok
    plane_d = ns * own_d

    gateup_cut = jnp.pad(gateup_weight, ((0, 0), (0, 0), (0, ff_pad)))
    gateup_cut = gateup_cut.reshape(own_d, 2, n, units).transpose(2, 0, 1, 3).reshape(n, own_d, 2 * units)
    down_cut = jnp.pad(down_weight, ((0, ff_pad), (0, 0))).reshape(n, units, own_d)
    gateup_mine = lax.all_to_all(gateup_cut, TOK, 0, 0, tiled=True).reshape(width, 2 * units)
    down_mine = lax.all_to_all(down_cut, TOK, 0, 0, tiled=True)
    down_mine = down_mine.transpose(1, 0, 2).reshape(units, width)

    input_rows = tokens_in.astype(F32)
    inverse_one = lax.rsqrt(jnp.mean(input_rows * input_rows, axis=1) + EPS_NORM)
    lanes = max(256, -(-max(own_d, tok) // 128) * 128)

    def line(v):
        return jnp.pad(v, ((0, 0), (0, lanes - v.shape[1])))

    small = jnp.concatenate(
        [line(norm_gains.astype(F32)), line(segment_ids.astype(F32)[None]), line(inverse_one[None]),
         jnp.zeros((4, lanes), F32)], axis=0)
    qkv_weight = jnp.concatenate(
        [query_weight, lax.dynamic_slice_in_dim(keyval_weight, m * HEAD_DIM, HEAD_DIM, 1)], axis=1)

    def plane_cut(value):
        return value.reshape(tok, ns, nd, own_d).transpose(2, 0, 1, 3).reshape(nd, tok, plane_d)

    tokens_plane, qkv_plane, small_all, cot_all = gather(
        0, mesh_shape,
        [(plane_cut(tokens_in), "swap"), (qkv_weight, "z"), (small, "all"),
         (lax.dynamic_slice_in_dim(block_cotangent, m * half, half, 0), "all")])
    tokens_plane = tokens_plane.reshape(plane_tok, plane_d)
    qkv_plane = qkv_plane.reshape(plane_d, q_cols + HEAD_DIM)
    cot_all = cot_all.reshape(n * tok, width)
    small_all = small_all[:, :, 0]
    gains_by = small_all[:, :, :2, :own_d]
    full_gains = gains_by.transpose(2, 0, 1, 3).reshape(2, width)
    tags = small_all[:, :, 2, :tok].reshape(n * tok)
    plane_scale = lax.dynamic_index_in_dim(small_all[:, :, 3, :tok], s, 0, False).reshape(plane_tok, 1)
    plane_gain = lax.dynamic_index_in_dim(gains_by[:, :, 0], d, 1, False).reshape(1, plane_d)

    def to_plane(value):
        return lax.all_to_all(plane_cut(value), "dp", 0, 0, tiled=True).reshape(plane_tok, plane_d)

    def from_plane(value):
        got = lax.all_to_all(value.reshape(nd, tok, plane_d), "dp", 0, 0, tiled=True)
        return got.reshape(nd, tok, ns, own_d).transpose(1, 2, 0, 3).reshape(tok, width)

    def plane_sum(value):
        got = lax.all_to_all(value.reshape(nd, tok, -1), "dp", 0, 0, tiled=True)
        return jnp.sum(got.astype(F32), axis=0)

    hidden_plane = (tokens_plane.astype(F32) * plane_scale * plane_gain).astype(BF16)
    qkv_raw = plane_sum(product(hidden_plane, qkv_plane).astype(BF16))

    pad = KV_BLOCKS * tok
    key_span = pad + tok
    start = me * tok
    tag_pad = jnp.concatenate([jnp.full((pad,), -1.0, F32), tags])
    key_tags = lax.dynamic_slice_in_dim(tag_pad, start, key_span, 0)
    own_tags = segment_ids.astype(F32)
    query_index = jnp.arange(tok, dtype=jnp.int32) + pad
    key_index = jnp.arange(key_span, dtype=jnp.int32)
    same_segment = key_tags[None, :] == own_tags[:, None]
    allowed = same_segment & (key_index[None, :] <= query_index[:, None])
    positions = jnp.sum(
        (same_segment & (key_index[None, :] < query_index[:, None])).astype(jnp.int32), axis=1)
    cosine, sine_rows = rope_tables(positions)
    cos_h, sin_h = cosine[:, None, :], sine_rows[:, None, :]
    score_scale = HEAD_DIM ** (-0.5)
    queries = rotate(qkv_raw[:, :q_cols].reshape(tok, heads_local, HEAD_DIM), cos_h, sin_h).astype(BF16)
    kv_raw = qkv_raw[:, q_cols:]
    kv_mine = jnp.where(m == 0, rotate(kv_raw, cosine, sine_rows), kv_raw).astype(BF16)
    (kv_all,) = gather(1, mesh_shape, [(kv_mine, "all")])
    kv_all = kv_all.reshape(n, 2, tok, HEAD_DIM)
    kv_pad = jnp.concatenate([jnp.zeros((KV_BLOCKS, 2, tok, HEAD_DIM), BF16), kv_all], axis=0)
    kv_window = lax.dynamic_slice_in_dim(kv_pad, me, KV_BLOCKS + 1, 0)
    key_rows = kv_window[:, 0].reshape(key_span, HEAD_DIM)
    value_rows = kv_window[:, 1].reshape(key_span, HEAD_DIM)
    scores = jnp.einsum("thd,kd->htk", queries, key_rows, preferred_element_type=F32) * score_scale
    scores = jnp.where(allowed[None], scores, -jnp.inf)
    row_max = jnp.max(scores, axis=2, keepdims=True)
    raw = jnp.exp(scores - row_max)
    probs = raw / jnp.sum(raw, axis=2, keepdims=True)
    probs_low = probs.astype(BF16)
    mixed = jnp.einsum("htk,kd->thd", probs_low, value_rows, preferred_element_type=F32)
    mixed_low = mixed.reshape(tok, q_cols).astype(BF16)
    mixed_plane, outproj_z = gather(
        2, mesh_shape, [(mixed_low, "plane"), (outproj_weight, "z")])
    mixed_plane = mixed_plane.reshape(plane_tok, q_cols)
    outproj_plane = outproj_z.transpose(1, 0, 2).reshape(q_cols, plane_d)
    attn_part = from_plane(product(mixed_plane, outproj_plane).astype(BF16))
    residual = input_rows + swap_add(attn_part)
    gain_two = full_gains[1]
    inverse_two = lax.rsqrt(jnp.mean(residual * residual, axis=1, keepdims=True) + EPS_NORM)
    hidden_two = (residual * inverse_two * gain_two).astype(BF16)
    (hidden_all,) = gather(
        3, mesh_shape, [(lax.dynamic_slice_in_dim(hidden_two, m * half, half, 0), "all")])
    hidden_all = hidden_all.reshape(n * tok, width)

    gateup_pre = product(hidden_all, gateup_mine)
    gate_pre, up_pre = gateup_pre[:, :units], gateup_pre[:, units:]
    gelu_val, gelu_pull = jax.vjp(partial(jax.nn.gelu, approximate=True), gate_pre)
    act_low = (gelu_val * up_pre).astype(BF16)
    act_grad = cols_product(cot_all, down_mine)
    gateup_low = jnp.concatenate(
        [gelu_pull(act_grad * up_pre)[0], act_grad * gelu_val], axis=1).astype(BF16)
    hidden_two_part = cols_product(gateup_low, gateup_mine).astype(BF16)
    hidden_two_grad = reduce_scatter(
        4, mesh_shape, hidden_two_part.reshape(ns, nd, 2, half, width), True).reshape(tok, width).astype(F32)
    gateup_grad = rows_product(hidden_all, gateup_low).astype(BF16).reshape(n, own_d, 2 * units)
    down_grad = rows_product(act_low, cot_all).astype(BF16)
    down_grad = down_grad.reshape(units, n, own_d).transpose(1, 0, 2)
    own_gateup = lax.all_to_all(gateup_grad, TOK, 0, 0, tiled=True).reshape(n, own_d, 2, units)
    own_gateup = own_gateup.transpose(1, 2, 0, 3).reshape(own_d, 2, n * units)[:, :, :ff_local].astype(F32)
    own_down = lax.all_to_all(down_grad, TOK, 0, 0, tiled=True).reshape(n * units, own_d)[:ff_local].astype(F32)
    ffn_part = product(act_low, down_mine).astype(BF16)
    ffn_sum = reduce_scatter(
        5, mesh_shape, ffn_part.reshape(ns, nd, 2, half, width), True).reshape(tok, width).astype(F32)
    block_out = (residual + ffn_sum).astype(BF16)

    def norm_back(rows, inverse, gain_row, grad):
        normed = rows * inverse
        scaled = grad * gain_row
        inner = jnp.mean(normed * scaled, axis=1, keepdims=True)
        return inverse * (scaled - normed * inner), jnp.sum(grad * normed, axis=0)

    residual_from, gain_two_grad = norm_back(residual, inverse_two, gain_two, hidden_two_grad)
    residual_grad = block_cotangent.astype(F32) + residual_from
    attn_low = to_plane(residual_grad.astype(BF16))
    mixed_grad = plane_sum(cols_product(attn_low, outproj_plane).astype(BF16))
    mixed_grad = mixed_grad.astype(BF16).reshape(tok, heads_local, HEAD_DIM)

    def z_sum(value):
        got = lax.all_to_all(value, "shard", 0, 0, tiled=True)
        return jnp.sum(got.astype(F32), axis=0)

    outproj_grad = rows_product(mixed_plane, attn_low).astype(BF16)
    own_outproj = z_sum(outproj_grad.reshape(q_cols, ns, own_d).transpose(1, 0, 2))

    probs_grad = jnp.einsum("thd,kd->htk", mixed_grad, value_rows, preferred_element_type=F32)
    value_grad = jnp.einsum("htk,thd->kd", probs_low, mixed_grad, preferred_element_type=F32)
    inner_sum = jnp.sum(probs * probs_grad, axis=2, keepdims=True)
    scores_low = (probs * (probs_grad - inner_sum) * score_scale).astype(BF16)
    query_rot_grad = jnp.einsum("htk,kd->thd", scores_low, key_rows, preferred_element_type=F32)
    key_rot_grad = jnp.einsum("htk,thd->kd", scores_low, queries, preferred_element_type=F32)
    window_grad = jnp.stack(
        [key_rot_grad.reshape(KV_BLOCKS + 1, tok, HEAD_DIM), value_grad.reshape(KV_BLOCKS + 1, tok, HEAD_DIM)],
        axis=1).astype(BF16)
    kv_grad_pad = lax.dynamic_update_slice_in_dim(
        jnp.zeros((KV_BLOCKS + n, 2, tok, HEAD_DIM), BF16), window_grad, me, 0)
    kv_grad = reduce_scatter(
        6, mesh_shape, kv_grad_pad[KV_BLOCKS:].reshape(ns, nd, 2, tok, HEAD_DIM), False).astype(F32)
    kv_low = jnp.where(m == 0, rotate(kv_grad, cosine, -sine_rows), kv_grad)
    query_low = rotate(query_rot_grad, cos_h, -sin_h).reshape(tok, q_cols)
    qkv_low = jnp.concatenate([query_low, kv_low], axis=1).astype(BF16)
    (qkv_low_plane,) = gather(7, mesh_shape, [(qkv_low, "plane")])
    qkv_low_plane = qkv_low_plane.reshape(plane_tok, q_cols + HEAD_DIM)
    hidden_part = from_plane(cols_product(qkv_low_plane, qkv_plane).astype(BF16))
    hidden_one_grad = swap_add(hidden_part)
    qkv_grad = rows_product(hidden_plane, qkv_low_plane).astype(BF16)
    own_qkv = z_sum(qkv_grad.reshape(ns, own_d, q_cols + HEAD_DIM))
    own_query = own_qkv[:, :q_cols]
    kv_own = own_qkv[:, q_cols:]
    kv_other = lax.ppermute(kv_own, "mp", [(0, 1), (1, 0)])
    own_keyval = jnp.where(
        m == 0, jnp.concatenate([kv_own, kv_other], axis=1), jnp.concatenate([kv_other, kv_own], axis=1))

    inverse_col = inverse_one[:, None]
    input_from, gain_one_grad = norm_back(input_rows, inverse_col, full_gains[0], hidden_one_grad)
    input_grad = residual_grad + input_from
    gains_cut = jnp.stack([gain_one_grad, gain_two_grad], axis=0).reshape(2, n, own_d).transpose(1, 0, 2)
    own_gains = jnp.sum(lax.all_to_all(gains_cut, TOK, 0, 0, tiled=True), axis=0)

    step_value = step_count[0].astype(F32)
    bias_first = 1.0 - jnp.power(BETA_ONE, step_value)
    bias_second = 1.0 - jnp.power(BETA_TWO, step_value)
    grads = (own_query, own_keyval, own_outproj, own_gateup, own_down, own_gains)
    weights = (query_weight, keyval_weight, outproj_weight, gateup_weight, down_weight, norm_gains)
    firsts = (query_first, keyval_first, outproj_first, gateup_first, down_first, gains_first)
    seconds = (query_second, keyval_second, outproj_second, gateup_second, down_second, gains_second)
    decays = (DECAY_RATE,) * 5 + (0.0,)
    news = [
        adam_update(g, w, a, b, bias_first, bias_second, c)
        for g, w, a, b, c in zip(grads, weights, firsts, seconds, decays)
    ]
    return (
        (block_out, input_grad)
        + grads
        + tuple(x[0] for x in news)
        + tuple(x[1] for x in news)
        + tuple(x[2] for x in news)
    )


def solution(mesh):
    rows, split_q, split_o = P(TOK, None), P(TOK, "mp"), P("mp", TOK)
    params = (split_q, rows, split_o, P(TOK, None, "mp"), split_o, P(None, TOK))
    in_specs = (rows, P(TOK), rows) + params * 3 + (P(),)
    out_specs = (rows, rows) + params * 4
    return jax.shard_map(
        partial(shards, dict(mesh.shape)), mesh=mesh, in_specs=in_specs, out_specs=out_specs, check_vma=False)
```

```python
from functools import partial

import jax
import jax.numpy as jnp
from jax import lax
from jax.experimental import pallas as pl
from jax.experimental.pallas import tpu as pltpu
from jax.sharding import PartitionSpec as P

HEAD_DIM = 256
KV_BLOCKS = 8

EPS_NORM = 1e-06
BETA_ONE = 0.9
BETA_TWO = 0.95
ADAM_EPS = 1e-08
LEARN_RATE = 0.01
DECAY_RATE = 0.1
ROPE_BASE = 10000.0

MESH = pl.DeviceIdType.MESH
TOK = ("shard", "dp")
VMEM_LIMIT = 56 << 20
F32 = jnp.float32
BF16 = jnp.bfloat16


def when(cond, fn):
    if cond is True:
        fn()
    else:
        pl.when(cond)(fn)


def planes(s, ns, far_first=False):
    steps = [(s, 0, 0, True)]
    for t in range(1, ns):
        steps.append((s - t, t, 1, s - t >= 0))
        steps.append((s + t, t, -1, s + t < ns))
    return steps[::-1] if far_first else steps


def greet(ns, nd, use_z, use_plane, use_core, z_all=False, everyone=False):
    s, d, m = (lax.axis_index(a) for a in ("shard", "dp", "mp"))
    bar = pltpu.get_barrier_semaphore()

    def hello(dev):
        pl.semaphore_signal(bar, 1, device_id=dev, device_id_type=MESH)

    count = 0
    if use_z and z_all:
        for k in range(1, ns):
            hello({"shard": lax.rem(s + k, ns)})
        count += ns - 1
    elif use_z:
        when(s < ns - 1, lambda: hello({"shard": s + 1}))
        when(s > 0, lambda: hello({"shard": s - 1}))
        count = (s < ns - 1).astype(jnp.int32) + (s > 0).astype(jnp.int32)
    if everyone:
        for b, e in others(ns, nd):
            hello({"shard": b, "dp": e})
        count += ns * nd - 1
    if use_plane:
        for k in range(1, nd):
            hello({"dp": lax.rem(d + k, nd)})
        count += nd - 1
    if use_core:
        hello({"mp": 1 - m})
        count += 1
    pl.semaphore_wait(bar, count)


def others(ns, nd):
    me = lax.axis_index("shard") * nd + lax.axis_index("dp")
    for k in range(1, ns * nd):
        p = lax.rem(me + k, ns * nd)
        yield p // nd, lax.rem(p, nd)


def square(d):
    low = lax.rem(d, 2)
    x = d + 1 - 2 * low
    y = lax.rem(d + 2, 4)
    return x, y, lax.rem(x + 2, 4)


def gather_kernel(ns, nd, modes, *refs):
    n = len(modes)
    ins, outs, sems = refs[:n], refs[n : 2 * n], refs[2 * n :]
    s, d, m = (lax.axis_index(a) for a in ("shard", "dp", "mp"))
    use_z = any(k in ("z", "all") for k in modes)
    use_plane = any(k in ("plane", "all", "swap") for k in modes)
    greet(ns, nd, use_z, use_plane, "all" in modes, everyone="spread" in modes)
    peers = [lax.rem(d + k, nd) for k in range(1, nd)]
    relay = [
        nd == 4 and modes[i] in ("all", "plane") and ins[i].shape[0] % 32 == 0 for i in range(n)]
    if nd == 4:
        x, y, across = square(d)

    def place(i, b, e, core):
        if modes[i] == "z":
            return outs[i].at[b]
        if modes[i] == "spread":
            return outs[i].at[b * nd + e]
        if modes[i] in ("plane", "swap"):
            return outs[i].at[e]
        return outs[i].at[b, e, core]

    def part(i, ref, k):
        if k is None:
            return ref
        rows = ins[i].shape[0] // 2
        return ref.at[pl.ds(k * rows, rows)]

    def zcopy(i, b, way, first):
        src = ins[i] if first else place(i, b, d, m)
        return pltpu.make_async_remote_copy(
            src, place(i, b, d, m), sems[7 * i].at[(way + 1) // 2, b], sems[7 * i + 1].at[b],
            device_id={"shard": s + way}, device_id_type=MESH)

    def pcopy(i, b, to, slot, first, e=None, k=None):
        e = d if e is None else e
        src = (ins[i].at[to] if modes[i] == "swap" else ins[i]) if first else place(i, b, e, m)
        return pltpu.make_async_remote_copy(
            part(i, src, k), part(i, place(i, b, e, m), k),
            sems[7 * i + 2].at[b, slot], sems[7 * i + 3].at[b, e, k or 0],
            device_id={"dp": to}, device_id_type=MESH)

    def precv(i, b, e, k=None):
        ref = place(i, b, e, m)
        return pltpu.make_async_remote_copy(
            part(i, ref, k), part(i, ref, k), sems[7 * i + 2].at[b, 0], sems[7 * i + 3].at[b, e, k or 0],
            device_id={"dp": peers[0]}, device_id_type=MESH)

    def own_copies(i, b, first):
        if relay[i]:
            return [pcopy(i, b, x, 0, first, k=0), pcopy(i, b, y, 1, first, k=1),
                    pcopy(i, b, x, 2, first, k=1), pcopy(i, b, y, 3, first, k=0)]
        return [pcopy(i, b, e, j, first) for j, e in enumerate(peers)]

    def pass_copies(i, b):
        return [(precv(i, b, x, 0), pcopy(i, b, y, 4, False, x, 0)),
                (precv(i, b, y, 1), pcopy(i, b, x, 5, False, y, 1))]

    def ccopy(i, b, e, first):
        src = ins[i] if first else place(i, b, e, m)
        return pltpu.make_async_remote_copy(
            src, place(i, b, e, m), sems[7 * i + 4].at[b, e], sems[7 * i + 5].at[b, e],
            device_id={"mp": 1 - m}, device_id_type=MESH)

    def crecv(i, b, e):
        ref = place(i, b, e, 1 - m)
        return pltpu.make_async_remote_copy(
            ref, ref, sems[7 * i + 4].at[b, e], sems[7 * i + 5].at[b, e],
            device_id={"mp": 1 - m}, device_id_type=MESH)

    def spread_copies(i, arriving):
        copies = []
        for b, e in others(ns, nd):
            to = outs[i].at[b * nd + e] if arriving else outs[i].at[s * nd + d]
            slot = (b, e, 0) if arriving else (s, d, 0)
            copies.append(pltpu.make_async_remote_copy(
                ins[i].at[b * nd + e], to, sems[7 * i + 2].at[b, e], sems[7 * i + 3].at[slot],
                device_id={"shard": b, "dp": e}, device_id_type=MESH))
        return copies

    def lcopy(i):
        src = ins[i].at[d] if modes[i] == "swap" else ins[i].at[s * nd + d] if modes[i] == "spread" else ins[i]
        return pltpu.make_async_copy(src, place(i, s, d, m), sems[7 * i + 6])

    def in_z(i):
        return modes[i] in ("z", "all")

    def in_plane(i, t):
        return modes[i] == "all" or (modes[i] in ("plane", "swap") and t == 0)

    def onward(i, b, t, way):
        first = t == 0
        if in_z(i):
            if way >= 0:
                when(s < ns - 1, lambda: zcopy(i, b, 1, first).start())
            if way <= 0:
                when(s > 0, lambda: zcopy(i, b, -1, first).start())
        if in_plane(i, t):
            for c in own_copies(i, b, first):
                c.start()
        if modes[i] == "all":
            ccopy(i, b, d, first).start()
        if modes[i] == "spread":
            for c in spread_copies(i, False):
                c.start()
        if first:
            lcopy(i).start()

    def arrive(i, b, t, way):
        zcopy(i, b, -way, False).wait_recv()
        onward(i, b, t, way)

    def pass_on(i, b):
        for got, on in pass_copies(i, b):
            got.wait_recv()
            on.start()

    def settle(i, b):
        if relay[i]:
            waits = [(x, [precv(i, b, x, 1)]), (y, [precv(i, b, y, 0)]),
                     (across, [precv(i, b, across, 0), precv(i, b, across, 1)])]
        else:
            waits = [(e, [precv(i, b, e)]) for e in peers]
        for e, got in waits:
            for w in got:
                w.wait_recv()
            if modes[i] == "all":
                ccopy(i, b, e, False).start()

    def finish(i, b, t, way):
        first = t == 0
        if in_z(i):
            if way >= 0:
                when(s < ns - 1, lambda: zcopy(i, b, 1, first).wait_send())
            if way <= 0:
                when(s > 0, lambda: zcopy(i, b, -1, first).wait_send())
        if in_plane(i, t):
            for c in own_copies(i, b, first):
                c.wait_send()
            if relay[i]:
                for _, on in pass_copies(i, b):
                    on.wait_send()
        if modes[i] == "spread":
            for c in spread_copies(i, False):
                c.wait_send()
            for c in spread_copies(i, True):
                c.wait_recv()
        if modes[i] == "all":
            for e in [d] + peers:
                crecv(i, b, e).wait_recv()
                ccopy(i, b, e, False).wait_send()
        if first:
            lcopy(i).wait()

    def each(steps, chosen, fn):
        for b, t, way, ok in steps:
            for i in range(n):
                if chosen(i, t):
                    when(ok, partial(fn, i, b, t, way))

    steps = planes(s, ns)
    levels = [[q for q in steps if q[1] == t] for t in range(ns)]
    each(levels[0], lambda i, t: True, onward)
    for t in range(1, ns + 1):
        if t < ns:
            each(levels[t], lambda i, t: in_z(i), arrive)
        each(levels[t - 1], lambda i, t: relay[i] and in_plane(i, t), lambda i, b, t, way: pass_on(i, b))
    each(steps, in_plane, lambda i, b, t, way: settle(i, b))
    each(steps, lambda i, t: t == 0 or in_z(i), finish)


def gather(collective, mesh_shape, items):
    ns, nd = mesh_shape["shard"], mesh_shape["dp"]
    modes = tuple(mode for _, mode in items)
    lead = {"z": (ns,), "plane": (nd,), "all": (ns, nd, 2), "swap": (), "spread": ()}
    shapes = [jax.ShapeDtypeStruct(lead[mode] + a.shape, a.dtype) for a, mode in items]
    sems = []
    dma = pltpu.SemaphoreType.DMA
    for _ in items:
        sems += [dma((2, ns)), dma((ns,)), dma((ns, max(nd, 6))), dma((ns, nd, 2)), dma((ns, nd)), dma((ns, nd)),
                 dma(())]
    return pl.pallas_call(
        partial(gather_kernel, ns, nd, modes),
        out_shape=shapes,
        in_specs=[pl.BlockSpec(memory_space=pl.ANY)] * len(items),
        out_specs=[pl.BlockSpec(memory_space=pl.ANY)] * len(items),
        scratch_shapes=sems,
        compiler_params=pltpu.CompilerParams(
            collective_id=collective, has_side_effects=True, vmem_limit_bytes=VMEM_LIMIT),
        cost_estimate=pl.CostEstimate(flops=0, bytes_accessed=1 << 20, transcendentals=0),
    )(*[a for a, _ in items])


def reduce_kernel(ns, nd, share, spans, *refs):
    count = len(spans) if spans else 1
    n_in = count + 1 if spans else 1
    ins, outs, scratch = refs[:n_in], refs[n_in : n_in + count], refs[n_in + count :]
    own, sib, give, got, mid, zgot, fin, lsem, ss, sr, ps, pr, zs, zr, fs, fr, ks = scratch
    s, d, m = (lax.axis_index(a) for a in ("shard", "dp", "mp"))
    h, c = fin.shape[1:]
    tile = 16
    greet(ns, nd, True, True, True, z_all=True)
    peers = [lax.rem(d + k, nd) for k in range(1, nd)]
    relay = nd == 4 and h % 32 == 0
    if relay:
        x, y, across = square(d)
        peers = [across, x, y]
    order = [lax.rem(s + k, ns) for k in sorted(range(1, ns), key=lambda k: abs(k - ns // 2))] + [s]
    items = [(a, k, order[k]) for k in range(ns) for a in range(count)]

    def score(a, k, b):
        src = give.at[a, k % 2] if spans else ins[0].at[b, :, 1 - m]
        return pltpu.make_async_remote_copy(
            src, sib.at[a, b], ss.at[a, b], sr.at[a, b], device_id={"mp": 1 - m}, device_id_type=MESH)

    def load(a, b):
        return pltpu.make_async_copy(ins[0].at[b, :, m], own.at[a, b], lsem.at[a, b])

    def multiply(a, b, core, store):
        lo, hi = spans[a]
        step = 512 if c % 512 == 0 else 128
        left = ins[a][b, :, core].reshape(nd * h, hi - lo)

        @pl.loop(0, c // step)
        def _(j):
            cols = pl.ds(pl.multiple_of(j * step, step), step)
            term = cols_product(left, ins[count][cols, lo:hi])
            store(cols, term.astype(BF16).reshape(nd, h, step))

    def zero(a, k, b):
        if not spans:
            score(a, k, b).start()
            load(a, b).start()
            return
        if k >= 2:
            score(a, k - 2, order[k - 2]).wait_send()

        def to_give(cols, v):
            give[a, k % 2, :, :, cols] = v

        def to_own(cols, v):
            own[a, b, :, :, cols] = v

        multiply(a, b, 1 - m, to_give)
        score(a, k, b).start()
        multiply(a, b, m, to_own)

    def pcopy(a, b, src, dst, slot, to):
        return pltpu.make_async_remote_copy(
            src, dst, ps.at[a, b, slot], pr.at[a, b, slot], device_id={"dp": to}, device_id_type=MESH)

    def sends(a, b):
        if not relay:
            return [pltpu.make_async_remote_copy(
                own.at[a, b, e], got.at[a, b, d], ps.at[a, b, e], pr.at[a, b, d],
                device_id={"dp": e}, device_id_type=MESH) for e in peers]
        half = h // 2
        first, last = pl.ds(0, half), pl.ds(half, half)
        return [
            pcopy(a, b, own.at[a, b, across, first], got.at[a, b, 0, first], 0, x),
            pcopy(a, b, own.at[a, b, across, last], got.at[a, b, 0, last], 1, y),
            pcopy(a, b, own.at[a, b, x], got.at[a, b, 1], 2, x),
            pcopy(a, b, own.at[a, b, y], got.at[a, b, 2], 3, y),
        ]

    def zcopy(a, b, to):
        return pltpu.make_async_remote_copy(
            mid.at[a, b], zgot.at[a, to], zs.at[a, b], zr.at[a, to], device_id={"shard": b}, device_id_type=MESH)

    def sum_rows(lo, hi, terms, store):
        @pl.loop(lo // tile, hi // tile)
        def _(r):
            at = pl.ds(pl.multiple_of(r * tile, tile), tile)
            v = terms[0](at).astype(F32)
            for f in terms[1:]:
                v = v + f(at).astype(F32)
            store(at, v.astype(BF16))

    def to_own(a, b, e):
        def store(at, v):
            own[a, b, e, at] = v
        return store

    def one(a, k, b):
        score(a, k, b).wait_recv()
        if not spans:
            load(a, b).wait()
        out_now = sends(a, b)
        for j, e in enumerate(peers + [d]):
            sum_rows(0, h, [lambda at, e=e: own[a, b, e, at], lambda at, e=e: sib[a, b, e, at]], to_own(a, b, e))
            if relay and j == 0:
                out_now[0].start()
                out_now[1].start()
            elif not relay and j < len(peers):
                out_now[j].start()

    def two(a, k, b):
        if not relay:
            return
        half = h // 2
        c0, c1, c2, c3 = sends(a, b)
        c0.wait_recv()
        sum_rows(0, half, [lambda at: own[a, b, y, at], lambda at: got[a, b, 0, at]], to_own(a, b, y))
        c3.start()
        c1.wait_recv()
        sum_rows(half, h, [lambda at: own[a, b, x, at], lambda at: got[a, b, 0, at]], to_own(a, b, x))
        c2.start()

    def plane_terms(a, b):
        slots = [1, 2] if relay else peers
        return [lambda at: own[a, b, d, at]] + [lambda at, e=e: got[a, b, e, at] for e in slots]

    def three(a, k, b):
        if relay:
            for w in sends(a, b)[2:]:
                w.wait_recv()
        else:
            for e in peers:
                pltpu.make_async_remote_copy(
                    own.at[a, b, e], got.at[a, b, e], ps.at[a, b, e], pr.at[a, b, e],
                    device_id={"dp": e}, device_id_type=MESH).wait_recv()
        if k < ns - 1:
            def store(at, v):
                mid[a, b, at] = v
            sum_rows(0, h, plane_terms(a, b), store)
            zcopy(a, b, s).start()

    stages = [zero, one, two, three]
    if not spans:
        for item in items:
            zero(*item)
        stages = stages[1:]
    for t in range(len(items) + len(stages) - 1):
        for j, stage in enumerate(stages):
            if 0 <= t - j < len(items):
                stage(*items[t - j])

    def give_out(a, core):
        return pltpu.make_async_remote_copy(
            fin.at[a], outs[a].at[core], fs.at[a], fr.at[a], device_id={"mp": 1 - m}, device_id_type=MESH)

    def keep(a):
        return pltpu.make_async_copy(fin.at[a], outs[a].at[m] if share else outs[a], ks.at[a])

    others = order[:-1]
    for a in range(count):
        for b in others:
            zcopy(a, b, b).wait_recv()

        def store(at, v, a=a):
            fin[a, at] = v

        sum_rows(0, h, plane_terms(a, s) + [lambda at, b=b: zgot[a, b, at] for b in others], store)
        if share:
            give_out(a, m).start()
        keep(a).start()
    for a in range(count):
        if share:
            give_out(a, 1 - m).wait_recv()
            give_out(a, m).wait_send()
        keep(a).wait()
        for k, b in enumerate(order):
            if not spans or k >= ns - 2:
                score(a, k, b).wait_send()
            for w in sends(a, b):
                w.wait_send()
        for b in others:
            zcopy(a, b, s).wait_send()


def reduce_scatter(collective, mesh_shape, share, blocks, terms=None, factors=None, weight=None):
    ns, nd = mesh_shape["shard"], mesh_shape["dp"]
    rows, c = blocks
    h = rows // 2
    count = len(factors) if factors else 1
    size = ns * nd * h * c * 2
    if size * count * 3 > (40 << 20):
        whole = [terms] if factors is None else [
            cols_product(x, weight[:, lo:hi]).astype(BF16) for x, lo, hi in factors]
        sums = []
        for p in whole:
            total = lax.psum_scatter(p.reshape(ns * nd, 2, h, c), TOK, scatter_dimension=0, tiled=True)[0]
            total = lax.psum(total, "mp")
            sums.append(total if share else lax.dynamic_index_in_dim(total, lax.axis_index("mp"), 0, False))
        return sums
    if factors is None:
        spans = None
        args = [terms.reshape(ns, nd, 2, h, c)]
        in_specs = [pl.BlockSpec(memory_space=pl.ANY)]
        give = (1, 1, 1, 16, 128)
    else:
        spans = tuple((lo, hi) for _, lo, hi in factors)
        args = [x.reshape(ns, nd, 2, h, hi - lo) for x, lo, hi in factors] + [weight]
        in_specs = [pl.BlockSpec(memory_space=pltpu.VMEM)] * (count + 1)
        give = (count, 2, nd, h, c)
    slots = 3 if nd == 4 and h % 32 == 0 else nd
    dma = pltpu.SemaphoreType.DMA
    return pl.pallas_call(
        partial(reduce_kernel, ns, nd, share, spans),
        out_shape=[jax.ShapeDtypeStruct((2, h, c) if share else (h, c), BF16)] * count,
        in_specs=in_specs,
        out_specs=[pl.BlockSpec(memory_space=pl.ANY)] * count,
        scratch_shapes=[
            pltpu.VMEM((count, ns, nd, h, c), BF16),
            pltpu.VMEM((count, ns, nd, h, c), BF16),
            pltpu.VMEM(give, BF16),
            pltpu.VMEM((count, ns, slots, h, c), BF16),
            pltpu.VMEM((count, ns, h, c), BF16),
            pltpu.VMEM((count, ns, h, c), BF16),
            pltpu.VMEM((count, h, c), BF16),
            dma((count, ns)), dma((count, ns)), dma((count, ns)),
            dma((count, ns, max(nd, 4))), dma((count, ns, max(nd, 4))),
            dma((count, ns)), dma((count, ns)), dma((count,)), dma((count,)), dma((count,)),
        ],
        compiler_params=pltpu.CompilerParams(
            collective_id=collective, has_side_effects=True, vmem_limit_bytes=VMEM_LIMIT),
        cost_estimate=pl.CostEstimate(flops=0, bytes_accessed=1 << 20, transcendentals=0),
    )(*args)


def plane_kernel(ns, nd, p, out, own, sib, ls, ss, sr, ps, pr, fs, fr, ks):
    d, m = lax.axis_index("dp"), lax.axis_index("mp")
    h, c = own.shape[1:]
    tile = 16
    greet(ns, nd, False, True, True)
    peers = [lax.rem(d + k, nd) for k in range(1, nd)]
    order = ([square(d)[2], square(d)[0], square(d)[1]] if nd == 4 else peers) + [d]
    other = {"mp": 1 - m}

    def score(e):
        return pltpu.make_async_remote_copy(
            p.at[e, 1 - m], sib.at[e], ss.at[e], sr.at[e], device_id=other, device_id_type=MESH)

    def load(e):
        return pltpu.make_async_copy(p.at[e, m], own.at[e], ls.at[e])

    def send(e, block):
        return pltpu.make_async_remote_copy(
            own.at[e], out.at[block, m], ps.at[e], pr.at[block], device_id={"dp": e}, device_id_type=MESH)

    def share(e, core):
        src = own.at[d] if e is d else out.at[e, m]
        return pltpu.make_async_remote_copy(
            src, out.at[e, core], fs.at[e], fr.at[e], device_id=other, device_id_type=MESH)

    for e in order:
        score(e).start()
        load(e).start()
    for e in order:
        score(e).wait_recv()
        load(e).wait()

        @pl.loop(0, h // tile)
        def _(r, e=e):
            at = pl.ds(pl.multiple_of(r * tile, tile), tile)
            own[e, at] = (own[e, at].astype(F32) + sib[e, at].astype(F32)).astype(BF16)

        if e is not d:
            send(e, d).start()
    keep = pltpu.make_async_copy(own.at[d], out.at[d, m], ks)
    keep.start()
    share(d, m).start()
    for e in order[:-1]:
        send(e, e).wait_recv()
        share(e, m).start()
    keep.wait()
    for e in order:
        share(e, 1 - m).wait_recv()
        share(e, m).wait_send()
        score(e).wait_send()
        if e is not d:
            send(e, d).wait_send()


def plane_reduce(collective, mesh_shape, p):
    ns, nd = mesh_shape["shard"], mesh_shape["dp"]
    h, c = p.shape[2:]
    dma = pltpu.SemaphoreType.DMA
    return pl.pallas_call(
        partial(plane_kernel, ns, nd),
        out_shape=jax.ShapeDtypeStruct(p.shape, BF16),
        in_specs=[pl.BlockSpec(memory_space=pl.ANY)],
        out_specs=pl.BlockSpec(memory_space=pl.ANY),
        scratch_shapes=[pltpu.VMEM((nd, h, c), BF16)] * 2 + [dma((nd,))] * 7 + [dma(())],
        compiler_params=pltpu.CompilerParams(
            collective_id=collective, has_side_effects=True, vmem_limit_bytes=VMEM_LIMIT),
        cost_estimate=pl.CostEstimate(flops=0, bytes_accessed=1 << 20, transcendentals=0),
    )(p)


def rope_tables(positions):
    half_dim = HEAD_DIM // 2
    exponent = jnp.arange(half_dim, dtype=F32) * (-2.0 / HEAD_DIM)
    angles = positions.astype(F32)[:, None] * jnp.power(ROPE_BASE, exponent)[None, :]
    return (jnp.cos(angles), jnp.sin(angles))


def rotate(values, cosine, sine_rows):
    half_dim = values.shape[-1] // 2
    front_half = values[..., :half_dim]
    back_half = values[..., half_dim:]
    return jnp.concatenate(
        [front_half * cosine - back_half * sine_rows, back_half * cosine + front_half * sine_rows], axis=-1)


def rows_product(left_side, right_side):
    return lax.dot_general(
        left_side, right_side, (((0,), (0,)), ((), ())), preferred_element_type=F32)


def cols_product(left_side, right_side):
    return lax.dot_general(
        left_side, right_side, (((1,), (1,)), ((), ())), preferred_element_type=F32)


def product(left_side, right_side):
    return jnp.dot(left_side, right_side, preferred_element_type=F32)


def pack_kernel(full, gateup, down, out):
    units = down.shape[1]
    here = pl.program_id(0) < full

    def keep(v):
        return jnp.where(here, v, jnp.zeros_like(v)).astype(BF16)

    out[0, :, :units] = keep(gateup[:, 0, :].astype(F32))
    out[0, :, units : 2 * units] = keep(gateup[:, 1, :].astype(F32))
    out[0, :, 2 * units :] = keep(down[...].astype(F32))


def pack(n, units, gateup_weight, down_cols):
    own_d, _, ff_local = gateup_weight.shape
    full = ff_local // units
    return pl.pallas_call(
        partial(pack_kernel, full),
        out_shape=jax.ShapeDtypeStruct((n, own_d, 3 * units), BF16),
        grid=(n,),
        in_specs=[
            pl.BlockSpec((own_d, 2, units), lambda j: (0, 0, jnp.minimum(j, full - 1))),
            pl.BlockSpec((own_d, units), lambda j: (0, jnp.minimum(j, full - 1))),
        ],
        out_specs=pl.BlockSpec((1, own_d, 3 * units), lambda j: (j, 0, 0)),
        compiler_params=pltpu.CompilerParams(vmem_limit_bytes=VMEM_LIMIT),
    )(gateup_weight, down_cols)


def adam_step(rates, grad, weight, first, second, decay):
    first_new = BETA_ONE * first + (1.0 - BETA_ONE) * grad
    second_new = BETA_TWO * second + (1.0 - BETA_TWO) * grad * grad
    direction = first_new * rates[0] / (jnp.sqrt(second_new * rates[1]) + ADAM_EPS)
    return first_new, second_new, -LEARN_RATE * (direction + decay * weight.astype(F32))


def unpack_kernel(rates, got, gw, gf, gs, dw, df, ds, gg, gfn, gsn, gu, dg, dfn, dsn, du):
    units = dw.shape[1]
    pair = (rates[0], rates[1])
    for k in range(2):
        grad = got[0, :, k * units : (k + 1) * units].astype(F32)
        gg[:, k, :] = grad
        gfn[:, k, :], gsn[:, k, :], gu[:, k, :] = adam_step(
            pair, grad, gw[:, k, :], gf[:, k, :], gs[:, k, :], DECAY_RATE)
    grad = got[0, :, 2 * units :].astype(F32)
    dg[...] = grad
    dfn[...], dsn[...], du[...] = adam_step(pair, grad, dw[...], df[...], ds[...], DECAY_RATE)


def unpack_adam(units, rates, got, gateup, down):
    own_d, _, ff_local = gateup[0].shape
    three = pl.BlockSpec((own_d, 2, units), lambda j: (0, 0, j))
    two = pl.BlockSpec((own_d, units), lambda j: (0, j))
    shape3 = jax.ShapeDtypeStruct(gateup[0].shape, F32)
    shape2 = jax.ShapeDtypeStruct(down[0].shape, F32)
    out = pl.pallas_call(
        unpack_kernel,
        out_shape=[shape3] * 4 + [shape2] * 4,
        grid=(ff_local // units,),
        in_specs=[
            pl.BlockSpec(memory_space=pltpu.SMEM),
            pl.BlockSpec((1, own_d, 3 * units), lambda j: (j, 0, 0)),
        ] + [three] * 3 + [two] * 3,
        out_specs=[three] * 4 + [two] * 4,
        compiler_params=pltpu.CompilerParams(vmem_limit_bytes=VMEM_LIMIT),
    )(rates, got, *gateup, *down)
    return out[:4], out[4:]


def shards(
    mesh_shape,
    tokens_in,
    segment_ids,
    block_cotangent,
    query_weight,
    keyval_weight,
    outproj_weight,
    gateup_weight,
    down_weight,
    norm_gains,
    query_first,
    keyval_first,
    outproj_first,
    gateup_first,
    down_first,
    gains_first,
    query_second,
    keyval_second,
    outproj_second,
    gateup_second,
    down_second,
    gains_second,
    step_count,
):
    ns, nd = mesh_shape["shard"], mesh_shape["dp"]
    n = ns * nd
    s, d, m = (lax.axis_index(a) for a in ("shard", "dp", "mp"))
    me = s * nd + d
    tok, width = tokens_in.shape
    own_d = query_weight.shape[0]
    q_cols = query_weight.shape[1]
    heads_local = q_cols // HEAD_DIM
    ff_local = gateup_weight.shape[2]
    units = -(-(-(-ff_local // n)) // 128) * 128
    ff_pad = units * n - ff_local
    half = tok // 2
    plane_tok = nd * tok
    plane_d = ns * own_d

    three = pack(n, units, gateup_weight, down_weight.T)

    input_rows = tokens_in.astype(F32)
    inverse_one = lax.rsqrt(jnp.mean(input_rows * input_rows, axis=1) + EPS_NORM)
    lanes = max(256, -(-max(own_d, tok) // 128) * 128)

    def line(v):
        return jnp.pad(v, ((0, 0), (0, lanes - v.shape[1])))

    small = jnp.concatenate(
        [line(norm_gains.astype(F32)), line(segment_ids.astype(F32)[None]), line(inverse_one[None]),
         jnp.zeros((4, lanes), F32)], axis=0)
    qkv_weight = jnp.concatenate(
        [query_weight, lax.dynamic_slice_in_dim(keyval_weight, m * HEAD_DIM, HEAD_DIM, 1)], axis=1)

    def plane_cut(value):
        return value.reshape(tok, ns, nd, own_d).transpose(2, 0, 1, 3).reshape(nd, tok, plane_d)

    small_all, tokens_plane, cot_all, qkv_plane = gather(
        0, mesh_shape,
        [(small, "all"), (plane_cut(tokens_in), "swap"),
         (lax.dynamic_slice_in_dim(block_cotangent, m * half, half, 0), "all"), (qkv_weight, "z")])
    tokens_plane = tokens_plane.reshape(plane_tok, plane_d)
    three, tokens_plane = lax.optimization_barrier((three, tokens_plane))
    three = lax.all_to_all(three, TOK, 0, 0, tiled=True).reshape(width, 3 * units)
    gateup_mine, down_mine = three[:, : 2 * units], three[:, 2 * units :]
    qkv_plane = qkv_plane.reshape(plane_d, q_cols + HEAD_DIM)
    cot_all = cot_all.reshape(n * tok, width)
    small_all = small_all[:, :, 0]
    gains_by = small_all[:, :, :2, :own_d]
    full_gains = gains_by.transpose(2, 0, 1, 3).reshape(2, width)
    tags = small_all[:, :, 2, :tok].reshape(n * tok)
    plane_scale = lax.dynamic_index_in_dim(small_all[:, :, 3, :tok], s, 0, False).reshape(plane_tok, 1)
    plane_gain = lax.dynamic_index_in_dim(gains_by[:, :, 0], d, 1, False).reshape(1, plane_d)

    def to_plane(collective, value):
        (got,) = gather(collective, mesh_shape, [(plane_cut(value), "swap")])
        return got.reshape(plane_tok, plane_d)

    def from_plane(collective, value):
        got = plane_reduce(collective, mesh_shape, value.reshape(nd, 2, half, plane_d))
        return got.reshape(nd, tok, ns, own_d).transpose(1, 2, 0, 3).reshape(tok, width).astype(F32)

    def plane_sum(collective, value):
        (got,) = gather(collective, mesh_shape, [(value.reshape(nd, tok, -1), "swap")])
        return jnp.sum(got.astype(F32), axis=0)

    hidden_plane = (tokens_plane.astype(F32) * plane_scale * plane_gain).astype(BF16)
    qkv_raw = plane_sum(8, product(hidden_plane, qkv_plane).astype(BF16))

    pad = KV_BLOCKS * tok
    key_span = pad + tok
    start = me * tok
    tag_pad = jnp.concatenate([jnp.full((pad,), -1.0, F32), tags])
    key_tags = lax.dynamic_slice_in_dim(tag_pad, start, key_span, 0)
    own_tags = segment_ids.astype(F32)
    query_index = jnp.arange(tok, dtype=jnp.int32) + pad
    key_index = jnp.arange(key_span, dtype=jnp.int32)
    same_segment = key_tags[None, :] == own_tags[:, None]
    allowed = same_segment & (key_index[None, :] <= query_index[:, None])
    positions = jnp.sum(
        (same_segment & (key_index[None, :] < query_index[:, None])).astype(jnp.int32), axis=1)
    cosine, sine_rows = rope_tables(positions)
    cos_h, sin_h = cosine[:, None, :], sine_rows[:, None, :]
    score_scale = HEAD_DIM ** (-0.5)
    queries = rotate(qkv_raw[:, :q_cols].reshape(tok, heads_local, HEAD_DIM), cos_h, sin_h).astype(BF16)
    kv_raw = qkv_raw[:, q_cols:]
    kv_mine = jnp.where(m == 0, rotate(kv_raw, cosine, sine_rows), kv_raw).astype(BF16)
    (kv_all,) = gather(1, mesh_shape, [(kv_mine, "all")])
    kv_all = kv_all.reshape(n, 2, tok, HEAD_DIM)
    kv_pad = jnp.concatenate([jnp.zeros((KV_BLOCKS, 2, tok, HEAD_DIM), BF16), kv_all], axis=0)
    kv_window = lax.dynamic_slice_in_dim(kv_pad, me, KV_BLOCKS + 1, 0)
    key_rows = kv_window[:, 0].reshape(key_span, HEAD_DIM)
    value_rows = kv_window[:, 1].reshape(key_span, HEAD_DIM)
    scores = jnp.einsum("thd,kd->htk", queries, key_rows, preferred_element_type=F32) * score_scale
    scores = jnp.where(allowed[None], scores, -jnp.inf)
    row_max = jnp.max(scores, axis=2, keepdims=True)
    raw = jnp.exp(scores - row_max)
    probs = raw / jnp.sum(raw, axis=2, keepdims=True)
    probs_low = probs.astype(BF16)
    mixed = jnp.einsum("htk,kd->thd", probs_low, value_rows, preferred_element_type=F32)
    mixed_low = mixed.reshape(tok, q_cols).astype(BF16)
    mixed_plane, outproj_z = gather(
        2, mesh_shape, [(mixed_low, "plane"), (outproj_weight.T, "z")])
    mixed_plane = mixed_plane.reshape(plane_tok, q_cols)
    outproj_plane = outproj_z.reshape(plane_d, q_cols)
    residual = input_rows + from_plane(9, cols_product(mixed_plane, outproj_plane).astype(BF16))
    gain_two = full_gains[1]
    inverse_two = lax.rsqrt(jnp.mean(residual * residual, axis=1, keepdims=True) + EPS_NORM)
    hidden_two = (residual * inverse_two * gain_two).astype(BF16)
    (hidden_all,) = gather(
        3, mesh_shape, [(lax.dynamic_slice_in_dim(hidden_two, m * half, half, 0), "all")])
    hidden_all = hidden_all.reshape(n * tok, width)

    gateup_pre = product(hidden_all, gateup_mine)
    gate_pre, up_pre = gateup_pre[:, :units], gateup_pre[:, units:]
    gelu_val, gelu_pull = jax.vjp(partial(jax.nn.gelu, approximate=True), gate_pre)
    act_low = (gelu_val * up_pre).astype(BF16)
    act_grad = product(cot_all, down_mine)
    gateup_low = jnp.concatenate(
        [gelu_pull(act_grad * up_pre)[0], act_grad * gelu_val], axis=1).astype(BF16)
    three_grad = jnp.concatenate(
        [rows_product(hidden_all, gateup_low).astype(BF16), rows_product(cot_all, act_low).astype(BF16)], axis=1)
    three_grad, act_low, gateup_low = lax.optimization_barrier((three_grad, act_low, gateup_low))
    three_grad = lax.all_to_all(three_grad.reshape(n, own_d, 3 * units), TOK, 0, 0, tiled=True)
    hidden_two_grad, ffn_sum = reduce_scatter(
        4, mesh_shape, True, (tok, width),
        factors=[(gateup_low, 0, 2 * units), (act_low, 2 * units, 3 * units)], weight=three)
    hidden_two_grad = hidden_two_grad.reshape(tok, width).astype(F32)
    ffn_sum = ffn_sum.reshape(tok, width).astype(F32)
    block_out = (residual + ffn_sum).astype(BF16)

    def norm_back(rows, inverse, gain_row, grad):
        normed = rows * inverse
        scaled = grad * gain_row
        inner = jnp.mean(normed * scaled, axis=1, keepdims=True)
        return inverse * (scaled - normed * inner), jnp.sum(grad * normed, axis=0)

    residual_from, gain_two_grad = norm_back(residual, inverse_two, gain_two, hidden_two_grad)
    residual_grad = block_cotangent.astype(F32) + residual_from
    attn_low = to_plane(10, residual_grad.astype(BF16))
    mixed_grad = plane_sum(11, product(attn_low, outproj_plane).astype(BF16))
    mixed_grad = mixed_grad.astype(BF16).reshape(tok, heads_local, HEAD_DIM)

    def z_sum(value):
        got = lax.all_to_all(value, "shard", 0, 0, tiled=True)
        return jnp.sum(got.astype(F32), axis=0)

    outproj_grad = rows_product(attn_low, mixed_plane).astype(BF16)
    outproj_grad, three_grad = lax.optimization_barrier((outproj_grad, three_grad))
    own_outproj = z_sum(outproj_grad.reshape(ns, own_d, q_cols))

    probs_grad = jnp.einsum("thd,kd->htk", mixed_grad, value_rows, preferred_element_type=F32)
    value_grad = jnp.einsum("htk,thd->kd", probs_low, mixed_grad, preferred_element_type=F32)
    inner_sum = jnp.sum(probs * probs_grad, axis=2, keepdims=True)
    scores_low = (probs * (probs_grad - inner_sum) * score_scale).astype(BF16)
    query_rot_grad = jnp.einsum("htk,kd->thd", scores_low, key_rows, preferred_element_type=F32)
    key_rot_grad = jnp.einsum("htk,thd->kd", scores_low, queries, preferred_element_type=F32)
    window_grad = jnp.stack(
        [key_rot_grad.reshape(KV_BLOCKS + 1, tok, HEAD_DIM), value_grad.reshape(KV_BLOCKS + 1, tok, HEAD_DIM)],
        axis=1).astype(BF16)
    kv_grad_pad = lax.dynamic_update_slice_in_dim(
        jnp.zeros((KV_BLOCKS + n, 2, tok, HEAD_DIM), BF16), window_grad, me, 0)
    (kv_grad,) = reduce_scatter(6, mesh_shape, False, (2 * tok, HEAD_DIM), terms=kv_grad_pad[KV_BLOCKS:])
    kv_grad = kv_grad.astype(F32)
    kv_low = jnp.where(m == 0, rotate(kv_grad, cosine, -sine_rows), kv_grad)
    query_low = rotate(query_rot_grad, cos_h, -sin_h).reshape(tok, q_cols)
    qkv_low = jnp.concatenate([query_low, kv_low], axis=1).astype(BF16)
    (qkv_low_plane,) = gather(7, mesh_shape, [(qkv_low, "plane")])
    qkv_low_plane = qkv_low_plane.reshape(plane_tok, q_cols + HEAD_DIM)
    hidden_one_grad = from_plane(12, cols_product(qkv_low_plane, qkv_plane).astype(BF16))
    qkv_grad = rows_product(hidden_plane, qkv_low_plane).astype(BF16)
    own_qkv = z_sum(qkv_grad.reshape(ns, own_d, q_cols + HEAD_DIM))
    own_query = own_qkv[:, :q_cols]
    kv_own = own_qkv[:, q_cols:]
    kv_other = lax.ppermute(kv_own, "mp", [(0, 1), (1, 0)])
    own_keyval = jnp.where(
        m == 0, jnp.concatenate([kv_own, kv_other], axis=1), jnp.concatenate([kv_other, kv_own], axis=1))

    inverse_col = inverse_one[:, None]
    input_from, gain_one_grad = norm_back(input_rows, inverse_col, full_gains[0], hidden_one_grad)
    input_grad = residual_grad + input_from
    gains_cut = jnp.stack([gain_one_grad, gain_two_grad], axis=0).reshape(2, n, own_d).transpose(1, 0, 2)
    gains_cut = jnp.pad(gains_cut, ((0, 0), (0, 6), (0, lanes - own_d)))
    (gains_got,) = gather(13, mesh_shape, [(gains_cut, "spread")])
    own_gains = jnp.sum(gains_got[:, :2, :own_d], axis=0)

    step_value = step_count[0].astype(F32)
    bias_first = 1.0 - jnp.power(BETA_ONE, step_value)
    bias_second = 1.0 - jnp.power(BETA_TWO, step_value)
    rates = jnp.stack([1.0 / bias_first, 1.0 / bias_second])
    gateup_news, down_news = unpack_adam(
        units, rates, three_grad, (gateup_weight, gateup_first, gateup_second),
        (down_weight.T, down_first.T, down_second.T))
    down_news = [x.T for x in down_news]

    def adam(grad, weight, first, second, decay):
        return (grad,) + adam_step(rates, grad, weight, first, second, decay)

    news = [
        adam(own_query, query_weight, query_first, query_second, DECAY_RATE),
        adam(own_keyval, keyval_weight, keyval_first, keyval_second, DECAY_RATE),
        tuple(v.T for v in adam(own_outproj, outproj_weight.T, outproj_first.T, outproj_second.T, DECAY_RATE)),
        gateup_news,
        down_news,
        adam(own_gains, norm_gains, gains_first, gains_second, 0.0),
    ]
    return (block_out, input_grad) + tuple(x[k] for k in range(4) for x in news)


def solution(mesh):
    rows, split_q, split_o = P(TOK, None), P(TOK, "mp"), P("mp", TOK)
    params = (split_q, rows, split_o, P(TOK, None, "mp"), split_o, P(None, TOK))
    in_specs = (rows, P(TOK), rows) + params * 3 + (P(),)
    out_specs = (rows, rows) + params * 4
    return jax.shard_map(
        partial(shards, dict(mesh.shape)), mesh=mesh, in_specs=in_specs, out_specs=out_specs, check_vma=False)
```

```python
from functools import partial

import jax
import jax.numpy as jnp
from jax import lax
from jax.experimental import pallas as pl
from jax.experimental.pallas import tpu as pltpu
from jax.sharding import PartitionSpec as P

HEAD_DIM = 256
KV_BLOCKS = 8

EPS_NORM = 1e-06
BETA_ONE = 0.9
BETA_TWO = 0.95
ADAM_EPS = 1e-08
LEARN_RATE = 0.01
DECAY_RATE = 0.1
ROPE_BASE = 10000.0

MESH = pl.DeviceIdType.MESH
TOK = ("shard", "dp")
VMEM_LIMIT = 56 << 20
F32 = jnp.float32
BF16 = jnp.bfloat16


def when(cond, fn):
    if cond is True:
        fn()
    else:
        pl.when(cond)(fn)


def planes(s, ns, far_first=False):
    steps = [(s, 0, 0, True)]
    for t in range(1, ns):
        steps.append((s - t, t, 1, s - t >= 0))
        steps.append((s + t, t, -1, s + t < ns))
    return steps[::-1] if far_first else steps


def greet(ns, nd, use_z, use_plane, use_core, z_all=False):
    s, d, m = (lax.axis_index(a) for a in ("shard", "dp", "mp"))
    bar = pltpu.get_barrier_semaphore()

    def hello(dev):
        pl.semaphore_signal(bar, 1, device_id=dev, device_id_type=MESH)

    count = 0
    if use_z and z_all:
        for k in range(1, ns):
            hello({"shard": lax.rem(s + k, ns)})
        count += ns - 1
    elif use_z:
        when(s < ns - 1, lambda: hello({"shard": s + 1}))
        when(s > 0, lambda: hello({"shard": s - 1}))
        count = (s < ns - 1).astype(jnp.int32) + (s > 0).astype(jnp.int32)
    if use_plane:
        for k in range(1, nd):
            hello({"dp": lax.rem(d + k, nd)})
        count += nd - 1
    if use_core:
        hello({"mp": 1 - m})
        count += 1
    pl.semaphore_wait(bar, count)


def square(d):
    low = lax.rem(d, 2)
    x = d + 1 - 2 * low
    y = lax.rem(d + 2, 4)
    return x, y, lax.rem(x + 2, 4)


def gather_kernel(ns, nd, modes, work, n_work, *refs):
    n = len(modes)
    ins, more_in = refs[:n], refs[n : n + n_work]
    outs, more_out = refs[n + n_work : 2 * n + n_work], refs[2 * n + n_work : 2 * n + 2 * n_work - (n_work > 0)]
    sems = refs[-7 * n :]
    s, d, m = (lax.axis_index(a) for a in ("shard", "dp", "mp"))
    use_z = any(k in ("z", "all") for k in modes)
    use_plane = any(k in ("plane", "all", "swap") for k in modes)
    direct = [modes[i] == "all" and ins[i].size * ins[i].dtype.itemsize < 128 << 10 for i in range(n)]
    late = [modes[i] == "z" and any(k == "all" and not q for k, q in zip(modes, direct)) for i in range(n)]
    greet(ns, nd, use_z, use_plane, "all" in modes, z_all=any(direct))
    peers = [lax.rem(d + k, nd) for k in range(1, nd)]
    relay = [
        nd == 4 and modes[i] in ("all", "plane") and ins[i].shape[0] % 32 == 0 and not direct[i] for i in range(n)]
    if nd == 4:
        x, y, across = square(d)

    def place(i, b, e, core):
        if modes[i] == "z":
            return outs[i].at[b]
        if modes[i] in ("plane", "swap"):
            return outs[i].at[e]
        return outs[i].at[b, e, core]

    def half_of(i, ref, k):
        if k is None:
            return ref
        rows = ins[i].shape[0] // 2
        return ref.at[pl.ds(k * rows, rows)]

    def zcopy(i, b, way, first):
        src = ins[i] if first else place(i, b, d, m)
        return pltpu.make_async_remote_copy(
            src, place(i, b, d, m), sems[7 * i].at[(way + 1) // 2, b], sems[7 * i + 1].at[b],
            device_id={"shard": s + way}, device_id_type=MESH)

    def pcopy(i, b, to, slot, first, e=None, k=None):
        e = d if e is None else e
        src = (ins[i].at[to] if modes[i] == "swap" else ins[i]) if first else place(i, b, e, m)
        return pltpu.make_async_remote_copy(
            half_of(i, src, k), half_of(i, place(i, b, e, m), k),
            sems[7 * i + 2].at[b, slot], sems[7 * i + 3].at[b, e, k or 0],
            device_id={"dp": to}, device_id_type=MESH)

    def precv(i, b, e, k=None):
        ref = place(i, b, e, m)
        return pltpu.make_async_remote_copy(
            half_of(i, ref, k), half_of(i, ref, k), sems[7 * i + 2].at[b, 0], sems[7 * i + 3].at[b, e, k or 0],
            device_id={"dp": peers[0]}, device_id_type=MESH)

    def own_copies(i, b, first):
        if relay[i]:
            return [pcopy(i, b, x, 0, first, k=0), pcopy(i, b, y, 1, first, k=1),
                    pcopy(i, b, x, 2, first, k=1), pcopy(i, b, y, 3, first, k=0)]
        return [pcopy(i, b, e, j, first) for j, e in enumerate(peers)]

    def pass_copies(i, b):
        return [(precv(i, b, x, 0), pcopy(i, b, y, 4, False, x, 0)),
                (precv(i, b, y, 1), pcopy(i, b, x, 5, False, y, 1))]

    def ccopy(i, b, e, first):
        src = ins[i] if first else place(i, b, e, m)
        return pltpu.make_async_remote_copy(
            src, place(i, b, e, m), sems[7 * i + 4].at[b, e], sems[7 * i + 5].at[b, e],
            device_id={"mp": 1 - m}, device_id_type=MESH)

    def crecv(i, b, e):
        ref = place(i, b, e, 1 - m)
        return pltpu.make_async_remote_copy(
            ref, ref, sems[7 * i + 4].at[b, e], sems[7 * i + 5].at[b, e],
            device_id={"mp": 1 - m}, device_id_type=MESH)

    def dcopy(i, to, block):
        return pltpu.make_async_remote_copy(
            ins[i], place(i, block, d, m), sems[7 * i].at[0, to], sems[7 * i + 1].at[block],
            device_id={"shard": to}, device_id_type=MESH)

    planes_off = [lax.rem(s + k, ns) for k in range(1, ns)]

    def lcopy(i):
        src = ins[i].at[d] if modes[i] == "swap" else ins[i]
        return pltpu.make_async_copy(src, place(i, s, d, m), sems[7 * i + 6])

    def in_z(i):
        return modes[i] in ("z", "all") and not direct[i]

    def in_plane(i, t):
        return modes[i] == "all" or (modes[i] in ("plane", "swap") and t == 0)

    def onward(i, b, t, way):
        first = t == 0
        if in_z(i):
            if way >= 0:
                when(s < ns - 1, lambda: zcopy(i, b, 1, first).start())
            if way <= 0:
                when(s > 0, lambda: zcopy(i, b, -1, first).start())
        if in_plane(i, t):
            for c in own_copies(i, b, first):
                c.start()
        if modes[i] == "all":
            ccopy(i, b, d, first).start()
        if first and direct[i]:
            for p in planes_off:
                dcopy(i, p, s).start()
        if first:
            lcopy(i).start()

    def arrive(i, b, t, way):
        zcopy(i, b, -way, False).wait_recv()
        onward(i, b, t, way)

    def pass_on(i, b):
        for got, on in pass_copies(i, b):
            got.wait_recv()
            on.start()

    def settle(i, b):
        if relay[i]:
            waits = [(x, [precv(i, b, x, 1)]), (y, [precv(i, b, y, 0)]),
                     (across, [precv(i, b, across, 0), precv(i, b, across, 1)])]
        else:
            waits = [(e, [precv(i, b, e)]) for e in peers]
        for e, got in waits:
            for w in got:
                w.wait_recv()
            if modes[i] == "all":
                ccopy(i, b, e, False).start()

    def finish(i, b, t, way):
        first = t == 0
        if in_z(i):
            if way >= 0:
                when(s < ns - 1, lambda: zcopy(i, b, 1, first).wait_send())
            if way <= 0:
                when(s > 0, lambda: zcopy(i, b, -1, first).wait_send())
        if in_plane(i, t):
            for c in own_copies(i, b, first):
                c.wait_send()
            if relay[i]:
                for _, on in pass_copies(i, b):
                    on.wait_send()
        if direct[i] and first:
            for p in planes_off:
                dcopy(i, p, s).wait_send()
        if modes[i] == "all":
            for e in [d] + peers:
                crecv(i, b, e).wait_recv()
                ccopy(i, b, e, False).wait_send()
        if first:
            lcopy(i).wait()

    def each(steps, chosen, fn):
        for b, t, way, ok in steps:
            for i in range(n):
                if chosen(i, t):
                    when(ok, partial(fn, i, b, t, way))

    steps = planes(s, ns)
    levels = [[q for q in steps if q[1] == t] for t in range(ns)]
    straight = [(b, 1, 0, True) for b in planes_off]
    lag = max(ns - 2, 1)
    each(levels[0], lambda i, t: not late[i], onward)

    def arrive_straight(i, b, t, way):
        dcopy(i, b, b).wait_recv()
        onward(i, b, t, way)

    def part(t):
        if work is not None and t < ns:
            work(t, ns, more_in, more_out)

    part(0)
    each(straight, lambda i, t: direct[i], arrive_straight)
    for t in range(1, ns + lag):
        if t < ns:
            each(levels[t], lambda i, t: in_z(i) and not late[i], arrive)
        if t == lag:
            each(levels[0], lambda i, t: late[i], onward)
        part(t)
        if t <= ns:
            each(levels[t - 1], lambda i, t: relay[i] and in_plane(i, t), lambda i, b, t, way: pass_on(i, b))
        if 1 <= t - lag:
            each(levels[t - lag], lambda i, t: late[i], arrive)
    each(steps, lambda i, t: in_plane(i, t) and not direct[i], lambda i, b, t, way: settle(i, b))
    each(levels[0] + straight, lambda i, t: direct[i], lambda i, b, t, way: settle(i, b))
    each(steps, lambda i, t: (t == 0 or in_z(i)) and not direct[i], finish)
    each(levels[0] + straight, lambda i, t: direct[i], finish)


def gather(collective, mesh_shape, items, work=None, work_args=(), work_out=None):
    ns, nd = mesh_shape["shard"], mesh_shape["dp"]
    modes = tuple(mode for _, mode in items)
    lead = {"z": (ns,), "plane": (nd,), "all": (ns, nd, 2), "swap": ()}
    shapes = [jax.ShapeDtypeStruct(lead[mode] + a.shape, a.dtype) for a, mode in items]
    sems = []
    dma = pltpu.SemaphoreType.DMA
    for _ in items:
        sems += [dma((2, ns)), dma((ns,)), dma((ns, max(nd, 6))), dma((ns, nd, 2)), dma((ns, nd)), dma((ns, nd)),
                 dma(())]
    return pl.pallas_call(
        partial(gather_kernel, ns, nd, modes, work, len(work_args)),
        out_shape=shapes + ([work_out] if work else []),
        in_specs=[pl.BlockSpec(memory_space=pl.ANY)] * len(items)
        + [pl.BlockSpec(memory_space=pltpu.VMEM)] * len(work_args),
        out_specs=[pl.BlockSpec(memory_space=pl.ANY)] * len(items)
        + ([pl.BlockSpec(memory_space=pltpu.VMEM)] if work else []),
        scratch_shapes=sems,
        compiler_params=pltpu.CompilerParams(
            collective_id=collective, has_side_effects=True, vmem_limit_bytes=VMEM_LIMIT),
        cost_estimate=pl.CostEstimate(flops=0, bytes_accessed=1 << 20, transcendentals=0),
    )(*[a for a, _ in items], *work_args)


def reduce_kernel(ns, nd, share, spans, *refs):
    count = len(spans) if spans else 1
    n_in = count + 1 if spans else 1
    ins, outs, scratch = refs[:n_in], refs[n_in : n_in + count], refs[n_in + count :]
    own, sib, give, got, mid, zgot, fin, lsem, ss, sr, ps, pr, zs, zr, fs, fr, ks = scratch
    s, d, m = (lax.axis_index(a) for a in ("shard", "dp", "mp"))
    h, c = fin.shape[1:]
    tile = 16
    greet(ns, nd, True, True, True, z_all=True)
    peers = [lax.rem(d + k, nd) for k in range(1, nd)]
    relay = nd == 4 and h % 32 == 0
    if relay:
        x, y, across = square(d)
        peers = [across, x, y]
    chain = bool(spans)
    if chain:
        order = []
        for k in range(ns - 1):
            up = jnp.where(k < ns - 1 - s, ns - 1 - k, k - (ns - 1 - s))
            down = jnp.where(k < s, k, ns - 1 - (k - s))
            order.append(jnp.where(2 * s < ns, up, down))
        order.append(s)
    else:
        order = [lax.rem(s + k, ns) for k in sorted(range(1, ns), key=lambda k: abs(k - ns // 2))] + [s]
    items = [(a, k, order[k]) for k in range(ns) for a in range(count)]

    def score(a, k, b):
        src = give.at[a, k % 2] if spans else ins[0].at[b, :, 1 - m]
        return pltpu.make_async_remote_copy(
            src, sib.at[a, b], ss.at[a, b], sr.at[a, b], device_id={"mp": 1 - m}, device_id_type=MESH)

    def load(a, b):
        return pltpu.make_async_copy(ins[0].at[b, :, m], own.at[a, b], lsem.at[a, b])

    def multiply(a, b, core, store):
        lo, hi = spans[a]
        step = 512 if c % 512 == 0 else 128
        left = ins[a][b, :, core].reshape(nd * h, hi - lo)

        @pl.loop(0, c // step)
        def _(j):
            cols = pl.ds(pl.multiple_of(j * step, step), step)
            term = cols_product(left, ins[count][cols, lo:hi])
            store(cols, term.astype(BF16).reshape(nd, h, step))

    def zero(a, k, b):
        if not spans:
            score(a, k, b).start()
            load(a, b).start()
            return
        if k >= 2:
            score(a, k - 2, order[k - 2]).wait_send()

        def to_give(cols, v):
            give[a, k % 2, :, :, cols] = v

        def to_own(cols, v):
            own[a, b, :, :, cols] = v

        multiply(a, b, 1 - m, to_give)
        score(a, k, b).start()
        multiply(a, b, m, to_own)

    def pcopy(a, b, src, dst, slot, to):
        return pltpu.make_async_remote_copy(
            src, dst, ps.at[a, b, slot], pr.at[a, b, slot], device_id={"dp": to}, device_id_type=MESH)

    def sends(a, b):
        if not relay:
            return [pltpu.make_async_remote_copy(
                own.at[a, b, e], got.at[a, b, d], ps.at[a, b, e], pr.at[a, b, d],
                device_id={"dp": e}, device_id_type=MESH) for e in peers]
        half = h // 2
        first, last = pl.ds(0, half), pl.ds(half, half)
        return [
            pcopy(a, b, own.at[a, b, across, first], got.at[a, b, 0, first], 0, x),
            pcopy(a, b, own.at[a, b, across, last], got.at[a, b, 0, last], 1, y),
            pcopy(a, b, own.at[a, b, x], got.at[a, b, 1], 2, x),
            pcopy(a, b, own.at[a, b, y], got.at[a, b, 2], 3, y),
        ]

    def zcopy(a, b, to):
        return pltpu.make_async_remote_copy(
            mid.at[a, b], zgot.at[a, to], zs.at[a, b], zr.at[a, to], device_id={"shard": b}, device_id_type=MESH)

    def sum_rows(lo, hi, terms, store):
        @pl.loop(lo // tile, hi // tile)
        def _(r):
            at = pl.ds(pl.multiple_of(r * tile, tile), tile)
            v = terms[0](at).astype(F32)
            for f in terms[1:]:
                v = v + f(at).astype(F32)
            store(at, v.astype(BF16))

    def to_own(a, b, e):
        def store(at, v):
            own[a, b, e, at] = v
        return store

    def one(a, k, b):
        score(a, k, b).wait_recv()
        if not spans:
            load(a, b).wait()
        out_now = sends(a, b)
        for j, e in enumerate(peers + [d]):
            sum_rows(0, h, [lambda at, e=e: own[a, b, e, at], lambda at, e=e: sib[a, b, e, at]], to_own(a, b, e))
            if relay and j == 0:
                out_now[0].start()
                out_now[1].start()
            elif not relay and j < len(peers):
                out_now[j].start()

    def two(a, k, b):
        if not relay:
            return
        half = h // 2
        c0, c1, c2, c3 = sends(a, b)
        c0.wait_recv()
        sum_rows(0, half, [lambda at: own[a, b, y, at], lambda at: got[a, b, 0, at]], to_own(a, b, y))
        c3.start()
        c1.wait_recv()
        sum_rows(half, h, [lambda at: own[a, b, x, at], lambda at: got[a, b, 0, at]], to_own(a, b, x))
        c2.start()

    def plane_terms(a, b):
        slots = [1, 2] if relay else peers
        return [lambda at: own[a, b, d, at]] + [lambda at, e=e: got[a, b, e, at] for e in slots]

    def three(a, k, b):
        if relay:
            for w in sends(a, b)[2:]:
                w.wait_recv()
        else:
            for e in peers:
                pltpu.make_async_remote_copy(
                    own.at[a, b, e], got.at[a, b, e], ps.at[a, b, e], pr.at[a, b, e],
                    device_id={"dp": e}, device_id_type=MESH).wait_recv()
        if k < ns - 1:
            def store(at, v):
                mid[a, b, at] = v
            sum_rows(0, h, plane_terms(a, b), store)
            if not chain:
                zcopy(a, b, s).start()

    def hop(a, b, way):
        slot = jnp.where(s + way == b, jnp.where(way > 0, b, ns), b)
        return pltpu.make_async_remote_copy(
            mid.at[a, b], zgot.at[a, slot], zs.at[a, b], zr.at[a, slot],
            device_id={"shard": s + way}, device_id_type=MESH)

    def came(a, slot):
        return pltpu.make_async_remote_copy(
            mid.at[a, s], zgot.at[a, slot], zs.at[a, s], zr.at[a, slot], device_id={"mp": 1 - m},
            device_id_type=MESH)

    def four(a, k, b):
        if k == ns - 1:
            return

        def add():
            came(a, b).wait_recv()

            def store(at, v):
                mid[a, b, at] = v
            sum_rows(0, h, [lambda at: mid[a, b, at], lambda at: zgot[a, b, at]], store)

        upward = b > s
        pl.when(jnp.where(upward, s > 0, s < ns - 1))(add)
        pl.when(upward)(lambda: hop(a, b, 1).start())
        pl.when(jnp.logical_not(upward))(lambda: hop(a, b, -1).start())

    stages = [zero, one, two, three] + ([four] if chain else [])
    if not spans:
        for item in items:
            zero(*item)
        stages = stages[1:]
    for t in range(len(items) + len(stages) - 1):
        for j, stage in enumerate(stages):
            if 0 <= t - j < len(items):
                stage(*items[t - j])

    def give_out(a, core):
        return pltpu.make_async_remote_copy(
            fin.at[a], outs[a].at[core], fs.at[a], fr.at[a], device_id={"mp": 1 - m}, device_id_type=MESH)

    def keep(a):
        return pltpu.make_async_copy(fin.at[a], outs[a].at[m] if share else outs[a], ks.at[a])

    others = order[:-1]
    for a in range(count):
        def store(at, v, a=a):
            fin[a, at] = v

        if chain:
            sum_rows(0, h, plane_terms(a, s), store)
            for slot, ok in ((s, s > 0), (ns, s < ns - 1)):

                def add(slot=slot):
                    came(a, slot).wait_recv()
                    sum_rows(0, h, [lambda at: fin[a, at], lambda at: zgot[a, slot, at]], store)

                pl.when(ok)(add)
        else:
            for b in others:
                zcopy(a, b, b).wait_recv()
            sum_rows(0, h, plane_terms(a, s) + [lambda at, b=b: zgot[a, b, at] for b in others], store)
        if share:
            give_out(a, m).start()
        keep(a).start()
    for a in range(count):
        if share:
            give_out(a, 1 - m).wait_recv()
            give_out(a, m).wait_send()
        keep(a).wait()
        for k, b in enumerate(order):
            if not spans or k >= ns - 2:
                score(a, k, b).wait_send()
            for w in sends(a, b):
                w.wait_send()
        for b in others:
            zcopy(a, b, s).wait_send()


def reduce_scatter(collective, mesh_shape, share, blocks, terms=None, factors=None, weight=None):
    ns, nd = mesh_shape["shard"], mesh_shape["dp"]
    rows, c = blocks
    h = rows // 2
    count = len(factors) if factors else 1
    size = ns * nd * h * c * 2
    if size * count * 3 > (40 << 20):
        whole = [terms] if factors is None else [
            cols_product(x, weight[:, lo:hi]).astype(BF16) for x, lo, hi in factors]
        sums = []
        for p in whole:
            total = lax.psum_scatter(p.reshape(ns * nd, 2, h, c), TOK, scatter_dimension=0, tiled=True)[0]
            total = lax.psum(total, "mp")
            sums.append(total if share else lax.dynamic_index_in_dim(total, lax.axis_index("mp"), 0, False))
        return sums
    if factors is None:
        spans = None
        args = [terms.reshape(ns, nd, 2, h, c)]
        in_specs = [pl.BlockSpec(memory_space=pl.ANY)]
        give = (1, 1, 1, 16, 128)
    else:
        spans = tuple((lo, hi) for _, lo, hi in factors)
        args = [x.reshape(ns, nd, 2, h, hi - lo) for x, lo, hi in factors] + [weight]
        in_specs = [pl.BlockSpec(memory_space=pltpu.VMEM)] * (count + 1)
        give = (count, 2, nd, h, c)
    slots = 3 if nd == 4 and h % 32 == 0 else nd
    dma = pltpu.SemaphoreType.DMA
    return pl.pallas_call(
        partial(reduce_kernel, ns, nd, share, spans),
        out_shape=[jax.ShapeDtypeStruct((2, h, c) if share else (h, c), BF16)] * count,
        in_specs=in_specs,
        out_specs=[pl.BlockSpec(memory_space=pl.ANY)] * count,
        scratch_shapes=[
            pltpu.VMEM((count, ns, nd, h, c), BF16),
            pltpu.VMEM((count, ns, nd, h, c), BF16),
            pltpu.VMEM(give, BF16),
            pltpu.VMEM((count, ns, slots, h, c), BF16),
            pltpu.VMEM((count, ns, h, c), BF16),
            pltpu.VMEM((count, ns + 1, h, c), BF16),
            pltpu.VMEM((count, h, c), BF16),
            dma((count, ns)), dma((count, ns)), dma((count, ns)),
            dma((count, ns, max(nd, 4))), dma((count, ns, max(nd, 4))),
            dma((count, ns)), dma((count, ns + 1)), dma((count,)), dma((count,)), dma((count,)),
        ],
        compiler_params=pltpu.CompilerParams(
            collective_id=collective, has_side_effects=True, vmem_limit_bytes=VMEM_LIMIT),
        cost_estimate=pl.CostEstimate(flops=0, bytes_accessed=1 << 20, transcendentals=0),
    )(*args)


def gelu_both(v):
    root, cube = 0.7978845608028654, 0.044715
    t = jnp.tanh(root * (v + cube * v * v * v))
    slope = 0.5 * (1.0 + t) + 0.5 * v * (1.0 - t * t) * (root * (1.0 + 3.0 * cube * v * v))
    return 0.5 * v * (1.0 + t), slope


def feed_kernel(ns, nd, x, cot, w, act, low, grad, hid, cots, acc, zs, zr, ps, pr, cs, cr, ls, ks):
    s, d, m = (lax.axis_index(a) for a in ("shard", "dp", "mp"))
    h, width = x.shape
    units = w.shape[1] // 3
    relay = nd == 4 and h % 32 == 0
    greet(ns, nd, True, True, True, z_all=True)
    turns = [0] + sorted(range(1, ns), key=lambda k: min(k, ns - k))
    order = [lax.rem(s + k, ns) for k in turns]
    peers = [lax.rem(d + k, nd) for k in range(1, nd)]
    if relay:
        xn, yn, across = square(d)
        peers = [xn, yn, across]

    def zsend(b):
        return pltpu.make_async_remote_copy(
            x, hid.at[s, d, m], zs.at[b], zr.at[s], device_id={"shard": b}, device_id_type=MESH)

    def zrecv(b):
        return pltpu.make_async_remote_copy(
            x, hid.at[b, d, m], zs.at[b], zr.at[b], device_id={"shard": b}, device_id_type=MESH)

    def part(ref, k):
        return ref if k is None else ref.at[pl.ds(k * (h // 2), h // 2)]

    def source(b, e, first):
        return x if first else hid.at[b, e, m]

    def psend(b, e, to, slot, k, first):
        return pltpu.make_async_remote_copy(
            part(source(b, e, first), k), part(hid.at[b, e, m], k), ps.at[b, slot], pr.at[b, e, k or 0],
            device_id={"dp": to}, device_id_type=MESH)

    def precv(b, e, k):
        ref = part(hid.at[b, e, m], k)
        return pltpu.make_async_remote_copy(
            ref, ref, ps.at[b, 0], pr.at[b, e, k or 0], device_id={"dp": peers[0]}, device_id_type=MESH)

    def own_sends(b, first):
        if relay:
            return [psend(b, d, xn, 0, 0, first), psend(b, d, yn, 1, 1, first),
                    psend(b, d, xn, 2, 1, first), psend(b, d, yn, 3, 0, first)]
        return [psend(b, d, e, j, None, first) for j, e in enumerate(peers)]

    def pass_sends(b):
        if relay:
            return [(precv(b, xn, 0), psend(b, xn, yn, 4, 0, False)),
                    (precv(b, yn, 1), psend(b, yn, xn, 5, 1, False))]
        return []

    def share(b, e, core, first=False):
        ref = hid.at[b, e, core]
        return pltpu.make_async_remote_copy(
            x if first else ref, ref, cs.at[b, e], cr.at[b, e], device_id={"mp": 1 - m}, device_id_type=MESH)

    def load(b):
        return pltpu.make_async_copy(cot.at[b], cots.at[b], ls.at[b])

    def begin(k):
        b = order[k]
        if k > 0:
            zrecv(b).wait_recv()
        for c in own_sends(b, k == 0):
            c.start()
        share(b, d, m, k == 0).start()

    def hand_on(k):
        for got, on in pass_sends(order[k]):
            got.wait_recv()
            on.start()

    def settle(k):
        b = order[k]
        for e in peers:
            for q in waits(e):
                precv(b, e, q).wait_recv()
            share(b, e, m).start()

    def waits(e):
        if not relay:
            return [None]
        return [1] if e is xn else [0] if e is yn else [0, 1]

    def ready(k):
        b = order[k]
        for e in [d] + peers:
            share(b, e, 1 - m).wait_recv()
        if k == 0:
            keep.wait()
        load(b).wait()

    count = nd // 2 if nd % 2 == 0 else nd

    def forward(k, q):
        b = order[k]
        at = pl.ds(q * count, count)
        rows = count * 2 * h
        pre = product(hid[b, at].reshape(rows, width), w[:, : 2 * units])
        back = product(cots[b, at].reshape(rows, width), w[:, 2 * units :])
        value, slope = gelu_both(pre[:, :units])
        up = pre[:, units:]
        act[b, at] = (value * up).astype(BF16).reshape(count, 2, h, units)
        low[b, at, :, :, :units] = (back * up * slope).astype(BF16).reshape(count, 2, h, units)
        low[b, at, :, :, units:] = (back * value).astype(BF16).reshape(count, 2, h, units)

    def backward(k):
        b = order[k]
        rows = nd * 2 * h
        step = 512 if width % 512 == 0 else 128
        lows = low[b].reshape(rows, 2 * units)
        acts = act[b].reshape(rows, units)

        @pl.loop(0, width // step)
        def _(j):
            at = pl.ds(pl.multiple_of(j * step, step), step)
            one = rows_product(hid[b, :, :, :, at].reshape(rows, step), lows)
            two = rows_product(cots[b, :, :, :, at].reshape(rows, step), acts)
            if k > 0:
                one = one + acc[at, : 2 * units]
                two = two + acc[at, 2 * units :]
            if k < ns - 1:
                acc[at, : 2 * units] = one
                acc[at, 2 * units :] = two
            else:
                grad[at, : 2 * units] = one.astype(BF16)
                grad[at, 2 * units :] = two.astype(BF16)

    for b in order[1:]:
        zsend(b).start()
    keep = pltpu.make_async_copy(x, hid.at[s, d, m], ks)
    keep.start()
    begin(0)
    for b in order:
        load(b).start()
    if ns > 1:
        begin(1)
    hand_on(0)
    if ns > 2:
        begin(2)
    for k in range(ns):
        settle(k)
        ready(k)
        forward(k, 0)
        if k + 1 < ns:
            hand_on(k + 1)
        if k + 3 < ns:
            begin(k + 3)
        if count < nd:
            forward(k, 1)
        backward(k)
    for k, b in enumerate(order):
        for c in own_sends(b, k == 0):
            c.wait_send()
        for _, c in pass_sends(b):
            c.wait_send()
        for e in [d] + peers:
            share(b, e, m).wait_send()
        if k > 0:
            zsend(b).wait_send()


def feed(collective, mesh_shape, x, cot, w):
    ns, nd = mesh_shape["shard"], mesh_shape["dp"]
    h, width = x.shape
    units = w.shape[1] // 3
    rows = (ns, nd, 2, h)
    if 2 * cot.size * 2 > (24 << 20):
        (hid,) = gather(collective, mesh_shape, [(x, "all")])
        hid, cot = hid.reshape(-1, width), cot.reshape(-1, width)
        pre = product(hid, w[:, : 2 * units])
        back = product(cot, w[:, 2 * units :])
        value, slope = gelu_both(pre[:, :units])
        up = pre[:, units:]
        act = (value * up).astype(BF16)
        low = jnp.concatenate([back * up * slope, back * value], axis=1).astype(BF16)
        grad = jnp.concatenate([rows_product(hid, low), rows_product(cot, act)], axis=1).astype(BF16)
        return act, low, grad
    dma = pltpu.SemaphoreType.DMA
    vmem = pl.BlockSpec(memory_space=pltpu.VMEM)
    act, low, grad = pl.pallas_call(
        partial(feed_kernel, ns, nd),
        out_shape=[
            jax.ShapeDtypeStruct(rows + (units,), BF16),
            jax.ShapeDtypeStruct(rows + (2 * units,), BF16),
            jax.ShapeDtypeStruct((width, 3 * units), BF16),
        ],
        in_specs=[vmem, pl.BlockSpec(memory_space=pl.ANY), vmem],
        out_specs=[vmem] * 3,
        scratch_shapes=[
            pltpu.VMEM(rows + (width,), BF16),
            pltpu.VMEM(rows + (width,), BF16),
            pltpu.VMEM((width, 3 * units), F32),
            dma((ns,)), dma((ns,)), dma((ns, max(nd, 6))), dma((ns, nd, 2)), dma((ns, nd)), dma((ns, nd)),
            dma((ns,)), dma(()),
        ],
        compiler_params=pltpu.CompilerParams(
            collective_id=collective, has_side_effects=True, vmem_limit_bytes=VMEM_LIMIT),
        cost_estimate=pl.CostEstimate(flops=0, bytes_accessed=1 << 20, transcendentals=0),
    )(x, cot, w)
    return act.reshape(-1, units), low.reshape(-1, 2 * units), grad


def plane_kernel(ns, nd, p, out, own, sib, ls, ss, sr, ps, pr, fs, fr, ks):
    d, m = lax.axis_index("dp"), lax.axis_index("mp")
    h, c = own.shape[1:]
    tile = 16
    greet(ns, nd, False, True, True)
    peers = [lax.rem(d + k, nd) for k in range(1, nd)]
    order = ([square(d)[2], square(d)[0], square(d)[1]] if nd == 4 else peers) + [d]
    other = {"mp": 1 - m}

    def score(e):
        return pltpu.make_async_remote_copy(
            p.at[e, 1 - m], sib.at[e], ss.at[e], sr.at[e], device_id=other, device_id_type=MESH)

    def load(e):
        return pltpu.make_async_copy(p.at[e, m], own.at[e], ls.at[e])

    def send(e, block):
        return pltpu.make_async_remote_copy(
            own.at[e], out.at[block, m], ps.at[e], pr.at[block], device_id={"dp": e}, device_id_type=MESH)

    def share(e, core):
        src = own.at[d] if e is d else out.at[e, m]
        return pltpu.make_async_remote_copy(
            src, out.at[e, core], fs.at[e], fr.at[e], device_id=other, device_id_type=MESH)

    for e in order:
        score(e).start()
        load(e).start()
    for e in order:
        score(e).wait_recv()
        load(e).wait()

        @pl.loop(0, h // tile)
        def _(r, e=e):
            at = pl.ds(pl.multiple_of(r * tile, tile), tile)
            own[e, at] = (own[e, at].astype(F32) + sib[e, at].astype(F32)).astype(BF16)

        if e is not d:
            send(e, d).start()
    keep = pltpu.make_async_copy(own.at[d], out.at[d, m], ks)
    keep.start()
    share(d, m).start()
    for e in order[:-1]:
        send(e, e).wait_recv()
        share(e, m).start()
    keep.wait()
    for e in order:
        share(e, 1 - m).wait_recv()
        share(e, m).wait_send()
        score(e).wait_send()
        if e is not d:
            send(e, d).wait_send()


def plane_reduce(collective, mesh_shape, p):
    ns, nd = mesh_shape["shard"], mesh_shape["dp"]
    h, c = p.shape[2:]
    dma = pltpu.SemaphoreType.DMA
    return pl.pallas_call(
        partial(plane_kernel, ns, nd),
        out_shape=jax.ShapeDtypeStruct(p.shape, BF16),
        in_specs=[pl.BlockSpec(memory_space=pl.ANY)],
        out_specs=pl.BlockSpec(memory_space=pl.ANY),
        scratch_shapes=[pltpu.VMEM((nd, h, c), BF16)] * 2 + [dma((nd,))] * 7 + [dma(())],
        compiler_params=pltpu.CompilerParams(
            collective_id=collective, has_side_effects=True, vmem_limit_bytes=VMEM_LIMIT),
        cost_estimate=pl.CostEstimate(flops=0, bytes_accessed=1 << 20, transcendentals=0),
    )(p)


def rope_tables(positions):
    half_dim = HEAD_DIM // 2
    exponent = jnp.arange(half_dim, dtype=F32) * (-2.0 / HEAD_DIM)
    angles = positions.astype(F32)[:, None] * jnp.power(ROPE_BASE, exponent)[None, :]
    return (jnp.cos(angles), jnp.sin(angles))


def rotate(values, cosine, sine_rows):
    half_dim = values.shape[-1] // 2
    front_half = values[..., :half_dim]
    back_half = values[..., half_dim:]
    return jnp.concatenate(
        [front_half * cosine - back_half * sine_rows, back_half * cosine + front_half * sine_rows], axis=-1)


def rows_product(left_side, right_side):
    return lax.dot_general(
        left_side, right_side, (((0,), (0,)), ((), ())), preferred_element_type=F32)


def cols_product(left_side, right_side):
    return lax.dot_general(
        left_side, right_side, (((1,), (1,)), ((), ())), preferred_element_type=F32)


def product(left_side, right_side):
    return jnp.dot(left_side, right_side, preferred_element_type=F32)


def pack(part, parts, ins, outs):
    gateup, down = ins
    (out,) = outs
    n, _, columns = out.shape
    units = columns // 3
    full = down.shape[1] // units
    share = -(-n // parts)
    for j in range(part * share, min((part + 1) * share, n)):
        if j >= full:
            out[j] = jnp.zeros(out.shape[1:], BF16)
            continue
        at = pl.ds(j * units, units)
        out[j, :, :units] = gateup[:, 0, at]
        out[j, :, units : 2 * units] = gateup[:, 1, at]
        out[j, :, 2 * units :] = down[:, at]


def adam_step(rates, grad, weight, first, second, decay):
    first_new = BETA_ONE * first + (1.0 - BETA_ONE) * grad
    second_new = BETA_TWO * second + (1.0 - BETA_TWO) * grad * grad
    direction = first_new * rates[0] / (jnp.sqrt(second_new * rates[1]) + ADAM_EPS)
    return first_new, second_new, -LEARN_RATE * (direction + decay * weight.astype(F32))


def unpack_kernel(rates, got, gw, gf, gs, dw, df, ds, gg, gfn, gsn, gu, dg, dfn, dsn, du):
    units = dw.shape[1]
    pair = (rates[0], rates[1])
    for k in range(2):
        grad = got[0, :, k * units : (k + 1) * units].astype(F32)
        gg[:, k, :] = grad
        gfn[:, k, :], gsn[:, k, :], gu[:, k, :] = adam_step(
            pair, grad, gw[:, k, :], gf[:, k, :], gs[:, k, :], DECAY_RATE)
    grad = got[0, :, 2 * units :].astype(F32)
    dg[...] = grad
    dfn[...], dsn[...], du[...] = adam_step(pair, grad, dw[...], df[...], ds[...], DECAY_RATE)


def unpack_adam(units, rates, got, gateup, down):
    own_d, _, ff_local = gateup[0].shape
    three = pl.BlockSpec((own_d, 2, units), lambda j: (0, 0, j))
    two = pl.BlockSpec((own_d, units), lambda j: (0, j))
    shape3 = jax.ShapeDtypeStruct(gateup[0].shape, F32)
    shape2 = jax.ShapeDtypeStruct(down[0].shape, F32)
    out = pl.pallas_call(
        unpack_kernel,
        out_shape=[shape3] * 4 + [shape2] * 4,
        grid=(ff_local // units,),
        in_specs=[
            pl.BlockSpec(memory_space=pltpu.SMEM),
            pl.BlockSpec((1, own_d, 3 * units), lambda j: (j, 0, 0)),
        ] + [three] * 3 + [two] * 3,
        out_specs=[three] * 4 + [two] * 4,
        compiler_params=pltpu.CompilerParams(vmem_limit_bytes=VMEM_LIMIT),
    )(rates, got, *gateup, *down)
    return out[:4], out[4:]


def shards(
    mesh_shape,
    tokens_in,
    segment_ids,
    block_cotangent,
    query_weight,
    keyval_weight,
    outproj_weight,
    gateup_weight,
    down_weight,
    norm_gains,
    query_first,
    keyval_first,
    outproj_first,
    gateup_first,
    down_first,
    gains_first,
    query_second,
    keyval_second,
    outproj_second,
    gateup_second,
    down_second,
    gains_second,
    step_count,
):
    ns, nd = mesh_shape["shard"], mesh_shape["dp"]
    n = ns * nd
    s, d, m = (lax.axis_index(a) for a in ("shard", "dp", "mp"))
    me = s * nd + d
    tok, width = tokens_in.shape
    own_d = query_weight.shape[0]
    q_cols = query_weight.shape[1]
    heads_local = q_cols // HEAD_DIM
    ff_local = gateup_weight.shape[2]
    units = -(-(-(-ff_local // n)) // 128) * 128
    ff_pad = units * n - ff_local
    half = tok // 2
    plane_tok = nd * tok
    plane_d = ns * own_d

    input_rows = tokens_in.astype(F32)
    inverse_one = lax.rsqrt(jnp.mean(input_rows * input_rows, axis=1) + EPS_NORM)
    lanes = max(256, -(-max(own_d, tok) // 128) * 128)

    def line(v):
        return jnp.pad(v, ((0, 0), (0, lanes - v.shape[1])))

    small = jnp.concatenate(
        [line(norm_gains.astype(F32)), line(segment_ids.astype(F32)[None]), line(inverse_one[None]),
         jnp.zeros((4, lanes), F32)], axis=0)
    qkv_weight = jnp.concatenate(
        [query_weight, lax.dynamic_slice_in_dim(keyval_weight, m * HEAD_DIM, HEAD_DIM, 1)], axis=1)

    def plane_cut(value):
        return value.reshape(tok, ns, nd, own_d).transpose(2, 0, 1, 3).reshape(nd, tok, plane_d)

    small_all, tokens_plane, cot_all, qkv_plane, three = gather(
        0, mesh_shape,
        [(small, "all"), (plane_cut(tokens_in), "swap"),
         (lax.dynamic_slice_in_dim(block_cotangent, m * half, half, 0), "all"), (qkv_weight, "z")],
        pack, (gateup_weight, down_weight.T), jax.ShapeDtypeStruct((n, own_d, 3 * units), BF16))
    tokens_plane = tokens_plane.reshape(plane_tok, plane_d)
    three, tokens_plane = lax.optimization_barrier((three, tokens_plane))
    three = lax.all_to_all(three, TOK, 0, 0, tiled=True).reshape(width, 3 * units)
    qkv_plane = qkv_plane.reshape(plane_d, q_cols + HEAD_DIM)
    small_all = small_all[:, :, 0]
    gains_by = small_all[:, :, :2, :own_d]
    full_gains = gains_by.transpose(2, 0, 1, 3).reshape(2, width)
    tags = small_all[:, :, 2, :tok].reshape(n * tok)
    plane_scale = lax.dynamic_index_in_dim(small_all[:, :, 3, :tok], s, 0, False).reshape(plane_tok, 1)
    plane_gain = lax.dynamic_index_in_dim(gains_by[:, :, 0], d, 1, False).reshape(1, plane_d)


    def from_plane(collective, value):
        got = plane_reduce(collective, mesh_shape, value.reshape(nd, 2, half, plane_d))
        return got.reshape(nd, tok, ns, own_d).transpose(1, 2, 0, 3).reshape(tok, width).astype(F32)

    def plane_sum(collective, value):
        (got,) = gather(collective, mesh_shape, [(value.reshape(nd, tok, -1), "swap")])
        return jnp.sum(got.astype(F32), axis=0)

    hidden_plane = (tokens_plane.astype(F32) * plane_scale * plane_gain).astype(BF16)
    qkv_raw = plane_sum(8, product(hidden_plane, qkv_plane).astype(BF16))

    pad = KV_BLOCKS * tok
    key_span = pad + tok
    start = me * tok
    tag_pad = jnp.concatenate([jnp.full((pad,), -1.0, F32), tags])
    key_tags = lax.dynamic_slice_in_dim(tag_pad, start, key_span, 0)
    own_tags = segment_ids.astype(F32)
    query_index = jnp.arange(tok, dtype=jnp.int32) + pad
    key_index = jnp.arange(key_span, dtype=jnp.int32)
    same_segment = key_tags[None, :] == own_tags[:, None]
    allowed = same_segment & (key_index[None, :] <= query_index[:, None])
    positions = jnp.sum(
        (same_segment & (key_index[None, :] < query_index[:, None])).astype(jnp.int32), axis=1)
    cosine, sine_rows = rope_tables(positions)
    cos_h, sin_h = cosine[:, None, :], sine_rows[:, None, :]
    score_scale = HEAD_DIM ** (-0.5)
    queries = rotate(qkv_raw[:, :q_cols].reshape(tok, heads_local, HEAD_DIM), cos_h, sin_h).astype(BF16)
    kv_raw = qkv_raw[:, q_cols:]
    kv_mine = jnp.where(m == 0, rotate(kv_raw, cosine, sine_rows), kv_raw).astype(BF16)
    (kv_all,) = gather(1, mesh_shape, [(kv_mine, "all")])
    kv_all = kv_all.reshape(n, 2, tok, HEAD_DIM)
    kv_pad = jnp.concatenate([jnp.zeros((KV_BLOCKS, 2, tok, HEAD_DIM), BF16), kv_all], axis=0)
    kv_window = lax.dynamic_slice_in_dim(kv_pad, me, KV_BLOCKS + 1, 0)
    key_rows = kv_window[:, 0].reshape(key_span, HEAD_DIM)
    value_rows = kv_window[:, 1].reshape(key_span, HEAD_DIM)
    scores = jnp.einsum("thd,kd->htk", queries, key_rows, preferred_element_type=F32) * score_scale
    scores = jnp.where(allowed[None], scores, -jnp.inf)
    row_max = jnp.max(scores, axis=2, keepdims=True)
    raw = jnp.exp(scores - row_max)
    probs = raw / jnp.sum(raw, axis=2, keepdims=True)
    probs_low = probs.astype(BF16)
    mixed = jnp.einsum("htk,kd->thd", probs_low, value_rows, preferred_element_type=F32)
    mixed_low = mixed.reshape(tok, q_cols).astype(BF16)
    mixed_plane, outproj_z = gather(
        2, mesh_shape, [(mixed_low, "plane"), (outproj_weight.T, "z")])
    mixed_plane = mixed_plane.reshape(plane_tok, q_cols)
    outproj_plane = outproj_z.reshape(plane_d, q_cols)
    residual = input_rows + from_plane(9, cols_product(mixed_plane, outproj_plane).astype(BF16))
    gain_two = full_gains[1]
    inverse_two = lax.rsqrt(jnp.mean(residual * residual, axis=1, keepdims=True) + EPS_NORM)
    hidden_two = (residual * inverse_two * gain_two).astype(BF16)

    act_low, gateup_low, three_grad = feed(
        3, mesh_shape, lax.dynamic_slice_in_dim(hidden_two, m * half, half, 0), cot_all, three)
    three_grad, act_low, gateup_low = lax.optimization_barrier((three_grad, act_low, gateup_low))
    three_grad = lax.all_to_all(three_grad.reshape(n, own_d, 3 * units), TOK, 0, 0, tiled=True)
    hidden_two_grad, ffn_sum = reduce_scatter(
        4, mesh_shape, True, (tok, width),
        factors=[(gateup_low, 0, 2 * units), (act_low, 2 * units, 3 * units)], weight=three)
    hidden_two_grad = hidden_two_grad.reshape(tok, width).astype(F32)
    ffn_sum = ffn_sum.reshape(tok, width).astype(F32)
    block_out = (residual + ffn_sum).astype(BF16)

    def norm_back(rows, inverse, gain_row, grad):
        normed = rows * inverse
        scaled = grad * gain_row
        inner = jnp.mean(normed * scaled, axis=1, keepdims=True)
        return inverse * (scaled - normed * inner), jnp.sum(grad * normed, axis=0)

    residual_from, gain_two_grad = norm_back(residual, inverse_two, gain_two, hidden_two_grad)
    residual_grad = block_cotangent.astype(F32) + residual_from
    gain_cut = gain_two_grad.reshape(1, ns, nd, own_d).transpose(2, 0, 1, 3).reshape(nd, 1, plane_d)
    attn_low, gain_two_part = gather(
        10, mesh_shape,
        [(plane_cut(residual_grad.astype(BF16)), "swap"), (jnp.pad(gain_cut, ((0, 0), (0, 7), (0, 0))), "swap")])
    attn_low = attn_low.reshape(plane_tok, plane_d)
    gain_two_part = jnp.where(m == 0, jnp.sum(gain_two_part[:, 0], axis=0), 0.0)
    mixed_grad = plane_sum(11, product(attn_low, outproj_plane).astype(BF16))
    mixed_grad = mixed_grad.astype(BF16).reshape(tok, heads_local, HEAD_DIM)

    def z_sum(value):
        got = lax.all_to_all(value, "shard", 0, 0, tiled=True)
        return jnp.sum(got.astype(F32), axis=0)

    outproj_grad = rows_product(attn_low, mixed_plane).astype(BF16)
    outproj_grad, three_grad = lax.optimization_barrier((outproj_grad, three_grad))
    own_outproj = z_sum(outproj_grad.reshape(ns, own_d, q_cols))

    probs_grad = jnp.einsum("thd,kd->htk", mixed_grad, value_rows, preferred_element_type=F32)
    value_grad = jnp.einsum("htk,thd->kd", probs_low, mixed_grad, preferred_element_type=F32)
    inner_sum = jnp.sum(probs * probs_grad, axis=2, keepdims=True)
    scores_low = (probs * (probs_grad - inner_sum) * score_scale).astype(BF16)
    query_rot_grad = jnp.einsum("htk,kd->thd", scores_low, key_rows, preferred_element_type=F32)
    key_rot_grad = jnp.einsum("htk,thd->kd", scores_low, queries, preferred_element_type=F32)
    window_grad = jnp.stack(
        [key_rot_grad.reshape(KV_BLOCKS + 1, tok, HEAD_DIM), value_grad.reshape(KV_BLOCKS + 1, tok, HEAD_DIM)],
        axis=1).astype(BF16)
    kv_grad_pad = lax.dynamic_update_slice_in_dim(
        jnp.zeros((KV_BLOCKS + n, 2, tok, HEAD_DIM), BF16), window_grad, me, 0)
    (kv_grad,) = reduce_scatter(6, mesh_shape, False, (2 * tok, HEAD_DIM), terms=kv_grad_pad[KV_BLOCKS:])
    kv_grad = kv_grad.astype(F32)
    kv_low = jnp.where(m == 0, rotate(kv_grad, cosine, -sine_rows), kv_grad)
    query_low = rotate(query_rot_grad, cos_h, -sin_h).reshape(tok, q_cols)
    qkv_low = jnp.concatenate([query_low, kv_low], axis=1).astype(BF16)
    (qkv_low_plane,) = gather(7, mesh_shape, [(qkv_low, "plane")])
    qkv_low_plane = qkv_low_plane.reshape(plane_tok, q_cols + HEAD_DIM)
    hidden_one_part = cols_product(qkv_low_plane, qkv_plane).astype(BF16)
    gain_one_part = jnp.sum(hidden_one_part.astype(F32) * (tokens_plane.astype(F32) * plane_scale), axis=0)
    hidden_one_grad = from_plane(12, hidden_one_part)
    gain_parts = jnp.stack([gain_one_part, gain_two_part], axis=1)
    qkv_grad = jnp.concatenate(
        [rows_product(hidden_plane, qkv_low_plane), jnp.pad(gain_parts, ((0, 0), (0, 126)))], axis=1).astype(BF16)
    qkv_grad, own_outproj = lax.optimization_barrier((qkv_grad, own_outproj))
    own_qkv = z_sum(qkv_grad.reshape(ns, own_d, -1))
    own_query = own_qkv[:, :q_cols]
    rest = own_qkv[:, q_cols:]
    rest_other = lax.ppermute(rest, "mp", [(0, 1), (1, 0)])
    kv_own, kv_other = rest[:, :HEAD_DIM], rest_other[:, :HEAD_DIM]
    own_keyval = jnp.where(
        m == 0, jnp.concatenate([kv_own, kv_other], axis=1), jnp.concatenate([kv_other, kv_own], axis=1))
    own_gains = (rest + rest_other)[:, HEAD_DIM : HEAD_DIM + 2].T

    inverse_col = inverse_one[:, None]
    input_from, _ = norm_back(input_rows, inverse_col, full_gains[0], hidden_one_grad)
    input_grad = residual_grad + input_from
    step_value = step_count[0].astype(F32)
    bias_first = 1.0 - jnp.power(BETA_ONE, step_value)
    bias_second = 1.0 - jnp.power(BETA_TWO, step_value)
    rates = jnp.stack([1.0 / bias_first, 1.0 / bias_second])
    gateup_news, down_news = unpack_adam(
        units, rates, three_grad, (gateup_weight, gateup_first, gateup_second),
        (down_weight.T, down_first.T, down_second.T))
    down_news = [x.T for x in down_news]

    def adam(grad, weight, first, second, decay):
        return (grad,) + adam_step(rates, grad, weight, first, second, decay)

    news = [
        adam(own_query, query_weight, query_first, query_second, DECAY_RATE),
        adam(own_keyval, keyval_weight, keyval_first, keyval_second, DECAY_RATE),
        tuple(v.T for v in adam(own_outproj, outproj_weight.T, outproj_first.T, outproj_second.T, DECAY_RATE)),
        gateup_news,
        down_news,
        adam(own_gains, norm_gains, gains_first, gains_second, 0.0),
    ]
    return (block_out, input_grad) + tuple(x[k] for k in range(4) for x in news)


def solution(mesh):
    rows, split_q, split_o = P(TOK, None), P(TOK, "mp"), P("mp", TOK)
    params = (split_q, rows, split_o, P(TOK, None, "mp"), split_o, P(None, TOK))
    in_specs = (rows, P(TOK), rows) + params * 3 + (P(),)
    out_specs = (rows, rows) + params * 4
    return jax.shard_map(
        partial(shards, dict(mesh.shape)), mesh=mesh, in_specs=in_specs, out_specs=out_specs, check_vma=False)
```

```python
from functools import partial

import jax
import jax.numpy as jnp
from jax import lax
from jax.experimental import pallas as pl
from jax.experimental.pallas import tpu as pltpu
from jax.sharding import PartitionSpec as P

HEAD_DIM = 256
KV_BLOCKS = 8

EPS_NORM = 1e-06
BETA_ONE = 0.9
BETA_TWO = 0.95
ADAM_EPS = 1e-08
LEARN_RATE = 0.01
DECAY_RATE = 0.1
ROPE_BASE = 10000.0

MESH = pl.DeviceIdType.MESH
TOK = ("shard", "dp")
VMEM_LIMIT = 56 << 20
F32 = jnp.float32
BF16 = jnp.bfloat16


def when(cond, fn):
    if cond is True:
        fn()
    else:
        pl.when(cond)(fn)


def planes(s, ns, far_first=False):
    steps = [(s, 0, 0, True)]
    for t in range(1, ns):
        steps.append((s - t, t, 1, s - t >= 0))
        steps.append((s + t, t, -1, s + t < ns))
    return steps[::-1] if far_first else steps


def greet(ns, nd, use_z, use_plane, use_core, z_all=False):
    s, d, m = (lax.axis_index(a) for a in ("shard", "dp", "mp"))
    bar = pltpu.get_barrier_semaphore()

    def hello(dev):
        pl.semaphore_signal(bar, 1, device_id=dev, device_id_type=MESH)

    count = 0
    if use_z and z_all:
        for k in range(1, ns):
            hello({"shard": lax.rem(s + k, ns)})
        count += ns - 1
    elif use_z:
        when(s < ns - 1, lambda: hello({"shard": s + 1}))
        when(s > 0, lambda: hello({"shard": s - 1}))
        count = (s < ns - 1).astype(jnp.int32) + (s > 0).astype(jnp.int32)
    if use_plane:
        for k in range(1, nd):
            hello({"dp": lax.rem(d + k, nd)})
        count += nd - 1
    if use_core:
        hello({"mp": 1 - m})
        count += 1
    pl.semaphore_wait(bar, count)


def square(d):
    low = lax.rem(d, 2)
    x = d + 1 - 2 * low
    y = lax.rem(d + 2, 4)
    return x, y, lax.rem(x + 2, 4)


def gather_kernel(ns, nd, modes, work, n_work, *refs):
    n = len(modes)
    ins, more_in = refs[:n], refs[n : n + n_work]
    outs, more_out = refs[n + n_work : 2 * n + n_work], refs[2 * n + n_work : 2 * n + 2 * n_work - (n_work > 0)]
    sems = refs[-7 * n :]
    s, d, m = (lax.axis_index(a) for a in ("shard", "dp", "mp"))
    use_z = any(k in ("z", "all") for k in modes)
    use_plane = any(k in ("plane", "all", "swap") for k in modes)
    direct = [modes[i] == "all" and ins[i].size * ins[i].dtype.itemsize < 128 << 10 for i in range(n)]
    late = [modes[i] == "z" and any(k == "all" and not q for k, q in zip(modes, direct)) for i in range(n)]
    greet(ns, nd, use_z, use_plane, "all" in modes, z_all=any(direct))
    peers = [lax.rem(d + k, nd) for k in range(1, nd)]
    relay = [
        nd == 4 and modes[i] in ("all", "plane") and ins[i].shape[0] % 32 == 0 and not direct[i] for i in range(n)]
    if nd == 4:
        x, y, across = square(d)

    def place(i, b, e, core):
        if modes[i] == "z":
            return outs[i].at[b]
        if modes[i] in ("plane", "swap"):
            return outs[i].at[e]
        return outs[i].at[b, e, core]

    def half_of(i, ref, k):
        if k is None:
            return ref
        rows = ins[i].shape[0] // 2
        return ref.at[pl.ds(k * rows, rows)]

    def zcopy(i, b, way, first):
        src = ins[i] if first else place(i, b, d, m)
        return pltpu.make_async_remote_copy(
            src, place(i, b, d, m), sems[7 * i].at[(way + 1) // 2, b], sems[7 * i + 1].at[b],
            device_id={"shard": s + way}, device_id_type=MESH)

    def pcopy(i, b, to, slot, first, e=None, k=None):
        e = d if e is None else e
        src = (ins[i].at[to] if modes[i] == "swap" else ins[i]) if first else place(i, b, e, m)
        return pltpu.make_async_remote_copy(
            half_of(i, src, k), half_of(i, place(i, b, e, m), k),
            sems[7 * i + 2].at[b, slot], sems[7 * i + 3].at[b, e, k or 0],
            device_id={"dp": to}, device_id_type=MESH)

    def precv(i, b, e, k=None):
        ref = place(i, b, e, m)
        return pltpu.make_async_remote_copy(
            half_of(i, ref, k), half_of(i, ref, k), sems[7 * i + 2].at[b, 0], sems[7 * i + 3].at[b, e, k or 0],
            device_id={"dp": peers[0]}, device_id_type=MESH)

    def own_copies(i, b, first):
        if relay[i]:
            return [pcopy(i, b, x, 0, first, k=0), pcopy(i, b, y, 1, first, k=1),
                    pcopy(i, b, x, 2, first, k=1), pcopy(i, b, y, 3, first, k=0)]
        return [pcopy(i, b, e, j, first) for j, e in enumerate(peers)]

    def pass_copies(i, b):
        return [(precv(i, b, x, 0), pcopy(i, b, y, 4, False, x, 0)),
                (precv(i, b, y, 1), pcopy(i, b, x, 5, False, y, 1))]

    def ccopy(i, b, e, first):
        src = ins[i] if first else place(i, b, e, m)
        return pltpu.make_async_remote_copy(
            src, place(i, b, e, m), sems[7 * i + 4].at[b, e], sems[7 * i + 5].at[b, e],
            device_id={"mp": 1 - m}, device_id_type=MESH)

    def crecv(i, b, e):
        ref = place(i, b, e, 1 - m)
        return pltpu.make_async_remote_copy(
            ref, ref, sems[7 * i + 4].at[b, e], sems[7 * i + 5].at[b, e],
            device_id={"mp": 1 - m}, device_id_type=MESH)

    def dcopy(i, to, block):
        return pltpu.make_async_remote_copy(
            ins[i], place(i, block, d, m), sems[7 * i].at[0, to], sems[7 * i + 1].at[block],
            device_id={"shard": to}, device_id_type=MESH)

    planes_off = [lax.rem(s + k, ns) for k in range(1, ns)]

    def lcopy(i):
        src = ins[i].at[d] if modes[i] == "swap" else ins[i]
        return pltpu.make_async_copy(src, place(i, s, d, m), sems[7 * i + 6])

    def in_z(i):
        return modes[i] in ("z", "all") and not direct[i]

    def in_plane(i, t):
        return modes[i] == "all" or (modes[i] in ("plane", "swap") and t == 0)

    def onward(i, b, t, way):
        first = t == 0
        if in_z(i):
            if way >= 0:
                when(s < ns - 1, lambda: zcopy(i, b, 1, first).start())
            if way <= 0:
                when(s > 0, lambda: zcopy(i, b, -1, first).start())
        if in_plane(i, t):
            for c in own_copies(i, b, first):
                c.start()
        if modes[i] == "all":
            ccopy(i, b, d, first).start()
        if first and direct[i]:
            for p in planes_off:
                dcopy(i, p, s).start()
        if first:
            lcopy(i).start()

    def arrive(i, b, t, way):
        zcopy(i, b, -way, False).wait_recv()
        onward(i, b, t, way)

    def pass_on(i, b):
        for got, on in pass_copies(i, b):
            got.wait_recv()
            on.start()

    def settle(i, b):
        if relay[i]:
            waits = [(x, [precv(i, b, x, 1)]), (y, [precv(i, b, y, 0)]),
                     (across, [precv(i, b, across, 0), precv(i, b, across, 1)])]
        else:
            waits = [(e, [precv(i, b, e)]) for e in peers]
        for e, got in waits:
            for w in got:
                w.wait_recv()
            if modes[i] == "all":
                ccopy(i, b, e, False).start()

    def finish(i, b, t, way):
        first = t == 0
        if in_z(i):
            if way >= 0:
                when(s < ns - 1, lambda: zcopy(i, b, 1, first).wait_send())
            if way <= 0:
                when(s > 0, lambda: zcopy(i, b, -1, first).wait_send())
        if in_plane(i, t):
            for c in own_copies(i, b, first):
                c.wait_send()
            if relay[i]:
                for _, on in pass_copies(i, b):
                    on.wait_send()
        if direct[i] and first:
            for p in planes_off:
                dcopy(i, p, s).wait_send()
        if modes[i] == "all":
            for e in [d] + peers:
                crecv(i, b, e).wait_recv()
                ccopy(i, b, e, False).wait_send()
        if first:
            lcopy(i).wait()

    def each(steps, chosen, fn):
        for b, t, way, ok in steps:
            for i in range(n):
                if chosen(i, t):
                    when(ok, partial(fn, i, b, t, way))

    steps = planes(s, ns)
    levels = [[q for q in steps if q[1] == t] for t in range(ns)]
    straight = [(b, 1, 0, True) for b in planes_off]
    lag = max(ns - 2, 1)
    each(levels[0], lambda i, t: not late[i], onward)

    def arrive_straight(i, b, t, way):
        dcopy(i, b, b).wait_recv()
        onward(i, b, t, way)

    def part(t):
        if work is not None and t < ns:
            work(t, ns, more_in, more_out)

    part(0)
    each(straight, lambda i, t: direct[i], arrive_straight)
    for t in range(1, ns + lag):
        if t < ns:
            each(levels[t], lambda i, t: in_z(i) and not late[i], arrive)
        if t == lag:
            each(levels[0], lambda i, t: late[i], onward)
        part(t)
        if t <= ns:
            each(levels[t - 1], lambda i, t: relay[i] and in_plane(i, t), lambda i, b, t, way: pass_on(i, b))
        if 1 <= t - lag:
            each(levels[t - lag], lambda i, t: late[i], arrive)
    each(steps, lambda i, t: in_plane(i, t) and not direct[i], lambda i, b, t, way: settle(i, b))
    each(levels[0] + straight, lambda i, t: direct[i], lambda i, b, t, way: settle(i, b))
    each(steps, lambda i, t: (t == 0 or in_z(i)) and not direct[i], finish)
    each(levels[0] + straight, lambda i, t: direct[i], finish)


def gather(collective, mesh_shape, items, work=None, work_args=(), work_out=None):
    ns, nd = mesh_shape["shard"], mesh_shape["dp"]
    modes = tuple(mode for _, mode in items)
    lead = {"z": (ns,), "plane": (nd,), "all": (ns, nd, 2), "swap": ()}
    shapes = [jax.ShapeDtypeStruct(lead[mode] + a.shape, a.dtype) for a, mode in items]
    sems = []
    dma = pltpu.SemaphoreType.DMA
    for _ in items:
        sems += [dma((2, ns)), dma((ns,)), dma((ns, max(nd, 6))), dma((ns, nd, 2)), dma((ns, nd)), dma((ns, nd)),
                 dma(())]
    return pl.pallas_call(
        partial(gather_kernel, ns, nd, modes, work, len(work_args)),
        out_shape=shapes + ([work_out] if work else []),
        in_specs=[pl.BlockSpec(memory_space=pl.ANY)] * len(items)
        + [pl.BlockSpec(memory_space=pltpu.VMEM)] * len(work_args),
        out_specs=[pl.BlockSpec(memory_space=pl.ANY)] * len(items)
        + ([pl.BlockSpec(memory_space=pltpu.VMEM)] if work else []),
        scratch_shapes=sems,
        compiler_params=pltpu.CompilerParams(
            collective_id=collective, has_side_effects=True, vmem_limit_bytes=VMEM_LIMIT),
        cost_estimate=pl.CostEstimate(flops=0, bytes_accessed=1 << 20, transcendentals=0),
    )(*[a for a, _ in items], *work_args)


def reduce_kernel(ns, nd, share, spans, *refs):
    count = len(spans) if spans else 1
    n_in = count + 1 if spans else 1
    ins, outs, scratch = refs[:n_in], refs[n_in : n_in + count], refs[n_in + count :]
    own, sib, give, got, mid, zgot, fin, lsem, ss, sr, ps, pr, zs, zr, fs, fr, ks = scratch
    s, d, m = (lax.axis_index(a) for a in ("shard", "dp", "mp"))
    h, c = fin.shape[1:]
    tile = 16
    greet(ns, nd, True, True, True, z_all=True)
    peers = [lax.rem(d + k, nd) for k in range(1, nd)]
    relay = nd == 4 and h % 32 == 0
    if relay:
        x, y, across = square(d)
        peers = [across, x, y]
    chain = bool(spans)
    if chain:
        order = []
        for k in range(ns - 1):
            up = jnp.where(k < ns - 1 - s, ns - 1 - k, k - (ns - 1 - s))
            down = jnp.where(k < s, k, ns - 1 - (k - s))
            order.append(jnp.where(2 * s < ns, up, down))
        order.append(s)
    else:
        order = [lax.rem(s + k, ns) for k in sorted(range(1, ns), key=lambda k: abs(k - ns // 2))] + [s]
    items = [(a, k, order[k]) for k in range(ns) for a in range(count)]

    def score(a, k, b):
        src = give.at[a, k % 2] if spans else ins[0].at[b, :, 1 - m]
        return pltpu.make_async_remote_copy(
            src, sib.at[a, b], ss.at[a, b], sr.at[a, b], device_id={"mp": 1 - m}, device_id_type=MESH)

    def load(a, b):
        return pltpu.make_async_copy(ins[0].at[b, :, m], own.at[a, b], lsem.at[a, b])

    def multiply(a, b, core, store):
        lo, hi = spans[a]
        step = 512 if c % 512 == 0 else 128
        left = ins[a][b, :, core].reshape(nd * h, hi - lo)

        @pl.loop(0, c // step)
        def _(j):
            cols = pl.ds(pl.multiple_of(j * step, step), step)
            term = cols_product(left, ins[count][cols, lo:hi])
            store(cols, term.astype(BF16).reshape(nd, h, step))

    def zero(a, k, b):
        if not spans:
            score(a, k, b).start()
            load(a, b).start()
            return
        if k >= 2:
            score(a, k - 2, order[k - 2]).wait_send()

        def to_give(cols, v):
            give[a, k % 2, :, :, cols] = v

        def to_own(cols, v):
            own[a, b, :, :, cols] = v

        multiply(a, b, 1 - m, to_give)
        score(a, k, b).start()
        multiply(a, b, m, to_own)

    def pcopy(a, b, src, dst, slot, to):
        return pltpu.make_async_remote_copy(
            src, dst, ps.at[a, b, slot], pr.at[a, b, slot], device_id={"dp": to}, device_id_type=MESH)

    def sends(a, b):
        if not relay:
            return [pltpu.make_async_remote_copy(
                own.at[a, b, e], got.at[a, b, d], ps.at[a, b, e], pr.at[a, b, d],
                device_id={"dp": e}, device_id_type=MESH) for e in peers]
        half = h // 2
        first, last = pl.ds(0, half), pl.ds(half, half)
        return [
            pcopy(a, b, own.at[a, b, across, first], got.at[a, b, 0, first], 0, x),
            pcopy(a, b, own.at[a, b, across, last], got.at[a, b, 0, last], 1, y),
            pcopy(a, b, own.at[a, b, x], got.at[a, b, 1], 2, x),
            pcopy(a, b, own.at[a, b, y], got.at[a, b, 2], 3, y),
        ]

    def zcopy(a, b, to):
        return pltpu.make_async_remote_copy(
            mid.at[a, b], zgot.at[a, to], zs.at[a, b], zr.at[a, to], device_id={"shard": b}, device_id_type=MESH)

    def sum_rows(lo, hi, terms, store):
        @pl.loop(lo // tile, hi // tile)
        def _(r):
            at = pl.ds(pl.multiple_of(r * tile, tile), tile)
            v = terms[0](at).astype(F32)
            for f in terms[1:]:
                v = v + f(at).astype(F32)
            store(at, v.astype(BF16))

    def to_own(a, b, e):
        def store(at, v):
            own[a, b, e, at] = v
        return store

    def one(a, k, b):
        score(a, k, b).wait_recv()
        if not spans:
            load(a, b).wait()
        out_now = sends(a, b)
        for j, e in enumerate(peers + [d]):
            sum_rows(0, h, [lambda at, e=e: own[a, b, e, at], lambda at, e=e: sib[a, b, e, at]], to_own(a, b, e))
            if relay and j == 0:
                out_now[0].start()
                out_now[1].start()
            elif not relay and j < len(peers):
                out_now[j].start()

    def two(a, k, b):
        if not relay:
            return
        half = h // 2
        c0, c1, c2, c3 = sends(a, b)
        c0.wait_recv()
        sum_rows(0, half, [lambda at: own[a, b, y, at], lambda at: got[a, b, 0, at]], to_own(a, b, y))
        c3.start()
        c1.wait_recv()
        sum_rows(half, h, [lambda at: own[a, b, x, at], lambda at: got[a, b, 0, at]], to_own(a, b, x))
        c2.start()

    def plane_terms(a, b):
        slots = [1, 2] if relay else peers
        return [lambda at: own[a, b, d, at]] + [lambda at, e=e: got[a, b, e, at] for e in slots]

    def three(a, k, b):
        if relay:
            for w in sends(a, b)[2:]:
                w.wait_recv()
        else:
            for e in peers:
                pltpu.make_async_remote_copy(
                    own.at[a, b, e], got.at[a, b, e], ps.at[a, b, e], pr.at[a, b, e],
                    device_id={"dp": e}, device_id_type=MESH).wait_recv()
        if k < ns - 1:
            def store(at, v):
                mid[a, b, at] = v
            sum_rows(0, h, plane_terms(a, b), store)
            if not chain:
                zcopy(a, b, s).start()

    def hop(a, b, way):
        slot = jnp.where(s + way == b, jnp.where(way > 0, b, ns), b)
        return pltpu.make_async_remote_copy(
            mid.at[a, b], zgot.at[a, slot], zs.at[a, b], zr.at[a, slot],
            device_id={"shard": s + way}, device_id_type=MESH)

    def came(a, slot):
        return pltpu.make_async_remote_copy(
            mid.at[a, s], zgot.at[a, slot], zs.at[a, s], zr.at[a, slot], device_id={"mp": 1 - m},
            device_id_type=MESH)

    def four(a, k, b):
        if k == ns - 1:
            return

        def add():
            came(a, b).wait_recv()

            def store(at, v):
                mid[a, b, at] = v
            sum_rows(0, h, [lambda at: mid[a, b, at], lambda at: zgot[a, b, at]], store)

        upward = b > s
        pl.when(jnp.where(upward, s > 0, s < ns - 1))(add)
        pl.when(upward)(lambda: hop(a, b, 1).start())
        pl.when(jnp.logical_not(upward))(lambda: hop(a, b, -1).start())

    stages = [zero, one, two, three] + ([four] if chain else [])
    if not spans:
        for item in items:
            zero(*item)
        stages = stages[1:]
    for t in range(len(items) + len(stages) - 1):
        for j, stage in enumerate(stages):
            if 0 <= t - j < len(items):
                stage(*items[t - j])

    def give_out(a, core):
        return pltpu.make_async_remote_copy(
            fin.at[a], outs[a].at[core], fs.at[a], fr.at[a], device_id={"mp": 1 - m}, device_id_type=MESH)

    def keep(a):
        return pltpu.make_async_copy(fin.at[a], outs[a].at[m] if share else outs[a], ks.at[a])

    others = order[:-1]
    for a in range(count):
        def store(at, v, a=a):
            fin[a, at] = v

        if chain:
            sum_rows(0, h, plane_terms(a, s), store)
            for slot, ok in ((s, s > 0), (ns, s < ns - 1)):

                def add(slot=slot):
                    came(a, slot).wait_recv()
                    sum_rows(0, h, [lambda at: fin[a, at], lambda at: zgot[a, slot, at]], store)

                pl.when(ok)(add)
        else:
            for b in others:
                zcopy(a, b, b).wait_recv()
            sum_rows(0, h, plane_terms(a, s) + [lambda at, b=b: zgot[a, b, at] for b in others], store)
        if share:
            give_out(a, m).start()
        keep(a).start()
    for a in range(count):
        if share:
            give_out(a, 1 - m).wait_recv()
            give_out(a, m).wait_send()
        keep(a).wait()
        for k, b in enumerate(order):
            if not spans or k >= ns - 2:
                score(a, k, b).wait_send()
            for w in sends(a, b):
                w.wait_send()
        for b in others:
            zcopy(a, b, s).wait_send()


def reduce_scatter(collective, mesh_shape, share, blocks, terms=None, factors=None, weight=None):
    ns, nd = mesh_shape["shard"], mesh_shape["dp"]
    rows, c = blocks
    h = rows // 2
    count = len(factors) if factors else 1
    size = ns * nd * h * c * 2
    if size * count * 3 > (40 << 20):
        whole = [terms] if factors is None else [
            cols_product(x, weight[:, lo:hi]).astype(BF16) for x, lo, hi in factors]
        sums = []
        for p in whole:
            total = lax.psum_scatter(p.reshape(ns * nd, 2, h, c), TOK, scatter_dimension=0, tiled=True)[0]
            total = lax.psum(total, "mp")
            sums.append(total if share else lax.dynamic_index_in_dim(total, lax.axis_index("mp"), 0, False))
        return sums
    if factors is None:
        spans = None
        args = [terms.reshape(ns, nd, 2, h, c)]
        in_specs = [pl.BlockSpec(memory_space=pl.ANY)]
        give = (1, 1, 1, 16, 128)
    else:
        spans = tuple((lo, hi) for _, lo, hi in factors)
        args = [x.reshape(ns, nd, 2, h, hi - lo) for x, lo, hi in factors] + [weight]
        in_specs = [pl.BlockSpec(memory_space=pltpu.VMEM)] * (count + 1)
        give = (count, 2, nd, h, c)
    slots = 3 if nd == 4 and h % 32 == 0 else nd
    dma = pltpu.SemaphoreType.DMA
    return pl.pallas_call(
        partial(reduce_kernel, ns, nd, share, spans),
        out_shape=[jax.ShapeDtypeStruct((2, h, c) if share else (h, c), BF16)] * count,
        in_specs=in_specs,
        out_specs=[pl.BlockSpec(memory_space=pl.ANY)] * count,
        scratch_shapes=[
            pltpu.VMEM((count, ns, nd, h, c), BF16),
            pltpu.VMEM((count, ns, nd, h, c), BF16),
            pltpu.VMEM(give, BF16),
            pltpu.VMEM((count, ns, slots, h, c), BF16),
            pltpu.VMEM((count, ns, h, c), BF16),
            pltpu.VMEM((count, ns + 1, h, c), BF16),
            pltpu.VMEM((count, h, c), BF16),
            dma((count, ns)), dma((count, ns)), dma((count, ns)),
            dma((count, ns, max(nd, 4))), dma((count, ns, max(nd, 4))),
            dma((count, ns)), dma((count, ns + 1)), dma((count,)), dma((count,)), dma((count,)),
        ],
        compiler_params=pltpu.CompilerParams(
            collective_id=collective, has_side_effects=True, vmem_limit_bytes=VMEM_LIMIT),
        cost_estimate=pl.CostEstimate(flops=0, bytes_accessed=1 << 20, transcendentals=0),
    )(*args)


def gelu_both(v):
    root, cube = 0.7978845608028654, 0.044715
    t = jnp.tanh(root * (v + cube * v * v * v))
    slope = 0.5 * (1.0 + t) + 0.5 * v * (1.0 - t * t) * (root * (1.0 + 3.0 * cube * v * v))
    return 0.5 * v * (1.0 + t), slope


def feed_kernel(ns, nd, x, cot, w, act, low, grad, hid, cots, acc, zs, zr, ps, pr, cs, cr, ls, ks):
    s, d, m = (lax.axis_index(a) for a in ("shard", "dp", "mp"))
    h, width = x.shape
    units = w.shape[1] // 3
    relay = nd == 4 and h % 32 == 0
    greet(ns, nd, True, True, True, z_all=True)
    turns = [0] + sorted(range(1, ns), key=lambda k: min(k, ns - k))
    order = [lax.rem(s + k, ns) for k in turns]
    peers = [lax.rem(d + k, nd) for k in range(1, nd)]
    if relay:
        xn, yn, across = square(d)
        peers = [xn, yn, across]

    def zsend(b):
        return pltpu.make_async_remote_copy(
            x, hid.at[s, d, m], zs.at[b], zr.at[s], device_id={"shard": b}, device_id_type=MESH)

    def zrecv(b):
        return pltpu.make_async_remote_copy(
            x, hid.at[b, d, m], zs.at[b], zr.at[b], device_id={"shard": b}, device_id_type=MESH)

    def part(ref, k):
        return ref if k is None else ref.at[pl.ds(k * (h // 2), h // 2)]

    def source(b, e, first):
        return x if first else hid.at[b, e, m]

    def psend(b, e, to, slot, k, first):
        return pltpu.make_async_remote_copy(
            part(source(b, e, first), k), part(hid.at[b, e, m], k), ps.at[b, slot], pr.at[b, e, k or 0],
            device_id={"dp": to}, device_id_type=MESH)

    def precv(b, e, k):
        ref = part(hid.at[b, e, m], k)
        return pltpu.make_async_remote_copy(
            ref, ref, ps.at[b, 0], pr.at[b, e, k or 0], device_id={"dp": peers[0]}, device_id_type=MESH)

    def own_sends(b, first):
        if relay:
            return [psend(b, d, xn, 0, 0, first), psend(b, d, yn, 1, 1, first),
                    psend(b, d, xn, 2, 1, first), psend(b, d, yn, 3, 0, first)]
        return [psend(b, d, e, j, None, first) for j, e in enumerate(peers)]

    def pass_sends(b):
        if relay:
            return [(precv(b, xn, 0), psend(b, xn, yn, 4, 0, False)),
                    (precv(b, yn, 1), psend(b, yn, xn, 5, 1, False))]
        return []

    def share(b, e, core, first=False):
        ref = hid.at[b, e, core]
        return pltpu.make_async_remote_copy(
            x if first else ref, ref, cs.at[b, e], cr.at[b, e], device_id={"mp": 1 - m}, device_id_type=MESH)

    def load(b):
        return pltpu.make_async_copy(cot.at[b], cots.at[b], ls.at[b])

    def begin(k):
        b = order[k]
        if k > 0:
            zrecv(b).wait_recv()
        for c in own_sends(b, k == 0):
            c.start()
        share(b, d, m, k == 0).start()

    def hand_on(k):
        for got, on in pass_sends(order[k]):
            got.wait_recv()
            on.start()

    def settle(k):
        b = order[k]
        for e in peers:
            for q in waits(e):
                precv(b, e, q).wait_recv()
            share(b, e, m).start()

    def waits(e):
        if not relay:
            return [None]
        return [1] if e is xn else [0] if e is yn else [0, 1]

    def ready(k):
        b = order[k]
        for e in [d] + peers:
            share(b, e, 1 - m).wait_recv()
        if k == 0:
            keep.wait()
        load(b).wait()

    count = nd // 2 if nd % 2 == 0 else nd

    def forward(k, q):
        b = order[k]
        at = pl.ds(q * count, count)
        rows = count * 2 * h
        pre = product(hid[b, at].reshape(rows, width), w[:, : 2 * units])
        back = product(cots[b, at].reshape(rows, width), w[:, 2 * units :])
        value, slope = gelu_both(pre[:, :units])
        up = pre[:, units:]
        act[b, at] = (value * up).astype(BF16).reshape(count, 2, h, units)
        low[b, at, :, :, :units] = (back * up * slope).astype(BF16).reshape(count, 2, h, units)
        low[b, at, :, :, units:] = (back * value).astype(BF16).reshape(count, 2, h, units)

    def backward(k):
        b = order[k]
        rows = nd * 2 * h
        step = 512 if width % 512 == 0 else 128
        lows = low[b].reshape(rows, 2 * units)
        acts = act[b].reshape(rows, units)

        @pl.loop(0, width // step)
        def _(j):
            at = pl.ds(pl.multiple_of(j * step, step), step)
            one = rows_product(hid[b, :, :, :, at].reshape(rows, step), lows)
            two = rows_product(cots[b, :, :, :, at].reshape(rows, step), acts)
            if k > 0:
                one = one + acc[at, : 2 * units]
                two = two + acc[at, 2 * units :]
            if k < ns - 1:
                acc[at, : 2 * units] = one
                acc[at, 2 * units :] = two
            else:
                grad[at, : 2 * units] = one.astype(BF16)
                grad[at, 2 * units :] = two.astype(BF16)

    for b in order[1:]:
        zsend(b).start()
    keep = pltpu.make_async_copy(x, hid.at[s, d, m], ks)
    keep.start()
    begin(0)
    for b in order:
        load(b).start()
    hand_on(0)
    if ns > 1:
        begin(1)
        hand_on(1)
    for k in range(ns):
        settle(k)
        ready(k)
        forward(k, 0)
        if count < nd:
            forward(k, 1)
        if k + 2 < ns:
            begin(k + 2)
        backward(k)
        if k + 2 < ns:
            hand_on(k + 2)
    for k, b in enumerate(order):
        for c in own_sends(b, k == 0):
            c.wait_send()
        for _, c in pass_sends(b):
            c.wait_send()
        for e in [d] + peers:
            share(b, e, m).wait_send()
        if k > 0:
            zsend(b).wait_send()


def feed(collective, mesh_shape, x, cot, w):
    ns, nd = mesh_shape["shard"], mesh_shape["dp"]
    h, width = x.shape
    units = w.shape[1] // 3
    rows = (ns, nd, 2, h)
    if 2 * cot.size * 2 > (24 << 20):
        (hid,) = gather(collective, mesh_shape, [(x, "all")])
        hid, cot = hid.reshape(-1, width), cot.reshape(-1, width)
        pre = product(hid, w[:, : 2 * units])
        back = product(cot, w[:, 2 * units :])
        value, slope = gelu_both(pre[:, :units])
        up = pre[:, units:]
        act = (value * up).astype(BF16)
        low = jnp.concatenate([back * up * slope, back * value], axis=1).astype(BF16)
        grad = jnp.concatenate([rows_product(hid, low), rows_product(cot, act)], axis=1).astype(BF16)
        return act, low, grad
    dma = pltpu.SemaphoreType.DMA
    vmem = pl.BlockSpec(memory_space=pltpu.VMEM)
    act, low, grad = pl.pallas_call(
        partial(feed_kernel, ns, nd),
        out_shape=[
            jax.ShapeDtypeStruct(rows + (units,), BF16),
            jax.ShapeDtypeStruct(rows + (2 * units,), BF16),
            jax.ShapeDtypeStruct((width, 3 * units), BF16),
        ],
        in_specs=[vmem, pl.BlockSpec(memory_space=pl.ANY), vmem],
        out_specs=[vmem] * 3,
        scratch_shapes=[
            pltpu.VMEM(rows + (width,), BF16),
            pltpu.VMEM(rows + (width,), BF16),
            pltpu.VMEM((width, 3 * units), F32),
            dma((ns,)), dma((ns,)), dma((ns, max(nd, 6))), dma((ns, nd, 2)), dma((ns, nd)), dma((ns, nd)),
            dma((ns,)), dma(()),
        ],
        compiler_params=pltpu.CompilerParams(
            collective_id=collective, has_side_effects=True, vmem_limit_bytes=VMEM_LIMIT),
        cost_estimate=pl.CostEstimate(flops=0, bytes_accessed=1 << 20, transcendentals=0),
    )(x, cot, w)
    return act.reshape(-1, units), low.reshape(-1, 2 * units), grad


def plane_kernel(ns, nd, p, out, own, sib, ls, ss, sr, ps, pr, fs, fr, ks):
    d, m = lax.axis_index("dp"), lax.axis_index("mp")
    h, c = own.shape[1:]
    tile = 16
    greet(ns, nd, False, True, True)
    peers = [lax.rem(d + k, nd) for k in range(1, nd)]
    order = ([square(d)[2], square(d)[0], square(d)[1]] if nd == 4 else peers) + [d]
    other = {"mp": 1 - m}

    def score(e):
        return pltpu.make_async_remote_copy(
            p.at[e, 1 - m], sib.at[e], ss.at[e], sr.at[e], device_id=other, device_id_type=MESH)

    def load(e):
        return pltpu.make_async_copy(p.at[e, m], own.at[e], ls.at[e])

    def send(e, block):
        return pltpu.make_async_remote_copy(
            own.at[e], out.at[block, m], ps.at[e], pr.at[block], device_id={"dp": e}, device_id_type=MESH)

    def share(e, core):
        src = own.at[d] if e is d else out.at[e, m]
        return pltpu.make_async_remote_copy(
            src, out.at[e, core], fs.at[e], fr.at[e], device_id=other, device_id_type=MESH)

    for e in order:
        score(e).start()
        load(e).start()
    for e in order:
        score(e).wait_recv()
        load(e).wait()

        @pl.loop(0, h // tile)
        def _(r, e=e):
            at = pl.ds(pl.multiple_of(r * tile, tile), tile)
            own[e, at] = (own[e, at].astype(F32) + sib[e, at].astype(F32)).astype(BF16)

        if e is not d:
            send(e, d).start()
    keep = pltpu.make_async_copy(own.at[d], out.at[d, m], ks)
    keep.start()
    share(d, m).start()
    for e in order[:-1]:
        send(e, e).wait_recv()
        share(e, m).start()
    keep.wait()
    for e in order:
        share(e, 1 - m).wait_recv()
        share(e, m).wait_send()
        score(e).wait_send()
        if e is not d:
            send(e, d).wait_send()


def plane_reduce(collective, mesh_shape, p):
    ns, nd = mesh_shape["shard"], mesh_shape["dp"]
    h, c = p.shape[2:]
    dma = pltpu.SemaphoreType.DMA
    return pl.pallas_call(
        partial(plane_kernel, ns, nd),
        out_shape=jax.ShapeDtypeStruct(p.shape, BF16),
        in_specs=[pl.BlockSpec(memory_space=pl.ANY)],
        out_specs=pl.BlockSpec(memory_space=pl.ANY),
        scratch_shapes=[pltpu.VMEM((nd, h, c), BF16)] * 2 + [dma((nd,))] * 7 + [dma(())],
        compiler_params=pltpu.CompilerParams(
            collective_id=collective, has_side_effects=True, vmem_limit_bytes=VMEM_LIMIT),
        cost_estimate=pl.CostEstimate(flops=0, bytes_accessed=1 << 20, transcendentals=0),
    )(p)


def rope_tables(positions):
    half_dim = HEAD_DIM // 2
    exponent = jnp.arange(half_dim, dtype=F32) * (-2.0 / HEAD_DIM)
    angles = positions.astype(F32)[:, None] * jnp.power(ROPE_BASE, exponent)[None, :]
    return (jnp.cos(angles), jnp.sin(angles))


def rotate(values, cosine, sine_rows):
    half_dim = values.shape[-1] // 2
    front_half = values[..., :half_dim]
    back_half = values[..., half_dim:]
    return jnp.concatenate(
        [front_half * cosine - back_half * sine_rows, back_half * cosine + front_half * sine_rows], axis=-1)


def rows_product(left_side, right_side):
    return lax.dot_general(
        left_side, right_side, (((0,), (0,)), ((), ())), preferred_element_type=F32)


def cols_product(left_side, right_side):
    return lax.dot_general(
        left_side, right_side, (((1,), (1,)), ((), ())), preferred_element_type=F32)


def product(left_side, right_side):
    return jnp.dot(left_side, right_side, preferred_element_type=F32)


def turn(v, cosine, sine):
    half_dim = HEAD_DIM // 2
    front, back = v[:, :half_dim], v[:, half_dim:]
    return front * cosine - back * sine, back * cosine + front * sine


def window(nd, kv, keys, values):
    me = lax.axis_index("shard") * nd + lax.axis_index("dp")
    tok = kv.shape[2]
    for j in range(KV_BLOCKS + 1):
        b = jnp.maximum(me + (j - KV_BLOCKS), 0)
        keys[j * tok : (j + 1) * tok] = kv[b, 0]
        values[j * tok : (j + 1) * tok] = kv[b, 1]


def attend_kernel(nd, got, kv, allowed, cosine, sine, mixed, queries, probs, keys, values):
    window(nd, kv, keys, values)
    scale = HEAD_DIM ** (-0.5)
    half_dim = HEAD_DIM // 2
    cos, sin = cosine[...], sine[...]
    for h in range(probs.shape[0]):
        at = h * HEAD_DIM
        raw = got[0, :, at : at + HEAD_DIM].astype(F32)
        for e in range(1, got.shape[0]):
            raw = raw + got[e, :, at : at + HEAD_DIM].astype(F32)
        front, back = turn(raw, cos, sin)
        queries[:, at : at + half_dim] = front.astype(BF16)
        queries[:, at + half_dim : at + HEAD_DIM] = back.astype(BF16)
        scores = cols_product(queries[:, at : at + HEAD_DIM], keys[...]) * scale
        scores = jnp.where(allowed[...] > 0.0, scores, -jnp.inf)
        raised = jnp.exp(scores - jnp.max(scores, axis=1, keepdims=True))
        prob = raised / jnp.sum(raised, axis=1, keepdims=True)
        probs[h] = prob
        mixed[:, at : at + HEAD_DIM] = product(prob.astype(BF16), values[...]).astype(BF16)


def attend(nd, heads, got, kv, allowed, cosine, sine):
    tok = got.shape[1]
    span = allowed.shape[1]
    return pl.pallas_call(
        partial(attend_kernel, nd),
        out_shape=[
            jax.ShapeDtypeStruct((tok, heads * HEAD_DIM), BF16),
            jax.ShapeDtypeStruct((tok, heads * HEAD_DIM), BF16),
            jax.ShapeDtypeStruct((heads, tok, span), F32),
        ],
        in_specs=[pl.BlockSpec(memory_space=pltpu.VMEM)] * 5,
        out_specs=[pl.BlockSpec(memory_space=pltpu.VMEM)] * 3,
        scratch_shapes=[pltpu.VMEM((span, HEAD_DIM), BF16)] * 2,
        compiler_params=pltpu.CompilerParams(vmem_limit_bytes=VMEM_LIMIT),
    )(got, kv, allowed, cosine, sine)


def attend_back_kernel(nd, got, kv, queries, probs, cosine, sine, kv_grad, low, keys, values, key_sum, value_sum):
    window(nd, kv, keys, values)
    me = lax.axis_index("shard") * nd + lax.axis_index("dp")
    scale = HEAD_DIM ** (-0.5)
    half_dim = HEAD_DIM // 2
    n, _, tok, _ = kv.shape
    cos, sin = cosine[...], sine[...]
    for h in range(probs.shape[0]):
        at = h * HEAD_DIM
        raw = got[0, :, at : at + HEAD_DIM].astype(F32)
        for e in range(1, got.shape[0]):
            raw = raw + got[e, :, at : at + HEAD_DIM].astype(F32)
        mixed_grad = raw.astype(BF16)
        prob = probs[h]
        prob_grad = cols_product(mixed_grad, values[...])
        inner = jnp.sum(prob * prob_grad, axis=1, keepdims=True)
        scores_low = (prob * (prob_grad - inner) * scale).astype(BF16)
        front, back = turn(product(scores_low, keys[...]), cos, -sin)
        low[:, at : at + half_dim] = front.astype(BF16)
        low[:, at + half_dim : at + HEAD_DIM] = back.astype(BF16)
        key_part = rows_product(scores_low, queries[:, at : at + HEAD_DIM])
        value_part = rows_product(prob.astype(BF16), mixed_grad)
        if h == 0:
            key_sum[...] = key_part
            value_sum[...] = value_part
        else:
            key_sum[...] += key_part
            value_sum[...] += value_part

    @pl.loop(0, n)
    def _(b):
        kv_grad[b] = jnp.zeros(kv_grad.shape[1:], BF16)

    for j in range(KV_BLOCKS + 1):
        b = me + (j - KV_BLOCKS)

        @pl.when(b >= 0)
        def _(j=j, b=b):
            kv_grad[b, 0] = key_sum[j * tok : (j + 1) * tok].astype(BF16)
            kv_grad[b, 1] = value_sum[j * tok : (j + 1) * tok].astype(BF16)


def attend_back(nd, got, kv, queries, probs, cosine, sine):
    span = probs.shape[2]
    return pl.pallas_call(
        partial(attend_back_kernel, nd),
        out_shape=[jax.ShapeDtypeStruct(kv.shape, BF16), jax.ShapeDtypeStruct(queries.shape, BF16)],
        in_specs=[pl.BlockSpec(memory_space=pltpu.VMEM)] * 6,
        out_specs=[pl.BlockSpec(memory_space=pltpu.VMEM)] * 2,
        scratch_shapes=[pltpu.VMEM((span, HEAD_DIM), BF16)] * 2 + [pltpu.VMEM((span, HEAD_DIM), F32)] * 2,
        compiler_params=pltpu.CompilerParams(vmem_limit_bytes=VMEM_LIMIT),
    )(got, kv, queries, probs, cosine, sine)


ROWS = 16


def row_tiles(count, body):
    @pl.loop(0, count // ROWS)
    def _(r):
        body(pl.ds(pl.multiple_of(r * ROWS, ROWS), ROWS))


def pieces(nd, width, plane_d, own_d):
    for j in range(width // own_d):
        yield j * own_d, j % nd, (j // nd) * own_d


def inverse_of(rows):
    return lax.rsqrt(jnp.mean(rows * rows, axis=1, keepdims=True) + EPS_NORM)


def norm_back(rows, gain, grad):
    inverse = inverse_of(rows)
    normed = rows * inverse
    scaled = grad * gain
    inner = jnp.mean(normed * scaled, axis=1, keepdims=True)
    return inverse * (scaled - normed * inner), grad * normed


def join_kernel(own_d, got, tokens, gain, residual, hidden):
    nd, tok, plane_d = got.shape
    half = hidden.shape[0]
    first = lax.axis_index("mp") * half

    def add(at):
        for c, e, p in pieces(nd, tokens.shape[1], plane_d, own_d):
            residual[at, c : c + own_d] = (
                got[e, at, p : p + own_d].astype(F32) + tokens[at, c : c + own_d].astype(F32))

    row_tiles(tok, add)

    @pl.loop(0, half // ROWS)
    def _(r):
        rows = residual[pl.ds(pl.multiple_of(first + r * ROWS, ROWS), ROWS)]
        at = pl.ds(pl.multiple_of(r * ROWS, ROWS), ROWS)
        hidden[at] = (rows * inverse_of(rows) * gain[...]).astype(BF16)


def split_kernel(own_d, grad, ffn, residual, gain, cot, block_out, residual_grad, cut, gain_cut, total):
    nd, tok, plane_d = cut.shape
    total[...] = jnp.zeros_like(total)

    def body(at):
        rows = residual[at]
        block_out[at] = (rows + ffn[at].astype(F32)).astype(BF16)
        back, terms = norm_back(rows, gain[...], grad[at].astype(F32))
        total[...] += terms
        value = cot[at].astype(F32) + back
        residual_grad[at] = value
        for c, e, p in pieces(nd, grad.shape[1], plane_d, own_d):
            cut[e, at, p : p + own_d] = value[:, c : c + own_d].astype(BF16)

    row_tiles(tok, body)
    gain_cut[...] = jnp.zeros_like(gain_cut)
    sums = jnp.sum(total[...], axis=0, keepdims=True)
    for c, e, p in pieces(nd, grad.shape[1], plane_d, own_d):
        gain_cut[e, 0:1, p : p + own_d] = sums[:, c : c + own_d]


def last_kernel(own_d, got, tokens, gain, residual_grad, out, grad):
    nd, tok, plane_d = got.shape

    def body(at):
        for c, e, p in pieces(nd, tokens.shape[1], plane_d, own_d):
            grad[:, c : c + own_d] = got[e, at, p : p + own_d].astype(F32)
        back, _ = norm_back(tokens[at].astype(F32), gain[...], grad[...])
        out[at] = residual_grad[at] + back

    row_tiles(tok, body)


def local(kernel, outs, args, scratch=()):
    return pl.pallas_call(
        kernel,
        out_shape=[jax.ShapeDtypeStruct(shape, dtype) for shape, dtype in outs],
        in_specs=[pl.BlockSpec(memory_space=pltpu.VMEM)] * len(args),
        out_specs=[pl.BlockSpec(memory_space=pltpu.VMEM)] * len(outs),
        scratch_shapes=[pltpu.VMEM(shape, dtype) for shape, dtype in scratch],
        compiler_params=pltpu.CompilerParams(vmem_limit_bytes=VMEM_LIMIT),
    )(*args)


def pack(part, parts, ins, outs):
    gateup, down = ins
    (out,) = outs
    n, _, columns = out.shape
    units = columns // 3
    full = down.shape[1] // units
    share = -(-n // parts)
    for j in range(part * share, min((part + 1) * share, n)):
        if j >= full:
            out[j] = jnp.zeros(out.shape[1:], BF16)
            continue
        at = pl.ds(j * units, units)
        out[j, :, :units] = gateup[:, 0, at]
        out[j, :, units : 2 * units] = gateup[:, 1, at]
        out[j, :, 2 * units :] = down[:, at]


def adam_step(rates, grad, weight, first, second, decay):
    first_new = BETA_ONE * first + (1.0 - BETA_ONE) * grad
    second_new = BETA_TWO * second + (1.0 - BETA_TWO) * grad * grad
    direction = first_new * rates[0] / (jnp.sqrt(second_new * rates[1]) + ADAM_EPS)
    return first_new, second_new, -LEARN_RATE * (direction + decay * weight.astype(F32))


def unpack_kernel(rates, got, gw, gf, gs, dw, df, ds, gg, gfn, gsn, gu, dg, dfn, dsn, du):
    units = dw.shape[1]
    pair = (rates[0], rates[1])
    for k in range(2):
        grad = got[0, :, k * units : (k + 1) * units].astype(F32)
        gg[:, k, :] = grad
        gfn[:, k, :], gsn[:, k, :], gu[:, k, :] = adam_step(
            pair, grad, gw[:, k, :], gf[:, k, :], gs[:, k, :], DECAY_RATE)
    grad = got[0, :, 2 * units :].astype(F32)
    dg[...] = grad
    dfn[...], dsn[...], du[...] = adam_step(pair, grad, dw[...], df[...], ds[...], DECAY_RATE)


def unpack_adam(units, rates, got, gateup, down):
    own_d, _, ff_local = gateup[0].shape
    three = pl.BlockSpec((own_d, 2, units), lambda j: (0, 0, j))
    two = pl.BlockSpec((own_d, units), lambda j: (0, j))
    shape3 = jax.ShapeDtypeStruct(gateup[0].shape, F32)
    shape2 = jax.ShapeDtypeStruct(down[0].shape, F32)
    out = pl.pallas_call(
        unpack_kernel,
        out_shape=[shape3] * 4 + [shape2] * 4,
        grid=(ff_local // units,),
        in_specs=[
            pl.BlockSpec(memory_space=pltpu.SMEM),
            pl.BlockSpec((1, own_d, 3 * units), lambda j: (j, 0, 0)),
        ] + [three] * 3 + [two] * 3,
        out_specs=[three] * 4 + [two] * 4,
        compiler_params=pltpu.CompilerParams(vmem_limit_bytes=VMEM_LIMIT),
    )(rates, got, *gateup, *down)
    return out[:4], out[4:]


def shards(
    mesh_shape,
    tokens_in,
    segment_ids,
    block_cotangent,
    query_weight,
    keyval_weight,
    outproj_weight,
    gateup_weight,
    down_weight,
    norm_gains,
    query_first,
    keyval_first,
    outproj_first,
    gateup_first,
    down_first,
    gains_first,
    query_second,
    keyval_second,
    outproj_second,
    gateup_second,
    down_second,
    gains_second,
    step_count,
):
    ns, nd = mesh_shape["shard"], mesh_shape["dp"]
    n = ns * nd
    s, d, m = (lax.axis_index(a) for a in ("shard", "dp", "mp"))
    me = s * nd + d
    tok, width = tokens_in.shape
    own_d = query_weight.shape[0]
    q_cols = query_weight.shape[1]
    heads_local = q_cols // HEAD_DIM
    ff_local = gateup_weight.shape[2]
    units = -(-(-(-ff_local // n)) // 128) * 128
    ff_pad = units * n - ff_local
    half = tok // 2
    plane_tok = nd * tok
    plane_d = ns * own_d

    input_rows = tokens_in.astype(F32)
    inverse_one = lax.rsqrt(jnp.mean(input_rows * input_rows, axis=1) + EPS_NORM)
    lanes = max(256, -(-max(own_d, tok) // 128) * 128)

    def line(v):
        return jnp.pad(v, ((0, 0), (0, lanes - v.shape[1])))

    small = jnp.concatenate(
        [line(norm_gains.astype(F32)), line(segment_ids.astype(F32)[None]), line(inverse_one[None]),
         jnp.zeros((4, lanes), F32)], axis=0)
    qkv_weight = jnp.concatenate(
        [query_weight, lax.dynamic_slice_in_dim(keyval_weight, m * HEAD_DIM, HEAD_DIM, 1)], axis=1)

    def plane_cut(value):
        return value.reshape(tok, ns, nd, own_d).transpose(2, 0, 1, 3).reshape(nd, tok, plane_d)

    small_all, tokens_plane, cot_all, qkv_plane, three = gather(
        0, mesh_shape,
        [(small, "all"), (plane_cut(tokens_in), "swap"),
         (lax.dynamic_slice_in_dim(block_cotangent, m * half, half, 0), "all"), (qkv_weight, "z")],
        pack, (gateup_weight, down_weight.T), jax.ShapeDtypeStruct((n, own_d, 3 * units), BF16))
    tokens_plane = tokens_plane.reshape(plane_tok, plane_d)
    three, tokens_plane = lax.optimization_barrier((three, tokens_plane))
    three = lax.all_to_all(three, TOK, 0, 0, tiled=True).reshape(width, 3 * units)
    qkv_plane = qkv_plane.reshape(plane_d, q_cols + HEAD_DIM)
    small_all = small_all[:, :, 0]
    gains_by = small_all[:, :, :2, :own_d]
    full_gains = gains_by.transpose(2, 0, 1, 3).reshape(2, width)
    tags = small_all[:, :, 2, :tok].reshape(n * tok)
    plane_scale = lax.dynamic_index_in_dim(small_all[:, :, 3, :tok], s, 0, False).reshape(plane_tok, 1)
    plane_gain = lax.dynamic_index_in_dim(gains_by[:, :, 0], d, 1, False).reshape(1, plane_d)


    def from_plane(collective, value):
        got = plane_reduce(collective, mesh_shape, value.reshape(nd, 2, half, plane_d))
        return got.reshape(nd, tok, plane_d)

    def plane_terms(collective, value):
        return gather(collective, mesh_shape, [(value.reshape(nd, tok, -1), "swap")])[0]

    hidden_plane = (tokens_plane.astype(F32) * plane_scale * plane_gain).astype(BF16)
    qkv_terms = plane_terms(8, product(hidden_plane, qkv_plane).astype(BF16))

    pad = KV_BLOCKS * tok
    key_span = pad + tok
    start = me * tok
    tag_pad = jnp.concatenate([jnp.full((pad,), -1.0, F32), tags])
    key_tags = lax.dynamic_slice_in_dim(tag_pad, start, key_span, 0)
    own_tags = segment_ids.astype(F32)
    query_index = jnp.arange(tok, dtype=jnp.int32) + pad
    key_index = jnp.arange(key_span, dtype=jnp.int32)
    same_segment = key_tags[None, :] == own_tags[:, None]
    allowed = same_segment & (key_index[None, :] <= query_index[:, None])
    positions = jnp.sum(
        (same_segment & (key_index[None, :] < query_index[:, None])).astype(jnp.int32), axis=1)
    cosine, sine_rows = rope_tables(positions)
    kv_raw = jnp.sum(qkv_terms[:, :, q_cols:].astype(F32), axis=0)
    kv_mine = jnp.where(m == 0, rotate(kv_raw, cosine, sine_rows), kv_raw).astype(BF16)
    (kv_all,) = gather(1, mesh_shape, [(kv_mine, "all")])
    kv_all = kv_all.reshape(n, 2, tok, HEAD_DIM)
    mixed_low, queries, probs = attend(
        nd, heads_local, qkv_terms, kv_all, allowed.astype(F32), cosine, sine_rows)
    mixed_plane, outproj_z = gather(
        2, mesh_shape, [(mixed_low, "plane"), (outproj_weight.T, "z")])
    mixed_plane = mixed_plane.reshape(plane_tok, q_cols)
    outproj_plane = outproj_z.reshape(plane_d, q_cols)
    residual, hidden_two = local(
        partial(join_kernel, own_d), [((tok, width), F32), ((half, width), BF16)],
        [from_plane(9, cols_product(mixed_plane, outproj_plane).astype(BF16)), tokens_in, full_gains[1:]])

    act_low, gateup_low, three_grad = feed(
        3, mesh_shape, hidden_two, cot_all, three)
    three_grad, act_low, gateup_low = lax.optimization_barrier((three_grad, act_low, gateup_low))
    three_grad = lax.all_to_all(three_grad.reshape(n, own_d, 3 * units), TOK, 0, 0, tiled=True)
    hidden_two_grad, ffn_sum = reduce_scatter(
        4, mesh_shape, True, (tok, width),
        factors=[(gateup_low, 0, 2 * units), (act_low, 2 * units, 3 * units)], weight=three)
    block_out, residual_grad, attn_cut, gain_cut = local(
        partial(split_kernel, own_d),
        [((tok, width), BF16), ((tok, width), F32), ((nd, tok, plane_d), BF16), ((nd, 8, plane_d), F32)],
        [hidden_two_grad.reshape(tok, width), ffn_sum.reshape(tok, width), residual, full_gains[1:],
         block_cotangent],
        [((ROWS, width), F32)])
    attn_low, gain_two_part = gather(10, mesh_shape, [(attn_cut, "swap"), (gain_cut, "swap")])
    attn_low = attn_low.reshape(plane_tok, plane_d)
    gain_two_part = jnp.where(m == 0, jnp.sum(gain_two_part[:, 0], axis=0), 0.0)
    mixed_terms = plane_terms(11, product(attn_low, outproj_plane).astype(BF16))

    def z_sum(value):
        got = lax.all_to_all(value, "shard", 0, 0, tiled=True)
        return jnp.sum(got.astype(F32), axis=0)

    outproj_grad = rows_product(attn_low, mixed_plane).astype(BF16)
    outproj_grad, three_grad = lax.optimization_barrier((outproj_grad, three_grad))
    own_outproj = z_sum(outproj_grad.reshape(ns, own_d, q_cols))

    kv_terms, query_low = attend_back(nd, mixed_terms, kv_all, queries, probs, cosine, sine_rows)
    (kv_grad,) = reduce_scatter(6, mesh_shape, False, (2 * tok, HEAD_DIM), terms=kv_terms)
    kv_grad = kv_grad.astype(F32)
    kv_low = jnp.where(m == 0, rotate(kv_grad, cosine, -sine_rows), kv_grad)
    qkv_low = jnp.concatenate([query_low, kv_low.astype(BF16)], axis=1)
    (qkv_low_plane,) = gather(7, mesh_shape, [(qkv_low, "plane")])
    qkv_low_plane = qkv_low_plane.reshape(plane_tok, q_cols + HEAD_DIM)
    hidden_one_part = cols_product(qkv_low_plane, qkv_plane).astype(BF16)
    gain_one_part = jnp.sum(hidden_one_part.astype(F32) * (tokens_plane.astype(F32) * plane_scale), axis=0)
    hidden_one_grad = from_plane(12, hidden_one_part)
    (input_grad,) = local(
        partial(last_kernel, own_d), [((tok, width), F32)],
        [hidden_one_grad, tokens_in, full_gains[:1], residual_grad], [((ROWS, width), F32)])
    gain_parts = jnp.stack([gain_one_part, gain_two_part], axis=1)
    qkv_grad = jnp.concatenate(
        [rows_product(hidden_plane, qkv_low_plane), jnp.pad(gain_parts, ((0, 0), (0, 126)))], axis=1).astype(BF16)
    qkv_grad, own_outproj = lax.optimization_barrier((qkv_grad, own_outproj))
    own_qkv = z_sum(qkv_grad.reshape(ns, own_d, -1))
    own_query = own_qkv[:, :q_cols]
    rest = own_qkv[:, q_cols:]
    rest_other = lax.ppermute(rest, "mp", [(0, 1), (1, 0)])
    kv_own, kv_other = rest[:, :HEAD_DIM], rest_other[:, :HEAD_DIM]
    own_keyval = jnp.where(
        m == 0, jnp.concatenate([kv_own, kv_other], axis=1), jnp.concatenate([kv_other, kv_own], axis=1))
    own_gains = (rest + rest_other)[:, HEAD_DIM : HEAD_DIM + 2].T

    step_value = step_count[0].astype(F32)
    bias_first = 1.0 - jnp.power(BETA_ONE, step_value)
    bias_second = 1.0 - jnp.power(BETA_TWO, step_value)
    rates = jnp.stack([1.0 / bias_first, 1.0 / bias_second])
    gateup_news, down_news = unpack_adam(
        units, rates, three_grad, (gateup_weight, gateup_first, gateup_second),
        (down_weight.T, down_first.T, down_second.T))
    down_news = [x.T for x in down_news]

    def adam(grad, weight, first, second, decay):
        return (grad,) + adam_step(rates, grad, weight, first, second, decay)

    news = [
        adam(own_query, query_weight, query_first, query_second, DECAY_RATE),
        adam(own_keyval, keyval_weight, keyval_first, keyval_second, DECAY_RATE),
        tuple(v.T for v in adam(own_outproj, outproj_weight.T, outproj_first.T, outproj_second.T, DECAY_RATE)),
        gateup_news,
        down_news,
        adam(own_gains, norm_gains, gains_first, gains_second, 0.0),
    ]
    return (block_out, input_grad) + tuple(x[k] for k in range(4) for x in news)


def solution(mesh):
    rows, split_q, split_o = P(TOK, None), P(TOK, "mp"), P("mp", TOK)
    params = (split_q, rows, split_o, P(TOK, None, "mp"), split_o, P(None, TOK))
    in_specs = (rows, P(TOK), rows) + params * 3 + (P(),)
    out_specs = (rows, rows) + params * 4
    return jax.shard_map(
        partial(shards, dict(mesh.shape)), mesh=mesh, in_specs=in_specs, out_specs=out_specs, check_vma=False)
```

```python
from functools import partial

import jax
import jax.numpy as jnp
from jax import lax
from jax.experimental import pallas as pl
from jax.experimental.pallas import tpu as pltpu
from jax.sharding import PartitionSpec as P

HEAD_DIM = 256
KV_BLOCKS = 8

EPS_NORM = 1e-06
BETA_ONE = 0.9
BETA_TWO = 0.95
ADAM_EPS = 1e-08
LEARN_RATE = 0.01
DECAY_RATE = 0.1
ROPE_BASE = 10000.0

MESH = pl.DeviceIdType.MESH
TOK = ("shard", "dp")
VMEM_LIMIT = 56 << 20
F32 = jnp.float32
BF16 = jnp.bfloat16


def when(cond, fn):
    if cond is True:
        fn()
    else:
        pl.when(cond)(fn)


def planes(s, ns, far_first=False):
    steps = [(s, 0, 0, True)]
    for t in range(1, ns):
        steps.append((s - t, t, 1, s - t >= 0))
        steps.append((s + t, t, -1, s + t < ns))
    return steps[::-1] if far_first else steps


def greet(ns, nd, use_z, use_plane, use_core, z_all=False):
    s, d, m = (lax.axis_index(a) for a in ("shard", "dp", "mp"))
    bar = pltpu.get_barrier_semaphore()

    def hello(dev):
        pl.semaphore_signal(bar, 1, device_id=dev, device_id_type=MESH)

    count = 0
    if use_z and z_all:
        for k in range(1, ns):
            hello({"shard": lax.rem(s + k, ns)})
        count += ns - 1
    elif use_z:
        when(s < ns - 1, lambda: hello({"shard": s + 1}))
        when(s > 0, lambda: hello({"shard": s - 1}))
        count = (s < ns - 1).astype(jnp.int32) + (s > 0).astype(jnp.int32)
    if use_plane:
        for k in range(1, nd):
            hello({"dp": lax.rem(d + k, nd)})
        count += nd - 1
    if use_core:
        hello({"mp": 1 - m})
        count += 1
    pl.semaphore_wait(bar, count)


def square(d):
    low = lax.rem(d, 2)
    x = d + 1 - 2 * low
    y = lax.rem(d + 2, 4)
    return x, y, lax.rem(x + 2, 4)


def gather_kernel(ns, nd, modes, work, n_work, *refs):
    n = len(modes)
    ins, more_in = refs[:n], refs[n : n + n_work]
    outs, more_out = refs[n + n_work : 2 * n + n_work], refs[2 * n + n_work : -7 * n]
    sems = refs[-7 * n :]
    s, d, m = (lax.axis_index(a) for a in ("shard", "dp", "mp"))
    use_z = any(k in ("z", "all") for k in modes)
    use_plane = any(k in ("plane", "all", "swap") for k in modes)
    direct = [modes[i] == "all" and ins[i].size * ins[i].dtype.itemsize < 128 << 10 for i in range(n)]
    late = [modes[i] == "z" and any(k == "all" and not q for k, q in zip(modes, direct)) for i in range(n)]
    greet(ns, nd, use_z, use_plane, "all" in modes, z_all=any(direct))
    peers = [lax.rem(d + k, nd) for k in range(1, nd)]
    relay = [
        nd == 4 and modes[i] in ("all", "plane") and ins[i].shape[0] % 32 == 0 and not direct[i] for i in range(n)]
    if nd == 4:
        x, y, across = square(d)

    def place(i, b, e, core):
        if modes[i] == "z":
            return outs[i].at[b]
        if modes[i] in ("plane", "swap"):
            return outs[i].at[e]
        return outs[i].at[b, e, core]

    def half_of(i, ref, k):
        if k is None:
            return ref
        rows = ins[i].shape[0] // 2
        return ref.at[pl.ds(k * rows, rows)]

    def zcopy(i, b, way, first):
        src = ins[i] if first else place(i, b, d, m)
        return pltpu.make_async_remote_copy(
            src, place(i, b, d, m), sems[7 * i].at[(way + 1) // 2, b], sems[7 * i + 1].at[b],
            device_id={"shard": s + way}, device_id_type=MESH)

    def pcopy(i, b, to, slot, first, e=None, k=None):
        e = d if e is None else e
        src = (ins[i].at[to] if modes[i] == "swap" else ins[i]) if first else place(i, b, e, m)
        return pltpu.make_async_remote_copy(
            half_of(i, src, k), half_of(i, place(i, b, e, m), k),
            sems[7 * i + 2].at[b, slot], sems[7 * i + 3].at[b, e, k or 0],
            device_id={"dp": to}, device_id_type=MESH)

    def precv(i, b, e, k=None):
        ref = place(i, b, e, m)
        return pltpu.make_async_remote_copy(
            half_of(i, ref, k), half_of(i, ref, k), sems[7 * i + 2].at[b, 0], sems[7 * i + 3].at[b, e, k or 0],
            device_id={"dp": peers[0]}, device_id_type=MESH)

    def own_copies(i, b, first):
        if relay[i]:
            return [pcopy(i, b, x, 0, first, k=0), pcopy(i, b, y, 1, first, k=1),
                    pcopy(i, b, x, 2, first, k=1), pcopy(i, b, y, 3, first, k=0)]
        return [pcopy(i, b, e, j, first) for j, e in enumerate(peers)]

    def pass_copies(i, b):
        return [(precv(i, b, x, 0), pcopy(i, b, y, 4, False, x, 0)),
                (precv(i, b, y, 1), pcopy(i, b, x, 5, False, y, 1))]

    def ccopy(i, b, e, first):
        src = ins[i] if first else place(i, b, e, m)
        return pltpu.make_async_remote_copy(
            src, place(i, b, e, m), sems[7 * i + 4].at[b, e], sems[7 * i + 5].at[b, e],
            device_id={"mp": 1 - m}, device_id_type=MESH)

    def crecv(i, b, e):
        ref = place(i, b, e, 1 - m)
        return pltpu.make_async_remote_copy(
            ref, ref, sems[7 * i + 4].at[b, e], sems[7 * i + 5].at[b, e],
            device_id={"mp": 1 - m}, device_id_type=MESH)

    def dcopy(i, to, block):
        return pltpu.make_async_remote_copy(
            ins[i], place(i, block, d, m), sems[7 * i].at[0, to], sems[7 * i + 1].at[block],
            device_id={"shard": to}, device_id_type=MESH)

    planes_off = [lax.rem(s + k, ns) for k in range(1, ns)]

    def lcopy(i):
        src = ins[i].at[d] if modes[i] == "swap" else ins[i]
        return pltpu.make_async_copy(src, place(i, s, d, m), sems[7 * i + 6])

    def in_z(i):
        return modes[i] in ("z", "all") and not direct[i]

    def in_plane(i, t):
        return modes[i] == "all" or (modes[i] in ("plane", "swap") and t == 0)

    def onward(i, b, t, way):
        first = t == 0
        if in_z(i):
            if way >= 0:
                when(s < ns - 1, lambda: zcopy(i, b, 1, first).start())
            if way <= 0:
                when(s > 0, lambda: zcopy(i, b, -1, first).start())
        if in_plane(i, t):
            for c in own_copies(i, b, first):
                c.start()
        if modes[i] == "all":
            ccopy(i, b, d, first).start()
        if first and direct[i]:
            for p in planes_off:
                dcopy(i, p, s).start()
        if first:
            lcopy(i).start()

    def arrive(i, b, t, way):
        zcopy(i, b, -way, False).wait_recv()
        onward(i, b, t, way)

    def pass_on(i, b):
        for got, on in pass_copies(i, b):
            got.wait_recv()
            on.start()

    def settle(i, b):
        if relay[i]:
            waits = [(x, [precv(i, b, x, 1)]), (y, [precv(i, b, y, 0)]),
                     (across, [precv(i, b, across, 0), precv(i, b, across, 1)])]
        else:
            waits = [(e, [precv(i, b, e)]) for e in peers]
        for e, got in waits:
            for w in got:
                w.wait_recv()
            if modes[i] == "all":
                ccopy(i, b, e, False).start()

    def finish(i, b, t, way):
        first = t == 0
        if in_z(i):
            if way >= 0:
                when(s < ns - 1, lambda: zcopy(i, b, 1, first).wait_send())
            if way <= 0:
                when(s > 0, lambda: zcopy(i, b, -1, first).wait_send())
        if in_plane(i, t):
            for c in own_copies(i, b, first):
                c.wait_send()
            if relay[i]:
                for _, on in pass_copies(i, b):
                    on.wait_send()
        if direct[i] and first:
            for p in planes_off:
                dcopy(i, p, s).wait_send()
        if modes[i] == "all":
            for e in [d] + peers:
                crecv(i, b, e).wait_recv()
                ccopy(i, b, e, False).wait_send()
        if first:
            lcopy(i).wait()

    def each(steps, chosen, fn):
        for b, t, way, ok in steps:
            for i in range(n):
                if chosen(i, t):
                    when(ok, partial(fn, i, b, t, way))

    steps = planes(s, ns)
    levels = [[q for q in steps if q[1] == t] for t in range(ns)]
    straight = [(b, 1, 0, True) for b in planes_off]
    lag = max(ns - 2, 1)
    each(levels[0], lambda i, t: not late[i], onward)

    def arrive_straight(i, b, t, way):
        dcopy(i, b, b).wait_recv()
        onward(i, b, t, way)

    def part(t):
        if work is not None and t < ns:
            work(t, ns, more_in, more_out)

    part(0)
    each(straight, lambda i, t: direct[i], arrive_straight)
    for t in range(1, ns + lag):
        if t < ns:
            each(levels[t], lambda i, t: in_z(i) and not late[i], arrive)
        if t == lag:
            each(levels[0], lambda i, t: late[i], onward)
        part(t)
        if t <= ns:
            each(levels[t - 1], lambda i, t: relay[i] and in_plane(i, t), lambda i, b, t, way: pass_on(i, b))
        if 1 <= t - lag:
            each(levels[t - lag], lambda i, t: late[i], arrive)
    each(steps, lambda i, t: in_plane(i, t) and not direct[i], lambda i, b, t, way: settle(i, b))
    each(levels[0] + straight, lambda i, t: direct[i], lambda i, b, t, way: settle(i, b))
    each(steps, lambda i, t: (t == 0 or in_z(i)) and not direct[i], finish)
    each(levels[0] + straight, lambda i, t: direct[i], finish)


def gather(collective, mesh_shape, items, work=None, work_args=(), work_outs=()):
    ns, nd = mesh_shape["shard"], mesh_shape["dp"]
    modes = tuple(mode for _, mode in items)
    lead = {"z": (ns,), "plane": (nd,), "all": (ns, nd, 2), "swap": ()}
    shapes = [jax.ShapeDtypeStruct(lead[mode] + a.shape, a.dtype) for a, mode in items]
    sems = []
    dma = pltpu.SemaphoreType.DMA
    for _ in items:
        sems += [dma((2, ns)), dma((ns,)), dma((ns, max(nd, 6))), dma((ns, nd, 2)), dma((ns, nd)), dma((ns, nd)),
                 dma(())]
    return pl.pallas_call(
        partial(gather_kernel, ns, nd, modes, work, len(work_args)),
        out_shape=shapes + list(work_outs),
        in_specs=[pl.BlockSpec(memory_space=pl.ANY)] * len(items)
        + [pl.BlockSpec(memory_space=pltpu.VMEM)] * len(work_args),
        out_specs=[pl.BlockSpec(memory_space=pl.ANY)] * len(items)
        + [pl.BlockSpec(memory_space=pltpu.VMEM)] * len(work_outs),
        scratch_shapes=sems,
        compiler_params=pltpu.CompilerParams(
            collective_id=collective, has_side_effects=True, vmem_limit_bytes=VMEM_LIMIT),
        cost_estimate=pl.CostEstimate(flops=0, bytes_accessed=1 << 20, transcendentals=0),
    )(*[a for a, _ in items], *work_args)


def reduce_kernel(ns, nd, share, count, made, *refs):
    n_in = 2 * count if made else 1
    ins, outs, scratch = refs[:n_in], refs[n_in : n_in + count], refs[n_in + count :]
    own, sib, give, got, mid, zgot, fin, lsem, ss, sr, ps, pr, zs, zr, fs, fr, ks = scratch
    s, d, m = (lax.axis_index(a) for a in ("shard", "dp", "mp"))
    h, c = fin.shape[1:]
    tile = 16
    greet(ns, nd, True, True, True, z_all=True)
    peers = [lax.rem(d + k, nd) for k in range(1, nd)]
    relay = nd == 4 and h % 32 == 0
    if relay:
        x, y, across = square(d)
        peers = [across, x, y]
    chain = bool(made)
    if chain:
        order = []
        for k in range(ns - 1):
            up = jnp.where(k < ns - 1 - s, ns - 1 - k, k - (ns - 1 - s))
            down = jnp.where(k < s, k, ns - 1 - (k - s))
            order.append(jnp.where(2 * s < ns, up, down))
        order.append(s)
    else:
        order = [lax.rem(s + k, ns) for k in sorted(range(1, ns), key=lambda k: abs(k - ns // 2))] + [s]
    items = [(a, k, order[k]) for k in range(ns) for a in range(count)]

    def score(a, k, b):
        src = give.at[a, k % 2] if made else ins[0].at[b, :, 1 - m]
        return pltpu.make_async_remote_copy(
            src, sib.at[a, b], ss.at[a, b], sr.at[a, b], device_id={"mp": 1 - m}, device_id_type=MESH)

    def load(a, b):
        return pltpu.make_async_copy(ins[0].at[b, :, m], own.at[a, b], lsem.at[a, b])

    def multiply(a, b, core, store):
        step = 512 if c % 512 == 0 else 128
        left = ins[a][b, :, core].reshape(nd * h, ins[a].shape[-1])

        @pl.loop(0, c // step)
        def _(j):
            cols = pl.ds(pl.multiple_of(j * step, step), step)
            term = cols_product(left, ins[count + a][cols])
            store(cols, term.astype(BF16).reshape(nd, h, step))

    def zero(a, k, b):
        if not made:
            score(a, k, b).start()
            load(a, b).start()
            return
        if k >= 2:
            score(a, k - 2, order[k - 2]).wait_send()

        def to_give(cols, v):
            give[a, k % 2, :, :, cols] = v

        def to_own(cols, v):
            own[a, b, :, :, cols] = v

        multiply(a, b, 1 - m, to_give)
        score(a, k, b).start()
        multiply(a, b, m, to_own)

    def pcopy(a, b, src, dst, slot, to):
        return pltpu.make_async_remote_copy(
            src, dst, ps.at[a, b, slot], pr.at[a, b, slot], device_id={"dp": to}, device_id_type=MESH)

    def sends(a, b):
        if not relay:
            return [pltpu.make_async_remote_copy(
                own.at[a, b, e], got.at[a, b, d], ps.at[a, b, e], pr.at[a, b, d],
                device_id={"dp": e}, device_id_type=MESH) for e in peers]
        half = h // 2
        first, last = pl.ds(0, half), pl.ds(half, half)
        return [
            pcopy(a, b, own.at[a, b, across, first], got.at[a, b, 0, first], 0, x),
            pcopy(a, b, own.at[a, b, across, last], got.at[a, b, 0, last], 1, y),
            pcopy(a, b, own.at[a, b, x], got.at[a, b, 1], 2, x),
            pcopy(a, b, own.at[a, b, y], got.at[a, b, 2], 3, y),
        ]

    def zcopy(a, b, to):
        return pltpu.make_async_remote_copy(
            mid.at[a, b], zgot.at[a, to], zs.at[a, b], zr.at[a, to], device_id={"shard": b}, device_id_type=MESH)

    def sum_rows(lo, hi, terms, store):
        @pl.loop(lo // tile, hi // tile)
        def _(r):
            at = pl.ds(pl.multiple_of(r * tile, tile), tile)
            v = terms[0](at).astype(F32)
            for f in terms[1:]:
                v = v + f(at).astype(F32)
            store(at, v.astype(BF16))

    def to_own(a, b, e):
        def store(at, v):
            own[a, b, e, at] = v
        return store

    def one(a, k, b):
        score(a, k, b).wait_recv()
        if not made:
            load(a, b).wait()
        out_now = sends(a, b)
        for j, e in enumerate(peers + [d]):
            sum_rows(0, h, [lambda at, e=e: own[a, b, e, at], lambda at, e=e: sib[a, b, e, at]], to_own(a, b, e))
            if relay and j == 0:
                out_now[0].start()
                out_now[1].start()
            elif not relay and j < len(peers):
                out_now[j].start()

    def two(a, k, b):
        if not relay:
            return
        half = h // 2
        c0, c1, c2, c3 = sends(a, b)
        c0.wait_recv()
        sum_rows(0, half, [lambda at: own[a, b, y, at], lambda at: got[a, b, 0, at]], to_own(a, b, y))
        c3.start()
        c1.wait_recv()
        sum_rows(half, h, [lambda at: own[a, b, x, at], lambda at: got[a, b, 0, at]], to_own(a, b, x))
        c2.start()

    def plane_terms(a, b):
        slots = [1, 2] if relay else peers
        return [lambda at: own[a, b, d, at]] + [lambda at, e=e: got[a, b, e, at] for e in slots]

    def three(a, k, b):
        if relay:
            for w in sends(a, b)[2:]:
                w.wait_recv()
        else:
            for e in peers:
                pltpu.make_async_remote_copy(
                    own.at[a, b, e], got.at[a, b, e], ps.at[a, b, e], pr.at[a, b, e],
                    device_id={"dp": e}, device_id_type=MESH).wait_recv()
        if k < ns - 1:
            def store(at, v):
                mid[a, b, at] = v
            sum_rows(0, h, plane_terms(a, b), store)
            if not chain:
                zcopy(a, b, s).start()

    def hop(a, b, way):
        slot = jnp.where(s + way == b, jnp.where(way > 0, b, ns), b)
        return pltpu.make_async_remote_copy(
            mid.at[a, b], zgot.at[a, slot], zs.at[a, b], zr.at[a, slot],
            device_id={"shard": s + way}, device_id_type=MESH)

    def came(a, slot):
        return pltpu.make_async_remote_copy(
            mid.at[a, s], zgot.at[a, slot], zs.at[a, s], zr.at[a, slot], device_id={"mp": 1 - m},
            device_id_type=MESH)

    def four(a, k, b):
        if k == ns - 1:
            return

        def add():
            came(a, b).wait_recv()

            def store(at, v):
                mid[a, b, at] = v
            sum_rows(0, h, [lambda at: mid[a, b, at], lambda at: zgot[a, b, at]], store)

        upward = b > s
        pl.when(jnp.where(upward, s > 0, s < ns - 1))(add)
        pl.when(upward)(lambda: hop(a, b, 1).start())
        pl.when(jnp.logical_not(upward))(lambda: hop(a, b, -1).start())

    stages = [zero, one, two, three] + ([four] if chain else [])
    if not made:
        for item in items:
            zero(*item)
        stages = stages[1:]
    for t in range(len(items) + len(stages) - 1):
        for j, stage in enumerate(stages):
            if 0 <= t - j < len(items):
                stage(*items[t - j])

    def give_out(a, core):
        return pltpu.make_async_remote_copy(
            fin.at[a], outs[a].at[core], fs.at[a], fr.at[a], device_id={"mp": 1 - m}, device_id_type=MESH)

    def keep(a):
        return pltpu.make_async_copy(fin.at[a], outs[a].at[m] if share else outs[a], ks.at[a])

    others = order[:-1]
    for a in range(count):
        def store(at, v, a=a):
            fin[a, at] = v

        if chain:
            sum_rows(0, h, plane_terms(a, s), store)
            for slot, ok in ((s, s > 0), (ns, s < ns - 1)):

                def add(slot=slot):
                    came(a, slot).wait_recv()
                    sum_rows(0, h, [lambda at: fin[a, at], lambda at: zgot[a, slot, at]], store)

                pl.when(ok)(add)
        else:
            for b in others:
                zcopy(a, b, b).wait_recv()
            sum_rows(0, h, plane_terms(a, s) + [lambda at, b=b: zgot[a, b, at] for b in others], store)
        if share:
            give_out(a, m).start()
        keep(a).start()
    for a in range(count):
        if share:
            give_out(a, 1 - m).wait_recv()
            give_out(a, m).wait_send()
        keep(a).wait()
        for k, b in enumerate(order):
            if not made or k >= ns - 2:
                score(a, k, b).wait_send()
            for w in sends(a, b):
                w.wait_send()
        for b in others:
            zcopy(a, b, s).wait_send()


def reduce_scatter(collective, mesh_shape, share, blocks, terms=None, factors=None):
    ns, nd = mesh_shape["shard"], mesh_shape["dp"]
    rows, c = blocks
    h = rows // 2
    count = len(factors) if factors else 1
    size = ns * nd * h * c * 2
    if size * count * 3 > (40 << 20):
        whole = [terms] if factors is None else [
            cols_product(x, w).astype(BF16) for x, w in factors]
        sums = []
        for p in whole:
            total = lax.psum_scatter(p.reshape(ns * nd, 2, h, c), TOK, scatter_dimension=0, tiled=True)[0]
            total = lax.psum(total, "mp")
            sums.append(total if share else lax.dynamic_index_in_dim(total, lax.axis_index("mp"), 0, False))
        return sums
    if factors is None:
        made = False
        args = [terms.reshape(ns, nd, 2, h, c)]
        in_specs = [pl.BlockSpec(memory_space=pl.ANY)]
        give = (1, 1, 1, 16, 128)
    else:
        made = True
        args = [x.reshape(ns, nd, 2, h, -1) for x, _ in factors] + [w for _, w in factors]
        in_specs = [pl.BlockSpec(memory_space=pltpu.VMEM)] * (2 * count)
        give = (count, 2, nd, h, c)
    slots = 3 if nd == 4 and h % 32 == 0 else nd
    dma = pltpu.SemaphoreType.DMA
    return pl.pallas_call(
        partial(reduce_kernel, ns, nd, share, count, made),
        out_shape=[jax.ShapeDtypeStruct((2, h, c) if share else (h, c), BF16)] * count,
        in_specs=in_specs,
        out_specs=[pl.BlockSpec(memory_space=pl.ANY)] * count,
        scratch_shapes=[
            pltpu.VMEM((count, ns, nd, h, c), BF16),
            pltpu.VMEM((count, ns, nd, h, c), BF16),
            pltpu.VMEM(give, BF16),
            pltpu.VMEM((count, ns, slots, h, c), BF16),
            pltpu.VMEM((count, ns, h, c), BF16),
            pltpu.VMEM((count, ns + 1, h, c), BF16),
            pltpu.VMEM((count, h, c), BF16),
            dma((count, ns)), dma((count, ns)), dma((count, ns)),
            dma((count, ns, max(nd, 4))), dma((count, ns, max(nd, 4))),
            dma((count, ns)), dma((count, ns + 1)), dma((count,)), dma((count,)), dma((count,)),
        ],
        compiler_params=pltpu.CompilerParams(
            collective_id=collective, has_side_effects=True, vmem_limit_bytes=VMEM_LIMIT),
        cost_estimate=pl.CostEstimate(flops=0, bytes_accessed=1 << 20, transcendentals=0),
    )(*args)


def gelu_both(v):
    root, cube = 0.7978845608028654, 0.044715
    t = jnp.tanh(root * (v + cube * v * v * v))
    slope = 0.5 * (1.0 + t) + 0.5 * v * (1.0 - t * t) * (root * (1.0 + 3.0 * cube * v * v))
    return 0.5 * v * (1.0 + t), slope


def feed_kernel(ns, nd, x, cot, wide, thin, act, low, wide_grad, thin_grad, hid, cots, acc, more, zs, zr, ps, pr, cs, cr,
                ls, ks):
    s, d, m = (lax.axis_index(a) for a in ("shard", "dp", "mp"))
    h, width = x.shape
    units = thin.shape[1]
    relay = nd == 4 and h % 32 == 0
    greet(ns, nd, True, True, True, z_all=True)
    turns = [0] + sorted(range(1, ns), key=lambda k: min(k, ns - k))
    order = [lax.rem(s + k, ns) for k in turns]
    peers = [lax.rem(d + k, nd) for k in range(1, nd)]
    if relay:
        xn, yn, across = square(d)
        peers = [xn, yn, across]

    def zsend(b):
        return pltpu.make_async_remote_copy(
            x, hid.at[s, d, m], zs.at[b], zr.at[s], device_id={"shard": b}, device_id_type=MESH)

    def zrecv(b):
        return pltpu.make_async_remote_copy(
            x, hid.at[b, d, m], zs.at[b], zr.at[b], device_id={"shard": b}, device_id_type=MESH)

    def part(ref, k):
        return ref if k is None else ref.at[pl.ds(k * (h // 2), h // 2)]

    def source(b, e, first):
        return x if first else hid.at[b, e, m]

    def psend(b, e, to, slot, k, first):
        return pltpu.make_async_remote_copy(
            part(source(b, e, first), k), part(hid.at[b, e, m], k), ps.at[b, slot], pr.at[b, e, k or 0],
            device_id={"dp": to}, device_id_type=MESH)

    def precv(b, e, k):
        ref = part(hid.at[b, e, m], k)
        return pltpu.make_async_remote_copy(
            ref, ref, ps.at[b, 0], pr.at[b, e, k or 0], device_id={"dp": peers[0]}, device_id_type=MESH)

    def own_sends(b, first):
        if relay:
            return [psend(b, d, xn, 0, 0, first), psend(b, d, yn, 1, 1, first),
                    psend(b, d, xn, 2, 1, first), psend(b, d, yn, 3, 0, first)]
        return [psend(b, d, e, j, None, first) for j, e in enumerate(peers)]

    def pass_sends(b):
        if relay:
            return [(precv(b, xn, 0), psend(b, xn, yn, 4, 0, False)),
                    (precv(b, yn, 1), psend(b, yn, xn, 5, 1, False))]
        return []

    def share(b, e, core, first=False):
        ref = hid.at[b, e, core]
        return pltpu.make_async_remote_copy(
            x if first else ref, ref, cs.at[b, e], cr.at[b, e], device_id={"mp": 1 - m}, device_id_type=MESH)

    def load(b):
        return pltpu.make_async_copy(cot.at[b], cots.at[b], ls.at[b])

    def begin(k):
        b = order[k]
        if k > 0:
            zrecv(b).wait_recv()
        for c in own_sends(b, k == 0):
            c.start()
        share(b, d, m, k == 0).start()

    def hand_on(k):
        for got, on in pass_sends(order[k]):
            got.wait_recv()
            on.start()

    def settle(k):
        b = order[k]
        for e in peers:
            for q in waits(e):
                precv(b, e, q).wait_recv()
            share(b, e, m).start()

    def waits(e):
        if not relay:
            return [None]
        return [1] if e is xn else [0] if e is yn else [0, 1]

    def ready(k):
        b = order[k]
        for e in [d] + peers:
            share(b, e, 1 - m).wait_recv()
        if k == 0:
            keep.wait()
        load(b).wait()

    count = nd // 2 if nd % 2 == 0 else nd

    def forward(k, q):
        b = order[k]
        at = pl.ds(q * count, count)
        rows = count * 2 * h
        pre = product(hid[b, at].reshape(rows, width), wide[...])
        back = product(cots[b, at].reshape(rows, width), thin[...])
        value, slope = gelu_both(pre[:, :units])
        up = pre[:, units:]
        act[b, at] = (value * up).astype(BF16).reshape(count, 2, h, units)
        low[b, at, :, :, :units] = (back * up * slope).astype(BF16).reshape(count, 2, h, units)
        low[b, at, :, :, units:] = (back * value).astype(BF16).reshape(count, 2, h, units)

    def backward(k):
        b = order[k]
        rows = nd * 2 * h
        step = 512 if width % 512 == 0 else 128
        lows = low[b].reshape(rows, 2 * units)
        acts = act[b].reshape(rows, units)

        @pl.loop(0, width // step)
        def _(j):
            at = pl.ds(pl.multiple_of(j * step, step), step)
            one = rows_product(hid[b, :, :, :, at].reshape(rows, step), lows)
            two = rows_product(cots[b, :, :, :, at].reshape(rows, step), acts)
            if k > 0:
                one = one + acc[at]
                two = two + more[at]
            if k < ns - 1:
                acc[at] = one
                more[at] = two
            else:
                wide_grad[at] = one.astype(BF16)
                thin_grad[at] = two.astype(BF16)

    for b in order[1:]:
        zsend(b).start()
    keep = pltpu.make_async_copy(x, hid.at[s, d, m], ks)
    keep.start()
    begin(0)
    for b in order:
        load(b).start()
    hand_on(0)
    if ns > 1:
        begin(1)
        hand_on(1)
    for k in range(ns):
        settle(k)
        ready(k)
        forward(k, 0)
        if count < nd:
            forward(k, 1)
        if k + 2 < ns:
            begin(k + 2)
        backward(k)
        if k + 2 < ns:
            hand_on(k + 2)
    for k, b in enumerate(order):
        for c in own_sends(b, k == 0):
            c.wait_send()
        for _, c in pass_sends(b):
            c.wait_send()
        for e in [d] + peers:
            share(b, e, m).wait_send()
        if k > 0:
            zsend(b).wait_send()


def feed(collective, mesh_shape, x, cot, wide, thin):
    ns, nd = mesh_shape["shard"], mesh_shape["dp"]
    h, width = x.shape
    units = thin.shape[1]
    rows = (ns, nd, 2, h)
    if 2 * cot.size * 2 > (24 << 20):
        (hid,) = gather(collective, mesh_shape, [(x, "all")])
        hid, cot = hid.reshape(-1, width), cot.reshape(-1, width)
        pre = product(hid, wide)
        back = product(cot, thin)
        value, slope = gelu_both(pre[:, :units])
        up = pre[:, units:]
        act = (value * up).astype(BF16)
        low = jnp.concatenate([back * up * slope, back * value], axis=1).astype(BF16)
        return act, low, rows_product(hid, low).astype(BF16), rows_product(cot, act).astype(BF16)
    dma = pltpu.SemaphoreType.DMA
    vmem = pl.BlockSpec(memory_space=pltpu.VMEM)
    act, low, wide_grad, thin_grad = pl.pallas_call(
        partial(feed_kernel, ns, nd),
        out_shape=[
            jax.ShapeDtypeStruct(rows + (units,), BF16),
            jax.ShapeDtypeStruct(rows + (2 * units,), BF16),
            jax.ShapeDtypeStruct((width, 2 * units), BF16),
            jax.ShapeDtypeStruct((width, units), BF16),
        ],
        in_specs=[vmem, pl.BlockSpec(memory_space=pl.ANY), vmem, vmem],
        out_specs=[vmem] * 4,
        scratch_shapes=[
            pltpu.VMEM(rows + (width,), BF16),
            pltpu.VMEM(rows + (width,), BF16),
            pltpu.VMEM((width, 2 * units), F32),
            pltpu.VMEM((width, units), F32),
            dma((ns,)), dma((ns,)), dma((ns, max(nd, 6))), dma((ns, nd, 2)), dma((ns, nd)), dma((ns, nd)),
            dma((ns,)), dma(()),
        ],
        compiler_params=pltpu.CompilerParams(
            collective_id=collective, has_side_effects=True, vmem_limit_bytes=VMEM_LIMIT),
        cost_estimate=pl.CostEstimate(flops=0, bytes_accessed=1 << 20, transcendentals=0),
    )(x, cot, wide, thin)
    return act.reshape(-1, units), low.reshape(-1, 2 * units), wide_grad, thin_grad


def plane_kernel(ns, nd, p, out, own, sib, ls, ss, sr, ps, pr, fs, fr, ks):
    d, m = lax.axis_index("dp"), lax.axis_index("mp")
    h, c = own.shape[1:]
    tile = 16
    greet(ns, nd, False, True, True)
    peers = [lax.rem(d + k, nd) for k in range(1, nd)]
    order = ([square(d)[2], square(d)[0], square(d)[1]] if nd == 4 else peers) + [d]
    other = {"mp": 1 - m}

    def score(e):
        return pltpu.make_async_remote_copy(
            p.at[e, 1 - m], sib.at[e], ss.at[e], sr.at[e], device_id=other, device_id_type=MESH)

    def load(e):
        return pltpu.make_async_copy(p.at[e, m], own.at[e], ls.at[e])

    def send(e, block):
        return pltpu.make_async_remote_copy(
            own.at[e], out.at[block, m], ps.at[e], pr.at[block], device_id={"dp": e}, device_id_type=MESH)

    def share(e, core):
        src = own.at[d] if e is d else out.at[e, m]
        return pltpu.make_async_remote_copy(
            src, out.at[e, core], fs.at[e], fr.at[e], device_id=other, device_id_type=MESH)

    for e in order:
        score(e).start()
        load(e).start()
    for e in order:
        score(e).wait_recv()
        load(e).wait()

        @pl.loop(0, h // tile)
        def _(r, e=e):
            at = pl.ds(pl.multiple_of(r * tile, tile), tile)
            own[e, at] = (own[e, at].astype(F32) + sib[e, at].astype(F32)).astype(BF16)

        if e is not d:
            send(e, d).start()
    keep = pltpu.make_async_copy(own.at[d], out.at[d, m], ks)
    keep.start()
    share(d, m).start()
    for e in order[:-1]:
        send(e, e).wait_recv()
        share(e, m).start()
    keep.wait()
    for e in order:
        share(e, 1 - m).wait_recv()
        share(e, m).wait_send()
        score(e).wait_send()
        if e is not d:
            send(e, d).wait_send()


def plane_reduce(collective, mesh_shape, p):
    ns, nd = mesh_shape["shard"], mesh_shape["dp"]
    h, c = p.shape[2:]
    dma = pltpu.SemaphoreType.DMA
    return pl.pallas_call(
        partial(plane_kernel, ns, nd),
        out_shape=jax.ShapeDtypeStruct(p.shape, BF16),
        in_specs=[pl.BlockSpec(memory_space=pl.ANY)],
        out_specs=pl.BlockSpec(memory_space=pl.ANY),
        scratch_shapes=[pltpu.VMEM((nd, h, c), BF16)] * 2 + [dma((nd,))] * 7 + [dma(())],
        compiler_params=pltpu.CompilerParams(
            collective_id=collective, has_side_effects=True, vmem_limit_bytes=VMEM_LIMIT),
        cost_estimate=pl.CostEstimate(flops=0, bytes_accessed=1 << 20, transcendentals=0),
    )(p)


def rope_tables(positions):
    half_dim = HEAD_DIM // 2
    exponent = jnp.arange(half_dim, dtype=F32) * (-2.0 / HEAD_DIM)
    angles = positions.astype(F32)[:, None] * jnp.power(ROPE_BASE, exponent)[None, :]
    return (jnp.cos(angles), jnp.sin(angles))


def rotate(values, cosine, sine_rows):
    half_dim = values.shape[-1] // 2
    front_half = values[..., :half_dim]
    back_half = values[..., half_dim:]
    return jnp.concatenate(
        [front_half * cosine - back_half * sine_rows, back_half * cosine + front_half * sine_rows], axis=-1)


def rows_product(left_side, right_side):
    return lax.dot_general(
        left_side, right_side, (((0,), (0,)), ((), ())), preferred_element_type=F32)


def cols_product(left_side, right_side):
    return lax.dot_general(
        left_side, right_side, (((1,), (1,)), ((), ())), preferred_element_type=F32)


def product(left_side, right_side):
    return jnp.dot(left_side, right_side, preferred_element_type=F32)


def turn(v, cosine, sine):
    half_dim = HEAD_DIM // 2
    front, back = v[:, :half_dim], v[:, half_dim:]
    return front * cosine - back * sine, back * cosine + front * sine


def window(nd, kv, keys, values):
    me = lax.axis_index("shard") * nd + lax.axis_index("dp")
    tok = kv.shape[2]
    for j in range(KV_BLOCKS + 1):
        b = jnp.maximum(me + (j - KV_BLOCKS), 0)
        keys[j * tok : (j + 1) * tok] = kv[b, 0]
        values[j * tok : (j + 1) * tok] = kv[b, 1]


def attend_kernel(nd, got, kv, allowed, cosine, sine, mixed, queries, probs, keys, values):
    window(nd, kv, keys, values)
    scale = HEAD_DIM ** (-0.5)
    half_dim = HEAD_DIM // 2
    cos, sin = cosine[...], sine[...]
    for h in range(probs.shape[0]):
        at = h * HEAD_DIM
        raw = got[0, :, at : at + HEAD_DIM].astype(F32)
        for e in range(1, got.shape[0]):
            raw = raw + got[e, :, at : at + HEAD_DIM].astype(F32)
        front, back = turn(raw, cos, sin)
        queries[:, at : at + half_dim] = front.astype(BF16)
        queries[:, at + half_dim : at + HEAD_DIM] = back.astype(BF16)
        scores = cols_product(queries[:, at : at + HEAD_DIM], keys[...]) * scale
        scores = jnp.where(allowed[...] > 0.0, scores, -jnp.inf)
        raised = jnp.exp(scores - jnp.max(scores, axis=1, keepdims=True))
        prob = raised / jnp.sum(raised, axis=1, keepdims=True)
        probs[h] = prob
        mixed[:, at : at + HEAD_DIM] = product(prob.astype(BF16), values[...]).astype(BF16)


def attend(nd, heads, got, kv, allowed, cosine, sine):
    tok = got.shape[1]
    span = allowed.shape[1]
    return pl.pallas_call(
        partial(attend_kernel, nd),
        out_shape=[
            jax.ShapeDtypeStruct((tok, heads * HEAD_DIM), BF16),
            jax.ShapeDtypeStruct((tok, heads * HEAD_DIM), BF16),
            jax.ShapeDtypeStruct((heads, tok, span), F32),
        ],
        in_specs=[pl.BlockSpec(memory_space=pltpu.VMEM)] * 5,
        out_specs=[pl.BlockSpec(memory_space=pltpu.VMEM)] * 3,
        scratch_shapes=[pltpu.VMEM((span, HEAD_DIM), BF16)] * 2,
        compiler_params=pltpu.CompilerParams(vmem_limit_bytes=VMEM_LIMIT),
    )(got, kv, allowed, cosine, sine)


def attend_back_kernel(nd, got, kv, queries, probs, cosine, sine, kv_grad, low, keys, values, key_sum, value_sum):
    window(nd, kv, keys, values)
    me = lax.axis_index("shard") * nd + lax.axis_index("dp")
    scale = HEAD_DIM ** (-0.5)
    half_dim = HEAD_DIM // 2
    n, _, tok, _ = kv.shape
    cos, sin = cosine[...], sine[...]
    for h in range(probs.shape[0]):
        at = h * HEAD_DIM
        raw = got[0, :, at : at + HEAD_DIM].astype(F32)
        for e in range(1, got.shape[0]):
            raw = raw + got[e, :, at : at + HEAD_DIM].astype(F32)
        mixed_grad = raw.astype(BF16)
        prob = probs[h]
        prob_grad = cols_product(mixed_grad, values[...])
        inner = jnp.sum(prob * prob_grad, axis=1, keepdims=True)
        scores_low = (prob * (prob_grad - inner) * scale).astype(BF16)
        front, back = turn(product(scores_low, keys[...]), cos, -sin)
        low[:, at : at + half_dim] = front.astype(BF16)
        low[:, at + half_dim : at + HEAD_DIM] = back.astype(BF16)
        key_part = rows_product(scores_low, queries[:, at : at + HEAD_DIM])
        value_part = rows_product(prob.astype(BF16), mixed_grad)
        if h == 0:
            key_sum[...] = key_part
            value_sum[...] = value_part
        else:
            key_sum[...] += key_part
            value_sum[...] += value_part

    @pl.loop(0, n)
    def _(b):
        kv_grad[b] = jnp.zeros(kv_grad.shape[1:], BF16)

    for j in range(KV_BLOCKS + 1):
        b = me + (j - KV_BLOCKS)

        @pl.when(b >= 0)
        def _(j=j, b=b):
            kv_grad[b, 0] = key_sum[j * tok : (j + 1) * tok].astype(BF16)
            kv_grad[b, 1] = value_sum[j * tok : (j + 1) * tok].astype(BF16)


def attend_back(nd, got, kv, queries, probs, cosine, sine):
    span = probs.shape[2]
    return pl.pallas_call(
        partial(attend_back_kernel, nd),
        out_shape=[jax.ShapeDtypeStruct(kv.shape, BF16), jax.ShapeDtypeStruct(queries.shape, BF16)],
        in_specs=[pl.BlockSpec(memory_space=pltpu.VMEM)] * 6,
        out_specs=[pl.BlockSpec(memory_space=pltpu.VMEM)] * 2,
        scratch_shapes=[pltpu.VMEM((span, HEAD_DIM), BF16)] * 2 + [pltpu.VMEM((span, HEAD_DIM), F32)] * 2,
        compiler_params=pltpu.CompilerParams(vmem_limit_bytes=VMEM_LIMIT),
    )(got, kv, queries, probs, cosine, sine)


ROWS = 16


def row_tiles(count, body):
    @pl.loop(0, count // ROWS)
    def _(r):
        body(pl.ds(pl.multiple_of(r * ROWS, ROWS), ROWS))


def pieces(nd, width, plane_d, own_d):
    for j in range(width // own_d):
        yield j * own_d, j % nd, (j // nd) * own_d


def inverse_of(rows):
    return lax.rsqrt(jnp.mean(rows * rows, axis=1, keepdims=True) + EPS_NORM)


def norm_back(rows, gain, grad):
    inverse = inverse_of(rows)
    normed = rows * inverse
    scaled = grad * gain
    inner = jnp.mean(normed * scaled, axis=1, keepdims=True)
    return inverse * (scaled - normed * inner), grad * normed


def join_kernel(own_d, got, tokens, gain, residual, hidden):
    nd, tok, plane_d = got.shape
    half = hidden.shape[0]
    first = lax.axis_index("mp") * half

    def add(at):
        for c, e, p in pieces(nd, tokens.shape[1], plane_d, own_d):
            residual[at, c : c + own_d] = (
                got[e, at, p : p + own_d].astype(F32) + tokens[at, c : c + own_d].astype(F32))

    row_tiles(tok, add)

    @pl.loop(0, half // ROWS)
    def _(r):
        rows = residual[pl.ds(pl.multiple_of(first + r * ROWS, ROWS), ROWS)]
        at = pl.ds(pl.multiple_of(r * ROWS, ROWS), ROWS)
        hidden[at] = (rows * inverse_of(rows) * gain[...]).astype(BF16)


def split_kernel(own_d, grad, ffn, residual, gain, cot, block_out, residual_grad, cut, gain_cut, total):
    nd, tok, plane_d = cut.shape
    total[...] = jnp.zeros_like(total)

    def body(at):
        rows = residual[at]
        block_out[at] = (rows + ffn[at].astype(F32)).astype(BF16)
        back, terms = norm_back(rows, gain[...], grad[at].astype(F32))
        total[...] += terms
        value = cot[at].astype(F32) + back
        residual_grad[at] = value
        for c, e, p in pieces(nd, grad.shape[1], plane_d, own_d):
            cut[e, at, p : p + own_d] = value[:, c : c + own_d].astype(BF16)

    row_tiles(tok, body)
    gain_cut[...] = jnp.zeros_like(gain_cut)
    sums = jnp.sum(total[...], axis=0, keepdims=True)
    for c, e, p in pieces(nd, grad.shape[1], plane_d, own_d):
        gain_cut[e, 0:1, p : p + own_d] = sums[:, c : c + own_d]


def last_kernel(own_d, got, tokens, gain, residual_grad, out, grad):
    nd, tok, plane_d = got.shape

    def body(at):
        for c, e, p in pieces(nd, tokens.shape[1], plane_d, own_d):
            grad[:, c : c + own_d] = got[e, at, p : p + own_d].astype(F32)
        back, _ = norm_back(tokens[at].astype(F32), gain[...], grad[...])
        out[at] = residual_grad[at] + back

    row_tiles(tok, body)


def local(kernel, outs, args, scratch=()):
    return pl.pallas_call(
        kernel,
        out_shape=[jax.ShapeDtypeStruct(shape, dtype) for shape, dtype in outs],
        in_specs=[pl.BlockSpec(memory_space=pltpu.VMEM)] * len(args),
        out_specs=[pl.BlockSpec(memory_space=pltpu.VMEM)] * len(outs),
        scratch_shapes=[pltpu.VMEM(shape, dtype) for shape, dtype in scratch],
        compiler_params=pltpu.CompilerParams(vmem_limit_bytes=VMEM_LIMIT),
    )(*args)


def pack(part, parts, ins, outs):
    gateup, down = ins
    pair, single = outs
    n, _, units = single.shape
    full = down.shape[1] // units
    share = -(-n // parts)
    for j in range(part * share, min((part + 1) * share, n)):
        if j >= full:
            pair[j] = jnp.zeros(pair.shape[1:], BF16)
            single[j] = jnp.zeros(single.shape[1:], BF16)
            continue
        at = pl.ds(j * units, units)
        pair[j, :, :units] = gateup[:, 0, at]
        pair[j, :, units:] = gateup[:, 1, at]
        single[j] = down[:, at]


def adam_step(rates, grad, weight, first, second, decay):
    first_new = BETA_ONE * first + (1.0 - BETA_ONE) * grad
    second_new = BETA_TWO * second + (1.0 - BETA_TWO) * grad * grad
    direction = first_new * rates[0] / (jnp.sqrt(second_new * rates[1]) + ADAM_EPS)
    return first_new, second_new, -LEARN_RATE * (direction + decay * weight.astype(F32))


def unpack_kernel(rates, pair_got, got, gw, gf, gs, dw, df, ds, gg, gfn, gsn, gu, dg, dfn, dsn, du):
    units = dw.shape[1]
    pair = (rates[0], rates[1])
    for k in range(2):
        grad = pair_got[0, :, k * units : (k + 1) * units].astype(F32)
        gg[:, k, :] = grad
        gfn[:, k, :], gsn[:, k, :], gu[:, k, :] = adam_step(
            pair, grad, gw[:, k, :], gf[:, k, :], gs[:, k, :], DECAY_RATE)
    grad = got[0].astype(F32)
    dg[...] = grad
    dfn[...], dsn[...], du[...] = adam_step(pair, grad, dw[...], df[...], ds[...], DECAY_RATE)


def unpack_adam(units, rates, pair_got, got, gateup, down):
    own_d, _, ff_local = gateup[0].shape
    three = pl.BlockSpec((own_d, 2, units), lambda j: (0, 0, j))
    two = pl.BlockSpec((own_d, units), lambda j: (0, j))
    shape3 = jax.ShapeDtypeStruct(gateup[0].shape, F32)
    shape2 = jax.ShapeDtypeStruct(down[0].shape, F32)
    out = pl.pallas_call(
        unpack_kernel,
        out_shape=[shape3] * 4 + [shape2] * 4,
        grid=(ff_local // units,),
        in_specs=[
            pl.BlockSpec(memory_space=pltpu.SMEM),
            pl.BlockSpec((1, own_d, 2 * units), lambda j: (j, 0, 0)),
            pl.BlockSpec((1, own_d, units), lambda j: (j, 0, 0)),
        ] + [three] * 3 + [two] * 3,
        out_specs=[three] * 4 + [two] * 4,
        compiler_params=pltpu.CompilerParams(vmem_limit_bytes=VMEM_LIMIT),
    )(rates, pair_got, got, *gateup, *down)
    return out[:4], out[4:]


def shards(
    mesh_shape,
    tokens_in,
    segment_ids,
    block_cotangent,
    query_weight,
    keyval_weight,
    outproj_weight,
    gateup_weight,
    down_weight,
    norm_gains,
    query_first,
    keyval_first,
    outproj_first,
    gateup_first,
    down_first,
    gains_first,
    query_second,
    keyval_second,
    outproj_second,
    gateup_second,
    down_second,
    gains_second,
    step_count,
):
    ns, nd = mesh_shape["shard"], mesh_shape["dp"]
    n = ns * nd
    s, d, m = (lax.axis_index(a) for a in ("shard", "dp", "mp"))
    me = s * nd + d
    tok, width = tokens_in.shape
    own_d = query_weight.shape[0]
    q_cols = query_weight.shape[1]
    heads_local = q_cols // HEAD_DIM
    ff_local = gateup_weight.shape[2]
    units = -(-(-(-ff_local // n)) // 128) * 128
    ff_pad = units * n - ff_local
    half = tok // 2
    plane_tok = nd * tok
    plane_d = ns * own_d

    input_rows = tokens_in.astype(F32)
    inverse_one = lax.rsqrt(jnp.mean(input_rows * input_rows, axis=1) + EPS_NORM)
    lanes = max(256, -(-max(own_d, tok) // 128) * 128)

    def line(v):
        return jnp.pad(v, ((0, 0), (0, lanes - v.shape[1])))

    small = jnp.concatenate(
        [line(norm_gains.astype(F32)), line(segment_ids.astype(F32)[None]), line(inverse_one[None]),
         jnp.zeros((4, lanes), F32)], axis=0)
    qkv_weight = jnp.concatenate(
        [query_weight, lax.dynamic_slice_in_dim(keyval_weight, m * HEAD_DIM, HEAD_DIM, 1)], axis=1)

    def plane_cut(value):
        return value.reshape(tok, ns, nd, own_d).transpose(2, 0, 1, 3).reshape(nd, tok, plane_d)

    small_all, tokens_plane, cot_all, qkv_plane, pair, single = gather(
        0, mesh_shape,
        [(small, "all"), (plane_cut(tokens_in), "swap"),
         (lax.dynamic_slice_in_dim(block_cotangent, m * half, half, 0), "all"), (qkv_weight, "z")],
        pack, (gateup_weight, down_weight.T),
        (jax.ShapeDtypeStruct((n, own_d, 2 * units), BF16), jax.ShapeDtypeStruct((n, own_d, units), BF16)))
    tokens_plane = tokens_plane.reshape(plane_tok, plane_d)

    def trade(value):
        return lax.all_to_all(value.reshape(n, own_d, -1), TOK, 0, 0, tiled=True)

    pair, tokens_plane = lax.optimization_barrier((pair, tokens_plane))
    pair = trade(pair).reshape(width, 2 * units)
    qkv_plane = qkv_plane.reshape(plane_d, q_cols + HEAD_DIM)
    small_all = small_all[:, :, 0]
    gains_by = small_all[:, :, :2, :own_d]
    full_gains = gains_by.transpose(2, 0, 1, 3).reshape(2, width)
    tags = small_all[:, :, 2, :tok].reshape(n * tok)
    plane_scale = lax.dynamic_index_in_dim(small_all[:, :, 3, :tok], s, 0, False).reshape(plane_tok, 1)
    plane_gain = lax.dynamic_index_in_dim(gains_by[:, :, 0], d, 1, False).reshape(1, plane_d)


    def from_plane(collective, value):
        got = plane_reduce(collective, mesh_shape, value.reshape(nd, 2, half, plane_d))
        return got.reshape(nd, tok, plane_d)

    def plane_terms(collective, value):
        return gather(collective, mesh_shape, [(value.reshape(nd, tok, -1), "swap")])[0]

    hidden_plane = (tokens_plane.astype(F32) * plane_scale * plane_gain).astype(BF16)
    qkv_terms = plane_terms(8, product(hidden_plane, qkv_plane).astype(BF16))

    pad = KV_BLOCKS * tok
    key_span = pad + tok
    start = me * tok
    tag_pad = jnp.concatenate([jnp.full((pad,), -1.0, F32), tags])
    key_tags = lax.dynamic_slice_in_dim(tag_pad, start, key_span, 0)
    own_tags = segment_ids.astype(F32)
    query_index = jnp.arange(tok, dtype=jnp.int32) + pad
    key_index = jnp.arange(key_span, dtype=jnp.int32)
    same_segment = key_tags[None, :] == own_tags[:, None]
    allowed = same_segment & (key_index[None, :] <= query_index[:, None])
    positions = jnp.sum(
        (same_segment & (key_index[None, :] < query_index[:, None])).astype(jnp.int32), axis=1)
    cosine, sine_rows = rope_tables(positions)
    kv_raw = jnp.sum(qkv_terms[:, :, q_cols:].astype(F32), axis=0)
    kv_mine = jnp.where(m == 0, rotate(kv_raw, cosine, sine_rows), kv_raw).astype(BF16)
    (kv_all,) = gather(1, mesh_shape, [(kv_mine, "all")])
    single, pair, kv_all = lax.optimization_barrier((single, pair, kv_all))
    single = trade(single).reshape(width, units)
    kv_all = kv_all.reshape(n, 2, tok, HEAD_DIM)
    mixed_low, queries, probs = attend(
        nd, heads_local, qkv_terms, kv_all, allowed.astype(F32), cosine, sine_rows)
    mixed_plane, outproj_z = gather(
        2, mesh_shape, [(mixed_low, "plane"), (outproj_weight.T, "z")])
    mixed_plane = mixed_plane.reshape(plane_tok, q_cols)
    outproj_plane = outproj_z.reshape(plane_d, q_cols)
    residual, hidden_two = local(
        partial(join_kernel, own_d), [((tok, width), F32), ((half, width), BF16)],
        [from_plane(9, cols_product(mixed_plane, outproj_plane).astype(BF16)), tokens_in, full_gains[1:]])

    act_low, gateup_low, pair_grad, single_grad = feed(3, mesh_shape, hidden_two, cot_all, pair, single)
    pair_grad, act_low, gateup_low = lax.optimization_barrier((pair_grad, act_low, gateup_low))
    pair_grad = trade(pair_grad)
    hidden_two_grad, ffn_sum = reduce_scatter(
        4, mesh_shape, True, (tok, width), factors=[(gateup_low, pair), (act_low, single)])
    hidden_two_grad, single_grad, pair_grad = lax.optimization_barrier((hidden_two_grad, single_grad, pair_grad))
    single_grad = trade(single_grad)
    block_out, residual_grad, attn_cut, gain_cut = local(
        partial(split_kernel, own_d),
        [((tok, width), BF16), ((tok, width), F32), ((nd, tok, plane_d), BF16), ((nd, 8, plane_d), F32)],
        [hidden_two_grad.reshape(tok, width), ffn_sum.reshape(tok, width), residual, full_gains[1:],
         block_cotangent],
        [((ROWS, width), F32)])
    attn_low, gain_two_part = gather(10, mesh_shape, [(attn_cut, "swap"), (gain_cut, "swap")])
    attn_low = attn_low.reshape(plane_tok, plane_d)
    gain_two_part = jnp.where(m == 0, jnp.sum(gain_two_part[:, 0], axis=0), 0.0)
    mixed_terms = plane_terms(11, product(attn_low, outproj_plane).astype(BF16))

    def z_sum(value):
        got = lax.all_to_all(value, "shard", 0, 0, tiled=True)
        return jnp.sum(got.astype(F32), axis=0)

    outproj_grad = rows_product(attn_low, mixed_plane).astype(BF16)
    outproj_grad, single_grad = lax.optimization_barrier((outproj_grad, single_grad))
    own_outproj = z_sum(outproj_grad.reshape(ns, own_d, q_cols))

    kv_terms, query_low = attend_back(nd, mixed_terms, kv_all, queries, probs, cosine, sine_rows)
    (kv_grad,) = reduce_scatter(6, mesh_shape, False, (2 * tok, HEAD_DIM), terms=kv_terms)
    kv_grad = kv_grad.astype(F32)
    kv_low = jnp.where(m == 0, rotate(kv_grad, cosine, -sine_rows), kv_grad)
    qkv_low = jnp.concatenate([query_low, kv_low.astype(BF16)], axis=1)
    (qkv_low_plane,) = gather(7, mesh_shape, [(qkv_low, "plane")])
    qkv_low_plane = qkv_low_plane.reshape(plane_tok, q_cols + HEAD_DIM)
    hidden_one_part = cols_product(qkv_low_plane, qkv_plane).astype(BF16)
    gain_one_part = jnp.sum(hidden_one_part.astype(F32) * (tokens_plane.astype(F32) * plane_scale), axis=0)
    hidden_one_grad = from_plane(12, hidden_one_part)
    (input_grad,) = local(
        partial(last_kernel, own_d), [((tok, width), F32)],
        [hidden_one_grad, tokens_in, full_gains[:1], residual_grad], [((ROWS, width), F32)])
    gain_parts = jnp.stack([gain_one_part, gain_two_part], axis=1)
    qkv_grad = jnp.concatenate(
        [rows_product(hidden_plane, qkv_low_plane), jnp.pad(gain_parts, ((0, 0), (0, 126)))], axis=1).astype(BF16)
    qkv_grad, own_outproj = lax.optimization_barrier((qkv_grad, own_outproj))
    own_qkv = z_sum(qkv_grad.reshape(ns, own_d, -1))
    own_query = own_qkv[:, :q_cols]
    rest = own_qkv[:, q_cols:]
    rest_other = lax.ppermute(rest, "mp", [(0, 1), (1, 0)])
    kv_own, kv_other = rest[:, :HEAD_DIM], rest_other[:, :HEAD_DIM]
    own_keyval = jnp.where(
        m == 0, jnp.concatenate([kv_own, kv_other], axis=1), jnp.concatenate([kv_other, kv_own], axis=1))
    own_gains = (rest + rest_other)[:, HEAD_DIM : HEAD_DIM + 2].T

    step_value = step_count[0].astype(F32)
    bias_first = 1.0 - jnp.power(BETA_ONE, step_value)
    bias_second = 1.0 - jnp.power(BETA_TWO, step_value)
    rates = jnp.stack([1.0 / bias_first, 1.0 / bias_second])
    gateup_news, down_news = unpack_adam(
        units, rates, pair_grad, single_grad, (gateup_weight, gateup_first, gateup_second),
        (down_weight.T, down_first.T, down_second.T))
    down_news = [x.T for x in down_news]

    def adam(grad, weight, first, second, decay):
        return (grad,) + adam_step(rates, grad, weight, first, second, decay)

    news = [
        adam(own_query, query_weight, query_first, query_second, DECAY_RATE),
        adam(own_keyval, keyval_weight, keyval_first, keyval_second, DECAY_RATE),
        tuple(v.T for v in adam(own_outproj, outproj_weight.T, outproj_first.T, outproj_second.T, DECAY_RATE)),
        gateup_news,
        down_news,
        adam(own_gains, norm_gains, gains_first, gains_second, 0.0),
    ]
    return (block_out, input_grad) + tuple(x[k] for k in range(4) for x in news)


def solution(mesh):
    rows, split_q, split_o = P(TOK, None), P(TOK, "mp"), P("mp", TOK)
    params = (split_q, rows, split_o, P(TOK, None, "mp"), split_o, P(None, TOK))
    in_specs = (rows, P(TOK), rows) + params * 3 + (P(),)
    out_specs = (rows, rows) + params * 4
    return jax.shard_map(
        partial(shards, dict(mesh.shape)), mesh=mesh, in_specs=in_specs, out_specs=out_specs, check_vma=False)
```

```python
from functools import partial

import jax
import jax.numpy as jnp
from jax import lax
from jax.experimental import pallas as pl
from jax.experimental.pallas import tpu as pltpu
from jax.sharding import PartitionSpec as P

HEAD_DIM = 256
KV_BLOCKS = 8

EPS_NORM = 1e-06
BETA_ONE = 0.9
BETA_TWO = 0.95
ADAM_EPS = 1e-08
LEARN_RATE = 0.01
DECAY_RATE = 0.1
ROPE_BASE = 10000.0

MESH = pl.DeviceIdType.MESH
TOK = ("shard", "dp")
VMEM_LIMIT = 56 << 20
F32 = jnp.float32
BF16 = jnp.bfloat16


def when(cond, fn):
    if cond is True:
        fn()
    else:
        pl.when(cond)(fn)


def planes(s, ns, far_first=False):
    steps = [(s, 0, 0, True)]
    for t in range(1, ns):
        steps.append((s - t, t, 1, s - t >= 0))
        steps.append((s + t, t, -1, s + t < ns))
    return steps[::-1] if far_first else steps


def greet(ns, nd, use_z, use_plane, use_core, z_all=False):
    s, d, m = (lax.axis_index(a) for a in ("shard", "dp", "mp"))
    bar = pltpu.get_barrier_semaphore()

    def hello(dev):
        pl.semaphore_signal(bar, 1, device_id=dev, device_id_type=MESH)

    count = 0
    if use_z and z_all:
        for k in range(1, ns):
            hello({"shard": lax.rem(s + k, ns)})
        count += ns - 1
    elif use_z:
        when(s < ns - 1, lambda: hello({"shard": s + 1}))
        when(s > 0, lambda: hello({"shard": s - 1}))
        count = (s < ns - 1).astype(jnp.int32) + (s > 0).astype(jnp.int32)
    if use_plane:
        for k in range(1, nd):
            hello({"dp": lax.rem(d + k, nd)})
        count += nd - 1
    if use_core:
        hello({"mp": 1 - m})
        count += 1
    pl.semaphore_wait(bar, count)


def square(d):
    low = lax.rem(d, 2)
    x = d + 1 - 2 * low
    y = lax.rem(d + 2, 4)
    return x, y, lax.rem(x + 2, 4)


def gather_kernel(ns, nd, modes, work, n_work, *refs):
    n = len(modes)
    ins, more_in = refs[:n], refs[n : n + n_work]
    outs, more_out = refs[n + n_work : 2 * n + n_work], refs[2 * n + n_work : -7 * n]
    sems = refs[-7 * n :]
    s, d, m = (lax.axis_index(a) for a in ("shard", "dp", "mp"))
    use_z = any(k in ("z", "all") for k in modes)
    use_plane = any(k in ("plane", "all", "swap") for k in modes)
    direct = [modes[i] == "all" and ins[i].size * ins[i].dtype.itemsize < 128 << 10 for i in range(n)]
    late = [modes[i] == "z" and any(k == "all" and not q for k, q in zip(modes, direct)) for i in range(n)]
    greet(ns, nd, use_z, use_plane, "all" in modes, z_all=any(direct))
    peers = [lax.rem(d + k, nd) for k in range(1, nd)]
    relay = [
        nd == 4 and modes[i] in ("all", "plane") and ins[i].shape[0] % 32 == 0 and not direct[i] for i in range(n)]
    if nd == 4:
        x, y, across = square(d)

    def place(i, b, e, core):
        if modes[i] == "z":
            return outs[i].at[b]
        if modes[i] in ("plane", "swap"):
            return outs[i].at[e]
        return outs[i].at[b, e, core]

    def half_of(i, ref, k):
        if k is None:
            return ref
        rows = ins[i].shape[0] // 2
        return ref.at[pl.ds(k * rows, rows)]

    def zcopy(i, b, way, first):
        src = ins[i] if first else place(i, b, d, m)
        return pltpu.make_async_remote_copy(
            src, place(i, b, d, m), sems[7 * i].at[(way + 1) // 2, b], sems[7 * i + 1].at[b],
            device_id={"shard": s + way}, device_id_type=MESH)

    def pcopy(i, b, to, slot, first, e=None, k=None):
        e = d if e is None else e
        src = (ins[i].at[to] if modes[i] == "swap" else ins[i]) if first else place(i, b, e, m)
        return pltpu.make_async_remote_copy(
            half_of(i, src, k), half_of(i, place(i, b, e, m), k),
            sems[7 * i + 2].at[b, slot], sems[7 * i + 3].at[b, e, k or 0],
            device_id={"dp": to}, device_id_type=MESH)

    def precv(i, b, e, k=None):
        ref = place(i, b, e, m)
        return pltpu.make_async_remote_copy(
            half_of(i, ref, k), half_of(i, ref, k), sems[7 * i + 2].at[b, 0], sems[7 * i + 3].at[b, e, k or 0],
            device_id={"dp": peers[0]}, device_id_type=MESH)

    def own_copies(i, b, first):
        if relay[i]:
            return [pcopy(i, b, x, 0, first, k=0), pcopy(i, b, y, 1, first, k=1),
                    pcopy(i, b, x, 2, first, k=1), pcopy(i, b, y, 3, first, k=0)]
        return [pcopy(i, b, e, j, first) for j, e in enumerate(peers)]

    def pass_copies(i, b):
        return [(precv(i, b, x, 0), pcopy(i, b, y, 4, False, x, 0)),
                (precv(i, b, y, 1), pcopy(i, b, x, 5, False, y, 1))]

    def ccopy(i, b, e, first):
        src = ins[i] if first else place(i, b, e, m)
        return pltpu.make_async_remote_copy(
            src, place(i, b, e, m), sems[7 * i + 4].at[b, e], sems[7 * i + 5].at[b, e],
            device_id={"mp": 1 - m}, device_id_type=MESH)

    def crecv(i, b, e):
        ref = place(i, b, e, 1 - m)
        return pltpu.make_async_remote_copy(
            ref, ref, sems[7 * i + 4].at[b, e], sems[7 * i + 5].at[b, e],
            device_id={"mp": 1 - m}, device_id_type=MESH)

    def dcopy(i, to, block):
        return pltpu.make_async_remote_copy(
            ins[i], place(i, block, d, m), sems[7 * i].at[0, to], sems[7 * i + 1].at[block],
            device_id={"shard": to}, device_id_type=MESH)

    planes_off = [lax.rem(s + k, ns) for k in range(1, ns)]

    def bcopy(i, b, core):
        ref = outs[i].at[b, :, core]
        return pltpu.make_async_remote_copy(
            ref, ref, sems[7 * i + 4].at[b, 0], sems[7 * i + 5].at[b, 0],
            device_id={"mp": 1 - m}, device_id_type=MESH)

    def lcopy(i):
        src = ins[i].at[d] if modes[i] == "swap" else ins[i]
        return pltpu.make_async_copy(src, place(i, s, d, m), sems[7 * i + 6])

    def in_z(i):
        return modes[i] in ("z", "all") and not direct[i]

    def in_plane(i, t):
        return modes[i] == "all" or (modes[i] in ("plane", "swap") and t == 0)

    def onward(i, b, t, way):
        first = t == 0
        if in_z(i):
            if way >= 0:
                when(s < ns - 1, lambda: zcopy(i, b, 1, first).start())
            if way <= 0:
                when(s > 0, lambda: zcopy(i, b, -1, first).start())
        if in_plane(i, t):
            for c in own_copies(i, b, first):
                c.start()
        if modes[i] == "all" and not direct[i]:
            ccopy(i, b, d, first).start()
        if first and direct[i]:
            for p in planes_off:
                dcopy(i, p, s).start()
        if first:
            lcopy(i).start()

    def arrive(i, b, t, way):
        zcopy(i, b, -way, False).wait_recv()
        onward(i, b, t, way)

    def pass_on(i, b):
        for got, on in pass_copies(i, b):
            got.wait_recv()
            on.start()

    def settle(i, b, t):
        if relay[i]:
            waits = [(x, [precv(i, b, x, 1)]), (y, [precv(i, b, y, 0)]),
                     (across, [precv(i, b, across, 0), precv(i, b, across, 1)])]
        else:
            waits = [(e, [precv(i, b, e)]) for e in peers]
        for e, got in waits:
            for w in got:
                w.wait_recv()
            if modes[i] == "all" and not direct[i]:
                ccopy(i, b, e, False).start()
        if direct[i]:
            if t == 0:
                lcopy(i).wait()
            bcopy(i, b, m).start()

    def finish(i, b, t, way):
        first = t == 0
        if in_z(i):
            if way >= 0:
                when(s < ns - 1, lambda: zcopy(i, b, 1, first).wait_send())
            if way <= 0:
                when(s > 0, lambda: zcopy(i, b, -1, first).wait_send())
        if in_plane(i, t):
            for c in own_copies(i, b, first):
                c.wait_send()
            if relay[i]:
                for _, on in pass_copies(i, b):
                    on.wait_send()
        if direct[i] and first:
            for p in planes_off:
                dcopy(i, p, s).wait_send()
        if direct[i]:
            bcopy(i, b, 1 - m).wait_recv()
            bcopy(i, b, m).wait_send()
        elif modes[i] == "all":
            for e in [d] + peers:
                crecv(i, b, e).wait_recv()
                ccopy(i, b, e, False).wait_send()
        if first and not direct[i]:
            lcopy(i).wait()

    def each(steps, chosen, fn):
        for b, t, way, ok in steps:
            for i in range(n):
                if chosen(i, t):
                    when(ok, partial(fn, i, b, t, way))

    steps = planes(s, ns)
    levels = [[q for q in steps if q[1] == t] for t in range(ns)]
    straight = [(b, 1, 0, True) for b in planes_off]
    lag = max(ns - 2, 1)
    each(levels[0], lambda i, t: not late[i], onward)

    def arrive_straight(i, b, t, way):
        dcopy(i, b, b).wait_recv()
        onward(i, b, t, way)

    def part(t):
        if work is not None and t < ns:
            work(t, ns, more_in, more_out)

    part(0)
    each(straight, lambda i, t: direct[i], arrive_straight)
    for t in range(1, ns + lag):
        if t < ns:
            each(levels[t], lambda i, t: in_z(i) and not late[i], arrive)
        if t == lag:
            each(levels[0], lambda i, t: late[i], onward)
        part(t)
        if t <= ns:
            each(levels[t - 1], lambda i, t: relay[i] and in_plane(i, t), lambda i, b, t, way: pass_on(i, b))
        if 1 <= t - lag:
            each(levels[t - lag], lambda i, t: late[i], arrive)
    each(steps, lambda i, t: in_plane(i, t) and not direct[i], lambda i, b, t, way: settle(i, b, t))
    each(levels[0] + straight, lambda i, t: direct[i], lambda i, b, t, way: settle(i, b, t))
    each(steps, lambda i, t: (t == 0 or in_z(i)) and not direct[i], finish)
    each(levels[0] + straight, lambda i, t: direct[i], finish)


def gather(collective, mesh_shape, items, work=None, work_args=(), work_outs=()):
    ns, nd = mesh_shape["shard"], mesh_shape["dp"]
    modes = tuple(mode for _, mode in items)
    lead = {"z": (ns,), "plane": (nd,), "all": (ns, nd, 2), "swap": ()}
    shapes = [jax.ShapeDtypeStruct(lead[mode] + a.shape, a.dtype) for a, mode in items]
    sems = []
    dma = pltpu.SemaphoreType.DMA
    for _ in items:
        sems += [dma((2, ns)), dma((ns,)), dma((ns, max(nd, 6))), dma((ns, nd, 2)), dma((ns, nd)), dma((ns, nd)),
                 dma(())]
    return pl.pallas_call(
        partial(gather_kernel, ns, nd, modes, work, len(work_args)),
        out_shape=shapes + list(work_outs),
        in_specs=[pl.BlockSpec(memory_space=pl.ANY)] * len(items)
        + [pl.BlockSpec(memory_space=pltpu.VMEM)] * len(work_args),
        out_specs=[pl.BlockSpec(memory_space=pl.ANY)] * len(items)
        + [pl.BlockSpec(memory_space=pltpu.VMEM)] * len(work_outs),
        scratch_shapes=sems,
        compiler_params=pltpu.CompilerParams(
            collective_id=collective, has_side_effects=True, vmem_limit_bytes=VMEM_LIMIT),
        cost_estimate=pl.CostEstimate(flops=0, bytes_accessed=1 << 20, transcendentals=0),
    )(*[a for a, _ in items], *work_args)


def reduce_kernel(ns, nd, share, count, made, *refs):
    n_in = 2 * count if made else 1
    ins, outs, scratch = refs[:n_in], refs[n_in : n_in + count], refs[n_in + count :]
    own, sib, give, got, mid, zgot, fin, lsem, ss, sr, ps, pr, zs, zr, fs, fr, ks = scratch
    s, d, m = (lax.axis_index(a) for a in ("shard", "dp", "mp"))
    h, c = fin.shape[1:]
    tile = 16
    greet(ns, nd, True, True, True, z_all=True)
    peers = [lax.rem(d + k, nd) for k in range(1, nd)]
    relay = nd == 4 and h % 32 == 0
    if relay:
        x, y, across = square(d)
        peers = [across, x, y]
    chain = bool(made)
    if chain:
        order = []
        for k in range(ns - 1):
            up = jnp.where(k < ns - 1 - s, ns - 1 - k, k - (ns - 1 - s))
            down = jnp.where(k < s, k, ns - 1 - (k - s))
            order.append(jnp.where(2 * s < ns, up, down))
        order.append(s)
    else:
        order = [lax.rem(s + k, ns) for k in sorted(range(1, ns), key=lambda k: abs(k - ns // 2))] + [s]
    items = [(a, k, order[k]) for k in range(ns) for a in range(count)]

    def score(a, k, b):
        src = give.at[a, k % 2] if made else ins[0].at[b, :, 1 - m]
        return pltpu.make_async_remote_copy(
            src, sib.at[a, b], ss.at[a, b], sr.at[a, b], device_id={"mp": 1 - m}, device_id_type=MESH)

    def load(a, b):
        return pltpu.make_async_copy(ins[0].at[b, :, m], own.at[a, b], lsem.at[a, b])

    def multiply(a, b, core, store):
        step = 512 if c % 512 == 0 else 128
        left = ins[a][b, :, core].reshape(nd * h, ins[a].shape[-1])

        @pl.loop(0, c // step)
        def _(j):
            cols = pl.ds(pl.multiple_of(j * step, step), step)
            term = cols_product(left, ins[count + a][cols])
            store(cols, term.astype(BF16).reshape(nd, h, step))

    def zero(a, k, b):
        if not made:
            score(a, k, b).start()
            load(a, b).start()
            return
        if k >= 2:
            score(a, k - 2, order[k - 2]).wait_send()

        def to_give(cols, v):
            give[a, k % 2, :, :, cols] = v

        def to_own(cols, v):
            own[a, b, :, :, cols] = v

        multiply(a, b, 1 - m, to_give)
        score(a, k, b).start()
        multiply(a, b, m, to_own)

    def pcopy(a, b, src, dst, slot, to):
        return pltpu.make_async_remote_copy(
            src, dst, ps.at[a, b, slot], pr.at[a, b, slot], device_id={"dp": to}, device_id_type=MESH)

    def sends(a, b):
        if not relay:
            return [pltpu.make_async_remote_copy(
                own.at[a, b, e], got.at[a, b, d], ps.at[a, b, e], pr.at[a, b, d],
                device_id={"dp": e}, device_id_type=MESH) for e in peers]
        half = h // 2
        first, last = pl.ds(0, half), pl.ds(half, half)
        return [
            pcopy(a, b, own.at[a, b, across, first], got.at[a, b, 0, first], 0, x),
            pcopy(a, b, own.at[a, b, across, last], got.at[a, b, 0, last], 1, y),
            pcopy(a, b, own.at[a, b, x], got.at[a, b, 1], 2, x),
            pcopy(a, b, own.at[a, b, y], got.at[a, b, 2], 3, y),
        ]

    def zcopy(a, b, to):
        return pltpu.make_async_remote_copy(
            mid.at[a, b], zgot.at[a, to], zs.at[a, b], zr.at[a, to], device_id={"shard": b}, device_id_type=MESH)

    def sum_rows(lo, hi, terms, store):
        @pl.loop(lo // tile, hi // tile)
        def _(r):
            at = pl.ds(pl.multiple_of(r * tile, tile), tile)
            v = terms[0](at).astype(F32)
            for f in terms[1:]:
                v = v + f(at).astype(F32)
            store(at, v.astype(BF16))

    def to_own(a, b, e):
        def store(at, v):
            own[a, b, e, at] = v
        return store

    def one(a, k, b):
        score(a, k, b).wait_recv()
        if not made:
            load(a, b).wait()
        out_now = sends(a, b)
        for j, e in enumerate(peers + [d]):
            sum_rows(0, h, [lambda at, e=e: own[a, b, e, at], lambda at, e=e: sib[a, b, e, at]], to_own(a, b, e))
            if relay and j == 0:
                out_now[0].start()
                out_now[1].start()
            elif not relay and j < len(peers):
                out_now[j].start()

    def two(a, k, b):
        if not relay:
            return
        half = h // 2
        c0, c1, c2, c3 = sends(a, b)
        c0.wait_recv()
        sum_rows(0, half, [lambda at: own[a, b, y, at], lambda at: got[a, b, 0, at]], to_own(a, b, y))
        c3.start()
        c1.wait_recv()
        sum_rows(half, h, [lambda at: own[a, b, x, at], lambda at: got[a, b, 0, at]], to_own(a, b, x))
        c2.start()

    def plane_terms(a, b):
        slots = [1, 2] if relay else peers
        return [lambda at: own[a, b, d, at]] + [lambda at, e=e: got[a, b, e, at] for e in slots]

    def three(a, k, b):
        if relay:
            for w in sends(a, b)[2:]:
                w.wait_recv()
        else:
            for e in peers:
                pltpu.make_async_remote_copy(
                    own.at[a, b, e], got.at[a, b, e], ps.at[a, b, e], pr.at[a, b, e],
                    device_id={"dp": e}, device_id_type=MESH).wait_recv()
        if k < ns - 1:
            def store(at, v):
                mid[a, b, at] = v
            sum_rows(0, h, plane_terms(a, b), store)
            if not chain:
                zcopy(a, b, s).start()

    def hop(a, b, way):
        slot = jnp.where(s + way == b, jnp.where(way > 0, b, ns), b)
        return pltpu.make_async_remote_copy(
            mid.at[a, b], zgot.at[a, slot], zs.at[a, b], zr.at[a, slot],
            device_id={"shard": s + way}, device_id_type=MESH)

    def came(a, slot):
        return pltpu.make_async_remote_copy(
            mid.at[a, s], zgot.at[a, slot], zs.at[a, s], zr.at[a, slot], device_id={"mp": 1 - m},
            device_id_type=MESH)

    def four(a, k, b):
        if k == ns - 1:
            return

        def add():
            came(a, b).wait_recv()

            def store(at, v):
                mid[a, b, at] = v
            sum_rows(0, h, [lambda at: mid[a, b, at], lambda at: zgot[a, b, at]], store)

        upward = b > s
        pl.when(jnp.where(upward, s > 0, s < ns - 1))(add)
        pl.when(upward)(lambda: hop(a, b, 1).start())
        pl.when(jnp.logical_not(upward))(lambda: hop(a, b, -1).start())

    stages = [zero, one, two, three] + ([four] if chain else [])
    if not made:
        for item in items:
            zero(*item)
        stages = stages[1:]
    for t in range(len(items) + len(stages) - 1):
        for j, stage in enumerate(stages):
            if 0 <= t - j < len(items):
                stage(*items[t - j])

    def give_out(a, core):
        return pltpu.make_async_remote_copy(
            fin.at[a], outs[a].at[core], fs.at[a], fr.at[a], device_id={"mp": 1 - m}, device_id_type=MESH)

    def keep(a):
        return pltpu.make_async_copy(fin.at[a], outs[a].at[m] if share else outs[a], ks.at[a])

    others = order[:-1]
    for a in range(count):
        def store(at, v, a=a):
            fin[a, at] = v

        if chain:
            sum_rows(0, h, plane_terms(a, s), store)
            for slot, ok in ((s, s > 0), (ns, s < ns - 1)):

                def add(slot=slot):
                    came(a, slot).wait_recv()
                    sum_rows(0, h, [lambda at: fin[a, at], lambda at: zgot[a, slot, at]], store)

                pl.when(ok)(add)
        else:
            for b in others:
                zcopy(a, b, b).wait_recv()
            sum_rows(0, h, plane_terms(a, s) + [lambda at, b=b: zgot[a, b, at] for b in others], store)
        if share:
            give_out(a, m).start()
        keep(a).start()
    for a in range(count):
        if share:
            give_out(a, 1 - m).wait_recv()
            give_out(a, m).wait_send()
        keep(a).wait()
        for k, b in enumerate(order):
            if not made or k >= ns - 2:
                score(a, k, b).wait_send()
            for w in sends(a, b):
                w.wait_send()
        for b in others:
            zcopy(a, b, s).wait_send()


def reduce_scatter(collective, mesh_shape, share, blocks, terms=None, factors=None):
    ns, nd = mesh_shape["shard"], mesh_shape["dp"]
    rows, c = blocks
    h = rows // 2
    count = len(factors) if factors else 1
    size = ns * nd * h * c * 2
    if size * count * 3 > (40 << 20):
        whole = [terms] if factors is None else [
            cols_product(x, w).astype(BF16) for x, w in factors]
        sums = []
        for p in whole:
            total = lax.psum_scatter(p.reshape(ns * nd, 2, h, c), TOK, scatter_dimension=0, tiled=True)[0]
            total = lax.psum(total, "mp")
            sums.append(total if share else lax.dynamic_index_in_dim(total, lax.axis_index("mp"), 0, False))
        return sums
    if factors is None:
        made = False
        args = [terms.reshape(ns, nd, 2, h, c)]
        in_specs = [pl.BlockSpec(memory_space=pl.ANY)]
        give = (1, 1, 1, 16, 128)
    else:
        made = True
        args = [x.reshape(ns, nd, 2, h, -1) for x, _ in factors] + [w for _, w in factors]
        in_specs = [pl.BlockSpec(memory_space=pltpu.VMEM)] * (2 * count)
        give = (count, 2, nd, h, c)
    slots = 3 if nd == 4 and h % 32 == 0 else nd
    dma = pltpu.SemaphoreType.DMA
    return pl.pallas_call(
        partial(reduce_kernel, ns, nd, share, count, made),
        out_shape=[jax.ShapeDtypeStruct((2, h, c) if share else (h, c), BF16)] * count,
        in_specs=in_specs,
        out_specs=[pl.BlockSpec(memory_space=pl.ANY)] * count,
        scratch_shapes=[
            pltpu.VMEM((count, ns, nd, h, c), BF16),
            pltpu.VMEM((count, ns, nd, h, c), BF16),
            pltpu.VMEM(give, BF16),
            pltpu.VMEM((count, ns, slots, h, c), BF16),
            pltpu.VMEM((count, ns, h, c), BF16),
            pltpu.VMEM((count, ns + 1, h, c), BF16),
            pltpu.VMEM((count, h, c), BF16),
            dma((count, ns)), dma((count, ns)), dma((count, ns)),
            dma((count, ns, max(nd, 4))), dma((count, ns, max(nd, 4))),
            dma((count, ns)), dma((count, ns + 1)), dma((count,)), dma((count,)), dma((count,)),
        ],
        compiler_params=pltpu.CompilerParams(
            collective_id=collective, has_side_effects=True, vmem_limit_bytes=VMEM_LIMIT),
        cost_estimate=pl.CostEstimate(flops=0, bytes_accessed=1 << 20, transcendentals=0),
    )(*args)


def gelu_both(v):
    root, cube = 0.7978845608028654, 0.044715
    t = jnp.tanh(root * (v + cube * v * v * v))
    slope = 0.5 * (1.0 + t) + 0.5 * v * (1.0 - t * t) * (root * (1.0 + 3.0 * cube * v * v))
    return 0.5 * v * (1.0 + t), slope


def feed_kernel(ns, nd, x, cot, wide, thin, act, low, wide_grad, thin_grad, hid, cots, acc, more, zs, zr, ps, pr, cs, cr,
                ls, ks):
    s, d, m = (lax.axis_index(a) for a in ("shard", "dp", "mp"))
    h, width = x.shape
    units = thin.shape[1]
    relay = nd == 4 and h % 32 == 0
    greet(ns, nd, True, True, True, z_all=True)
    turns = [0] + sorted(range(1, ns), key=lambda k: min(k, ns - k))
    order = [lax.rem(s + k, ns) for k in turns]
    peers = [lax.rem(d + k, nd) for k in range(1, nd)]
    if relay:
        xn, yn, across = square(d)
        peers = [xn, yn, across]

    def zsend(b):
        return pltpu.make_async_remote_copy(
            x, hid.at[s, d, m], zs.at[b], zr.at[s], device_id={"shard": b}, device_id_type=MESH)

    def zrecv(b):
        return pltpu.make_async_remote_copy(
            x, hid.at[b, d, m], zs.at[b], zr.at[b], device_id={"shard": b}, device_id_type=MESH)

    def part(ref, k):
        return ref if k is None else ref.at[pl.ds(k * (h // 2), h // 2)]

    def source(b, e, first):
        return x if first else hid.at[b, e, m]

    def psend(b, e, to, slot, k, first):
        return pltpu.make_async_remote_copy(
            part(source(b, e, first), k), part(hid.at[b, e, m], k), ps.at[b, slot], pr.at[b, e, k or 0],
            device_id={"dp": to}, device_id_type=MESH)

    def precv(b, e, k):
        ref = part(hid.at[b, e, m], k)
        return pltpu.make_async_remote_copy(
            ref, ref, ps.at[b, 0], pr.at[b, e, k or 0], device_id={"dp": peers[0]}, device_id_type=MESH)

    def own_sends(b, first):
        if relay:
            return [psend(b, d, xn, 0, 0, first), psend(b, d, yn, 1, 1, first),
                    psend(b, d, xn, 2, 1, first), psend(b, d, yn, 3, 0, first)]
        return [psend(b, d, e, j, None, first) for j, e in enumerate(peers)]

    def pass_sends(b):
        if relay:
            return [(precv(b, xn, 0), psend(b, xn, yn, 4, 0, False)),
                    (precv(b, yn, 1), psend(b, yn, xn, 5, 1, False))]
        return []

    def share(b, e, core, first=False):
        ref = hid.at[b, e, core]
        return pltpu.make_async_remote_copy(
            x if first else ref, ref, cs.at[b, e], cr.at[b, e], device_id={"mp": 1 - m}, device_id_type=MESH)

    def load(b):
        return pltpu.make_async_copy(cot.at[b], cots.at[b], ls.at[b])

    def begin(k):
        b = order[k]
        if k > 0:
            zrecv(b).wait_recv()
        for c in own_sends(b, k == 0):
            c.start()
        share(b, d, m, k == 0).start()

    def hand_on(k):
        for got, on in pass_sends(order[k]):
            got.wait_recv()
            on.start()

    def settle(k):
        b = order[k]
        for e in peers:
            for q in waits(e):
                precv(b, e, q).wait_recv()
            share(b, e, m).start()

    def waits(e):
        if not relay:
            return [None]
        return [1] if e is xn else [0] if e is yn else [0, 1]

    def ready(k):
        b = order[k]
        for e in [d] + peers:
            share(b, e, 1 - m).wait_recv()
        if k == 0:
            keep.wait()
        load(b).wait()

    count = nd // 2 if nd % 2 == 0 else nd

    def forward(k, q):
        b = order[k]
        at = pl.ds(q * count, count)
        rows = count * 2 * h
        pre = product(hid[b, at].reshape(rows, width), wide[...])
        back = product(cots[b, at].reshape(rows, width), thin[...])
        value, slope = gelu_both(pre[:, :units])
        up = pre[:, units:]
        act[b, at] = (value * up).astype(BF16).reshape(count, 2, h, units)
        low[b, at, :, :, :units] = (back * up * slope).astype(BF16).reshape(count, 2, h, units)
        low[b, at, :, :, units:] = (back * value).astype(BF16).reshape(count, 2, h, units)

    def backward(k):
        b = order[k]
        rows = nd * 2 * h
        step = 512 if width % 512 == 0 else 128
        lows = low[b].reshape(rows, 2 * units)
        acts = act[b].reshape(rows, units)

        @pl.loop(0, width // step)
        def _(j):
            at = pl.ds(pl.multiple_of(j * step, step), step)
            one = rows_product(hid[b, :, :, :, at].reshape(rows, step), lows)
            two = rows_product(cots[b, :, :, :, at].reshape(rows, step), acts)
            if k > 0:
                one = one + acc[at]
                two = two + more[at]
            if k < ns - 1:
                acc[at] = one
                more[at] = two
            else:
                wide_grad[at] = one.astype(BF16)
                thin_grad[at] = two.astype(BF16)

    for b in order[1:]:
        zsend(b).start()
    keep = pltpu.make_async_copy(x, hid.at[s, d, m], ks)
    keep.start()
    begin(0)
    for b in order:
        load(b).start()
    hand_on(0)
    if ns > 1:
        begin(1)
        hand_on(1)
    for k in range(ns):
        settle(k)
        ready(k)
        forward(k, 0)
        if count < nd:
            forward(k, 1)
        if k + 2 < ns:
            begin(k + 2)
        backward(k)
        if k + 2 < ns:
            hand_on(k + 2)
    for k, b in enumerate(order):
        for c in own_sends(b, k == 0):
            c.wait_send()
        for _, c in pass_sends(b):
            c.wait_send()
        for e in [d] + peers:
            share(b, e, m).wait_send()
        if k > 0:
            zsend(b).wait_send()


def feed(collective, mesh_shape, x, cot, wide, thin):
    ns, nd = mesh_shape["shard"], mesh_shape["dp"]
    h, width = x.shape
    units = thin.shape[1]
    rows = (ns, nd, 2, h)
    if 2 * cot.size * 2 > (24 << 20):
        (hid,) = gather(collective, mesh_shape, [(x, "all")])
        hid, cot = hid.reshape(-1, width), cot.reshape(-1, width)
        pre = product(hid, wide)
        back = product(cot, thin)
        value, slope = gelu_both(pre[:, :units])
        up = pre[:, units:]
        act = (value * up).astype(BF16)
        low = jnp.concatenate([back * up * slope, back * value], axis=1).astype(BF16)
        return act, low, rows_product(hid, low).astype(BF16), rows_product(cot, act).astype(BF16)
    dma = pltpu.SemaphoreType.DMA
    vmem = pl.BlockSpec(memory_space=pltpu.VMEM)
    act, low, wide_grad, thin_grad = pl.pallas_call(
        partial(feed_kernel, ns, nd),
        out_shape=[
            jax.ShapeDtypeStruct(rows + (units,), BF16),
            jax.ShapeDtypeStruct(rows + (2 * units,), BF16),
            jax.ShapeDtypeStruct((width, 2 * units), BF16),
            jax.ShapeDtypeStruct((width, units), BF16),
        ],
        in_specs=[vmem, pl.BlockSpec(memory_space=pl.ANY), vmem, vmem],
        out_specs=[vmem] * 4,
        scratch_shapes=[
            pltpu.VMEM(rows + (width,), BF16),
            pltpu.VMEM(rows + (width,), BF16),
            pltpu.VMEM((width, 2 * units), F32),
            pltpu.VMEM((width, units), F32),
            dma((ns,)), dma((ns,)), dma((ns, max(nd, 6))), dma((ns, nd, 2)), dma((ns, nd)), dma((ns, nd)),
            dma((ns,)), dma(()),
        ],
        compiler_params=pltpu.CompilerParams(
            collective_id=collective, has_side_effects=True, vmem_limit_bytes=VMEM_LIMIT),
        cost_estimate=pl.CostEstimate(flops=0, bytes_accessed=1 << 20, transcendentals=0),
    )(x, cot, wide, thin)
    return act.reshape(-1, units), low.reshape(-1, 2 * units), wide_grad, thin_grad


def plane_kernel(ns, nd, p, out, own, sib, ls, ss, sr, ps, pr, fs, fr, ks):
    d, m = lax.axis_index("dp"), lax.axis_index("mp")
    h, c = own.shape[1:]
    tile = 16
    greet(ns, nd, False, True, True)
    peers = [lax.rem(d + k, nd) for k in range(1, nd)]
    order = ([square(d)[2], square(d)[0], square(d)[1]] if nd == 4 else peers) + [d]
    other = {"mp": 1 - m}

    def score(e):
        return pltpu.make_async_remote_copy(
            p.at[e, 1 - m], sib.at[e], ss.at[e], sr.at[e], device_id=other, device_id_type=MESH)

    def load(e):
        return pltpu.make_async_copy(p.at[e, m], own.at[e], ls.at[e])

    def send(e, block):
        return pltpu.make_async_remote_copy(
            own.at[e], out.at[block, m], ps.at[e], pr.at[block], device_id={"dp": e}, device_id_type=MESH)

    def share(e, core):
        src = own.at[d] if e is d else out.at[e, m]
        return pltpu.make_async_remote_copy(
            src, out.at[e, core], fs.at[e], fr.at[e], device_id=other, device_id_type=MESH)

    for e in order:
        score(e).start()
        load(e).start()
    for e in order:
        score(e).wait_recv()
        load(e).wait()

        @pl.loop(0, h // tile)
        def _(r, e=e):
            at = pl.ds(pl.multiple_of(r * tile, tile), tile)
            own[e, at] = (own[e, at].astype(F32) + sib[e, at].astype(F32)).astype(BF16)

        if e is not d:
            send(e, d).start()
    keep = pltpu.make_async_copy(own.at[d], out.at[d, m], ks)
    keep.start()
    share(d, m).start()
    for e in order[:-1]:
        send(e, e).wait_recv()
        share(e, m).start()
    keep.wait()
    for e in order:
        share(e, 1 - m).wait_recv()
        share(e, m).wait_send()
        score(e).wait_send()
        if e is not d:
            send(e, d).wait_send()


def plane_reduce(collective, mesh_shape, p):
    ns, nd = mesh_shape["shard"], mesh_shape["dp"]
    h, c = p.shape[2:]
    dma = pltpu.SemaphoreType.DMA
    return pl.pallas_call(
        partial(plane_kernel, ns, nd),
        out_shape=jax.ShapeDtypeStruct(p.shape, BF16),
        in_specs=[pl.BlockSpec(memory_space=pl.ANY)],
        out_specs=pl.BlockSpec(memory_space=pl.ANY),
        scratch_shapes=[pltpu.VMEM((nd, h, c), BF16)] * 2 + [dma((nd,))] * 7 + [dma(())],
        compiler_params=pltpu.CompilerParams(
            collective_id=collective, has_side_effects=True, vmem_limit_bytes=VMEM_LIMIT),
        cost_estimate=pl.CostEstimate(flops=0, bytes_accessed=1 << 20, transcendentals=0),
    )(p)


def rope_tables(positions):
    half_dim = HEAD_DIM // 2
    exponent = jnp.arange(half_dim, dtype=F32) * (-2.0 / HEAD_DIM)
    angles = positions.astype(F32)[:, None] * jnp.power(ROPE_BASE, exponent)[None, :]
    return (jnp.cos(angles), jnp.sin(angles))


def rotate(values, cosine, sine_rows):
    half_dim = values.shape[-1] // 2
    front_half = values[..., :half_dim]
    back_half = values[..., half_dim:]
    return jnp.concatenate(
        [front_half * cosine - back_half * sine_rows, back_half * cosine + front_half * sine_rows], axis=-1)


def rows_product(left_side, right_side):
    return lax.dot_general(
        left_side, right_side, (((0,), (0,)), ((), ())), preferred_element_type=F32)


def cols_product(left_side, right_side):
    return lax.dot_general(
        left_side, right_side, (((1,), (1,)), ((), ())), preferred_element_type=F32)


def product(left_side, right_side):
    return jnp.dot(left_side, right_side, preferred_element_type=F32)


def turn(v, cosine, sine):
    half_dim = HEAD_DIM // 2
    front, back = v[:, :half_dim], v[:, half_dim:]
    return front * cosine - back * sine, back * cosine + front * sine


def window(nd, kv, keys, values):
    me = lax.axis_index("shard") * nd + lax.axis_index("dp")
    tok = kv.shape[2]
    for j in range(KV_BLOCKS + 1):
        b = jnp.maximum(me + (j - KV_BLOCKS), 0)
        keys[j * tok : (j + 1) * tok] = kv[b, 0]
        values[j * tok : (j + 1) * tok] = kv[b, 1]


def attend_kernel(nd, got, kv, allowed, cosine, sine, mixed, queries, probs, keys, values):
    window(nd, kv, keys, values)
    scale = HEAD_DIM ** (-0.5)
    half_dim = HEAD_DIM // 2
    cos, sin = cosine[...], sine[...]
    for h in range(probs.shape[0]):
        at = h * HEAD_DIM
        raw = got[0, :, at : at + HEAD_DIM].astype(F32)
        for e in range(1, got.shape[0]):
            raw = raw + got[e, :, at : at + HEAD_DIM].astype(F32)
        front, back = turn(raw, cos, sin)
        queries[:, at : at + half_dim] = front.astype(BF16)
        queries[:, at + half_dim : at + HEAD_DIM] = back.astype(BF16)
        scores = cols_product(queries[:, at : at + HEAD_DIM], keys[...]) * scale
        scores = jnp.where(allowed[...] > 0.0, scores, -jnp.inf)
        raised = jnp.exp(scores - jnp.max(scores, axis=1, keepdims=True))
        prob = raised / jnp.sum(raised, axis=1, keepdims=True)
        probs[h] = prob
        mixed[:, at : at + HEAD_DIM] = product(prob.astype(BF16), values[...]).astype(BF16)


def attend(nd, heads, got, kv, allowed, cosine, sine):
    tok = got.shape[1]
    span = allowed.shape[1]
    return pl.pallas_call(
        partial(attend_kernel, nd),
        out_shape=[
            jax.ShapeDtypeStruct((tok, heads * HEAD_DIM), BF16),
            jax.ShapeDtypeStruct((tok, heads * HEAD_DIM), BF16),
            jax.ShapeDtypeStruct((heads, tok, span), F32),
        ],
        in_specs=[pl.BlockSpec(memory_space=pltpu.VMEM)] * 5,
        out_specs=[pl.BlockSpec(memory_space=pltpu.VMEM)] * 3,
        scratch_shapes=[pltpu.VMEM((span, HEAD_DIM), BF16)] * 2,
        compiler_params=pltpu.CompilerParams(vmem_limit_bytes=VMEM_LIMIT),
    )(got, kv, allowed, cosine, sine)


def attend_back_kernel(nd, got, kv, queries, probs, cosine, sine, kv_grad, low, keys, values, key_sum, value_sum):
    window(nd, kv, keys, values)
    me = lax.axis_index("shard") * nd + lax.axis_index("dp")
    scale = HEAD_DIM ** (-0.5)
    half_dim = HEAD_DIM // 2
    n, _, tok, _ = kv.shape
    cos, sin = cosine[...], sine[...]
    for h in range(probs.shape[0]):
        at = h * HEAD_DIM
        raw = got[0, :, at : at + HEAD_DIM].astype(F32)
        for e in range(1, got.shape[0]):
            raw = raw + got[e, :, at : at + HEAD_DIM].astype(F32)
        mixed_grad = raw.astype(BF16)
        prob = probs[h]
        prob_grad = cols_product(mixed_grad, values[...])
        inner = jnp.sum(prob * prob_grad, axis=1, keepdims=True)
        scores_low = (prob * (prob_grad - inner) * scale).astype(BF16)
        front, back = turn(product(scores_low, keys[...]), cos, -sin)
        low[:, at : at + half_dim] = front.astype(BF16)
        low[:, at + half_dim : at + HEAD_DIM] = back.astype(BF16)
        key_part = rows_product(scores_low, queries[:, at : at + HEAD_DIM])
        value_part = rows_product(prob.astype(BF16), mixed_grad)
        if h == 0:
            key_sum[...] = key_part
            value_sum[...] = value_part
        else:
            key_sum[...] += key_part
            value_sum[...] += value_part

    @pl.loop(0, n)
    def _(b):
        kv_grad[b] = jnp.zeros(kv_grad.shape[1:], BF16)

    for j in range(KV_BLOCKS + 1):
        b = me + (j - KV_BLOCKS)

        @pl.when(b >= 0)
        def _(j=j, b=b):
            kv_grad[b, 0] = key_sum[j * tok : (j + 1) * tok].astype(BF16)
            kv_grad[b, 1] = value_sum[j * tok : (j + 1) * tok].astype(BF16)


def attend_back(nd, got, kv, queries, probs, cosine, sine):
    span = probs.shape[2]
    return pl.pallas_call(
        partial(attend_back_kernel, nd),
        out_shape=[jax.ShapeDtypeStruct(kv.shape, BF16), jax.ShapeDtypeStruct(queries.shape, BF16)],
        in_specs=[pl.BlockSpec(memory_space=pltpu.VMEM)] * 6,
        out_specs=[pl.BlockSpec(memory_space=pltpu.VMEM)] * 2,
        scratch_shapes=[pltpu.VMEM((span, HEAD_DIM), BF16)] * 2 + [pltpu.VMEM((span, HEAD_DIM), F32)] * 2,
        compiler_params=pltpu.CompilerParams(vmem_limit_bytes=VMEM_LIMIT),
    )(got, kv, queries, probs, cosine, sine)


ROWS = 16


def row_tiles(count, body):
    @pl.loop(0, count // ROWS)
    def _(r):
        body(pl.ds(pl.multiple_of(r * ROWS, ROWS), ROWS))


def pieces(nd, width, plane_d, own_d):
    for j in range(width // own_d):
        yield j * own_d, j % nd, (j // nd) * own_d


def inverse_of(rows):
    return lax.rsqrt(jnp.mean(rows * rows, axis=1, keepdims=True) + EPS_NORM)


def norm_back(rows, gain, grad):
    inverse = inverse_of(rows)
    normed = rows * inverse
    scaled = grad * gain
    inner = jnp.mean(normed * scaled, axis=1, keepdims=True)
    return inverse * (scaled - normed * inner), grad * normed


def join_kernel(own_d, got, tokens, gain, residual, hidden):
    nd, tok, plane_d = got.shape
    half = hidden.shape[0]
    first = lax.axis_index("mp") * half

    def add(at):
        for c, e, p in pieces(nd, tokens.shape[1], plane_d, own_d):
            residual[at, c : c + own_d] = (
                got[e, at, p : p + own_d].astype(F32) + tokens[at, c : c + own_d].astype(F32))

    row_tiles(tok, add)

    @pl.loop(0, half // ROWS)
    def _(r):
        rows = residual[pl.ds(pl.multiple_of(first + r * ROWS, ROWS), ROWS)]
        at = pl.ds(pl.multiple_of(r * ROWS, ROWS), ROWS)
        hidden[at] = (rows * inverse_of(rows) * gain[...]).astype(BF16)


def split_kernel(own_d, grad, ffn, residual, gain, cot, block_out, residual_grad, cut, gain_cut, total):
    nd, tok, plane_d = cut.shape
    total[...] = jnp.zeros_like(total)

    def body(at):
        rows = residual[at]
        block_out[at] = (rows + ffn[at].astype(F32)).astype(BF16)
        back, terms = norm_back(rows, gain[...], grad[at].astype(F32))
        total[...] += terms
        value = cot[at].astype(F32) + back
        residual_grad[at] = value
        for c, e, p in pieces(nd, grad.shape[1], plane_d, own_d):
            cut[e, at, p : p + own_d] = value[:, c : c + own_d].astype(BF16)

    row_tiles(tok, body)
    gain_cut[...] = jnp.zeros_like(gain_cut)
    sums = jnp.sum(total[...], axis=0, keepdims=True)
    for c, e, p in pieces(nd, grad.shape[1], plane_d, own_d):
        gain_cut[e, 0:1, p : p + own_d] = sums[:, c : c + own_d]


def last_kernel(own_d, got, tokens, gain, residual_grad, out, grad):
    nd, tok, plane_d = got.shape

    def body(at):
        for c, e, p in pieces(nd, tokens.shape[1], plane_d, own_d):
            grad[:, c : c + own_d] = got[e, at, p : p + own_d].astype(F32)
        back, _ = norm_back(tokens[at].astype(F32), gain[...], grad[...])
        out[at] = residual_grad[at] + back

    row_tiles(tok, body)


def local(kernel, outs, args, scratch=()):
    return pl.pallas_call(
        kernel,
        out_shape=[jax.ShapeDtypeStruct(shape, dtype) for shape, dtype in outs],
        in_specs=[pl.BlockSpec(memory_space=pltpu.VMEM)] * len(args),
        out_specs=[pl.BlockSpec(memory_space=pltpu.VMEM)] * len(outs),
        scratch_shapes=[pltpu.VMEM(shape, dtype) for shape, dtype in scratch],
        compiler_params=pltpu.CompilerParams(vmem_limit_bytes=VMEM_LIMIT),
    )(*args)


def pack(part, parts, ins, outs):
    gateup, down = ins
    pair, single = outs
    n, _, units = single.shape
    full = down.shape[1] // units
    share = -(-n // parts)
    for j in range(part * share, min((part + 1) * share, n)):
        if j >= full:
            pair[j] = jnp.zeros(pair.shape[1:], BF16)
            single[j] = jnp.zeros(single.shape[1:], BF16)
            continue
        at = pl.ds(j * units, units)
        pair[j, :, :units] = gateup[:, 0, at]
        pair[j, :, units:] = gateup[:, 1, at]
        single[j] = down[:, at]


def adam_step(rates, grad, weight, first, second, decay):
    first_new = BETA_ONE * first + (1.0 - BETA_ONE) * grad
    second_new = BETA_TWO * second + (1.0 - BETA_TWO) * grad * grad
    direction = first_new * rates[0] / (jnp.sqrt(second_new * rates[1]) + ADAM_EPS)
    return first_new, second_new, -LEARN_RATE * (direction + decay * weight.astype(F32))


def unpack_kernel(rates, pair_got, got, gw, gf, gs, dw, df, ds, gg, gfn, gsn, gu, dg, dfn, dsn, du):
    units = dw.shape[1]
    pair = (rates[0], rates[1])
    for k in range(2):
        grad = pair_got[0, :, k * units : (k + 1) * units].astype(F32)
        gg[:, k, :] = grad
        gfn[:, k, :], gsn[:, k, :], gu[:, k, :] = adam_step(
            pair, grad, gw[:, k, :], gf[:, k, :], gs[:, k, :], DECAY_RATE)
    grad = got[0].astype(F32)
    dg[...] = grad
    dfn[...], dsn[...], du[...] = adam_step(pair, grad, dw[...], df[...], ds[...], DECAY_RATE)


def unpack_adam(units, rates, pair_got, got, gateup, down):
    own_d, _, ff_local = gateup[0].shape
    three = pl.BlockSpec((own_d, 2, units), lambda j: (0, 0, j))
    two = pl.BlockSpec((own_d, units), lambda j: (0, j))
    shape3 = jax.ShapeDtypeStruct(gateup[0].shape, F32)
    shape2 = jax.ShapeDtypeStruct(down[0].shape, F32)
    out = pl.pallas_call(
        unpack_kernel,
        out_shape=[shape3] * 4 + [shape2] * 4,
        grid=(ff_local // units,),
        in_specs=[
            pl.BlockSpec(memory_space=pltpu.SMEM),
            pl.BlockSpec((1, own_d, 2 * units), lambda j: (j, 0, 0)),
            pl.BlockSpec((1, own_d, units), lambda j: (j, 0, 0)),
        ] + [three] * 3 + [two] * 3,
        out_specs=[three] * 4 + [two] * 4,
        compiler_params=pltpu.CompilerParams(vmem_limit_bytes=VMEM_LIMIT),
    )(rates, pair_got, got, *gateup, *down)
    return out[:4], out[4:]


def shards(
    mesh_shape,
    tokens_in,
    segment_ids,
    block_cotangent,
    query_weight,
    keyval_weight,
    outproj_weight,
    gateup_weight,
    down_weight,
    norm_gains,
    query_first,
    keyval_first,
    outproj_first,
    gateup_first,
    down_first,
    gains_first,
    query_second,
    keyval_second,
    outproj_second,
    gateup_second,
    down_second,
    gains_second,
    step_count,
):
    ns, nd = mesh_shape["shard"], mesh_shape["dp"]
    n = ns * nd
    s, d, m = (lax.axis_index(a) for a in ("shard", "dp", "mp"))
    me = s * nd + d
    tok, width = tokens_in.shape
    own_d = query_weight.shape[0]
    q_cols = query_weight.shape[1]
    heads_local = q_cols // HEAD_DIM
    ff_local = gateup_weight.shape[2]
    units = -(-(-(-ff_local // n)) // 128) * 128
    ff_pad = units * n - ff_local
    half = tok // 2
    plane_tok = nd * tok
    plane_d = ns * own_d

    input_rows = tokens_in.astype(F32)
    inverse_one = lax.rsqrt(jnp.mean(input_rows * input_rows, axis=1) + EPS_NORM)
    lanes = max(256, -(-max(own_d, tok) // 128) * 128)

    def line(v):
        return jnp.pad(v, ((0, 0), (0, lanes - v.shape[1])))

    small = jnp.concatenate(
        [line(norm_gains.astype(F32)), line(segment_ids.astype(F32)[None]), line(inverse_one[None]),
         jnp.zeros((4, lanes), F32)], axis=0)
    qkv_weight = jnp.concatenate(
        [query_weight, lax.dynamic_slice_in_dim(keyval_weight, m * HEAD_DIM, HEAD_DIM, 1)], axis=1)

    def plane_cut(value):
        return value.reshape(tok, ns, nd, own_d).transpose(2, 0, 1, 3).reshape(nd, tok, plane_d)

    small_all, tokens_plane, cot_all, qkv_plane, pair, single = gather(
        0, mesh_shape,
        [(small, "all"), (plane_cut(tokens_in), "swap"),
         (lax.dynamic_slice_in_dim(block_cotangent, m * half, half, 0), "all"), (qkv_weight, "z")],
        pack, (gateup_weight, down_weight.T),
        (jax.ShapeDtypeStruct((n, own_d, 2 * units), BF16), jax.ShapeDtypeStruct((n, own_d, units), BF16)))
    tokens_plane = tokens_plane.reshape(plane_tok, plane_d)

    def trade(value):
        return lax.all_to_all(value.reshape(n, own_d, -1), TOK, 0, 0, tiled=True)

    pair, tokens_plane = lax.optimization_barrier((pair, tokens_plane))
    pair = trade(pair).reshape(width, 2 * units)
    qkv_plane = qkv_plane.reshape(plane_d, q_cols + HEAD_DIM)
    small_all = small_all[:, :, 0]
    gains_by = small_all[:, :, :2, :own_d]
    full_gains = gains_by.transpose(2, 0, 1, 3).reshape(2, width)
    tags = small_all[:, :, 2, :tok].reshape(n * tok)
    plane_scale = lax.dynamic_index_in_dim(small_all[:, :, 3, :tok], s, 0, False).reshape(plane_tok, 1)
    plane_gain = lax.dynamic_index_in_dim(gains_by[:, :, 0], d, 1, False).reshape(1, plane_d)


    def from_plane(collective, value):
        got = plane_reduce(collective, mesh_shape, value.reshape(nd, 2, half, plane_d))
        return got.reshape(nd, tok, plane_d)

    def plane_terms(collective, value):
        return gather(collective, mesh_shape, [(value.reshape(nd, tok, -1), "swap")])[0]

    hidden_plane = (tokens_plane.astype(F32) * plane_scale * plane_gain).astype(BF16)
    qkv_terms = plane_terms(8, product(hidden_plane, qkv_plane).astype(BF16))

    pad = KV_BLOCKS * tok
    key_span = pad + tok
    start = me * tok
    tag_pad = jnp.concatenate([jnp.full((pad,), -1.0, F32), tags])
    key_tags = lax.dynamic_slice_in_dim(tag_pad, start, key_span, 0)
    own_tags = segment_ids.astype(F32)
    query_index = jnp.arange(tok, dtype=jnp.int32) + pad
    key_index = jnp.arange(key_span, dtype=jnp.int32)
    same_segment = key_tags[None, :] == own_tags[:, None]
    allowed = same_segment & (key_index[None, :] <= query_index[:, None])
    positions = jnp.sum(
        (same_segment & (key_index[None, :] < query_index[:, None])).astype(jnp.int32), axis=1)
    cosine, sine_rows = rope_tables(positions)
    kv_raw = jnp.sum(qkv_terms[:, :, q_cols:].astype(F32), axis=0)
    kv_mine = jnp.where(m == 0, rotate(kv_raw, cosine, sine_rows), kv_raw).astype(BF16)
    (kv_all,) = gather(1, mesh_shape, [(kv_mine, "all")])
    single, pair, kv_all = lax.optimization_barrier((single, pair, kv_all))
    single = trade(single).reshape(width, units)
    kv_all = kv_all.reshape(n, 2, tok, HEAD_DIM)
    mixed_low, queries, probs = attend(
        nd, heads_local, qkv_terms, kv_all, allowed.astype(F32), cosine, sine_rows)
    mixed_plane, outproj_z = gather(
        2, mesh_shape, [(mixed_low, "plane"), (outproj_weight.T, "z")])
    mixed_plane = mixed_plane.reshape(plane_tok, q_cols)
    outproj_plane = outproj_z.reshape(plane_d, q_cols)
    residual, hidden_two = local(
        partial(join_kernel, own_d), [((tok, width), F32), ((half, width), BF16)],
        [from_plane(9, cols_product(mixed_plane, outproj_plane).astype(BF16)), tokens_in, full_gains[1:]])

    act_low, gateup_low, pair_grad, single_grad = feed(3, mesh_shape, hidden_two, cot_all, pair, single)
    pair_grad, act_low, gateup_low = lax.optimization_barrier((pair_grad, act_low, gateup_low))
    pair_grad = trade(pair_grad)
    hidden_two_grad, ffn_sum = reduce_scatter(
        4, mesh_shape, True, (tok, width), factors=[(gateup_low, pair), (act_low, single)])
    hidden_two_grad, single_grad, pair_grad = lax.optimization_barrier((hidden_two_grad, single_grad, pair_grad))
    single_grad = trade(single_grad)
    block_out, residual_grad, attn_cut, gain_cut = local(
        partial(split_kernel, own_d),
        [((tok, width), BF16), ((tok, width), F32), ((nd, tok, plane_d), BF16), ((nd, 8, plane_d), F32)],
        [hidden_two_grad.reshape(tok, width), ffn_sum.reshape(tok, width), residual, full_gains[1:],
         block_cotangent],
        [((ROWS, width), F32)])
    attn_low, gain_two_part = gather(10, mesh_shape, [(attn_cut, "swap"), (gain_cut, "swap")])
    attn_low = attn_low.reshape(plane_tok, plane_d)
    gain_two_part = jnp.where(m == 0, jnp.sum(gain_two_part[:, 0], axis=0), 0.0)
    mixed_terms = plane_terms(11, product(attn_low, outproj_plane).astype(BF16))

    def z_sum(value):
        got = lax.all_to_all(value, "shard", 0, 0, tiled=True)
        return jnp.sum(got.astype(F32), axis=0)

    outproj_grad = rows_product(attn_low, mixed_plane).astype(BF16)
    outproj_grad, single_grad = lax.optimization_barrier((outproj_grad, single_grad))
    own_outproj = z_sum(outproj_grad.reshape(ns, own_d, q_cols))

    kv_terms, query_low = attend_back(nd, mixed_terms, kv_all, queries, probs, cosine, sine_rows)
    (kv_grad,) = reduce_scatter(6, mesh_shape, False, (2 * tok, HEAD_DIM), terms=kv_terms)
    kv_grad = kv_grad.astype(F32)
    kv_low = jnp.where(m == 0, rotate(kv_grad, cosine, -sine_rows), kv_grad)
    qkv_low = jnp.concatenate([query_low, kv_low.astype(BF16)], axis=1)
    (qkv_low_plane,) = gather(7, mesh_shape, [(qkv_low, "plane")])
    qkv_low_plane = qkv_low_plane.reshape(plane_tok, q_cols + HEAD_DIM)
    hidden_one_part = cols_product(qkv_low_plane, qkv_plane).astype(BF16)
    gain_one_part = jnp.sum(hidden_one_part.astype(F32) * (tokens_plane.astype(F32) * plane_scale), axis=0)
    hidden_one_grad = from_plane(12, hidden_one_part)
    (input_grad,) = local(
        partial(last_kernel, own_d), [((tok, width), F32)],
        [hidden_one_grad, tokens_in, full_gains[:1], residual_grad], [((ROWS, width), F32)])
    gain_parts = jnp.stack([gain_one_part, gain_two_part], axis=1)
    qkv_grad = jnp.concatenate(
        [rows_product(hidden_plane, qkv_low_plane), jnp.pad(gain_parts, ((0, 0), (0, 126)))], axis=1).astype(BF16)
    qkv_grad, own_outproj = lax.optimization_barrier((qkv_grad, own_outproj))
    own_qkv = z_sum(qkv_grad.reshape(ns, own_d, -1))
    own_query = own_qkv[:, :q_cols]
    rest = own_qkv[:, q_cols:]
    rest_other = lax.ppermute(rest, "mp", [(0, 1), (1, 0)])
    kv_own, kv_other = rest[:, :HEAD_DIM], rest_other[:, :HEAD_DIM]
    own_keyval = jnp.where(
        m == 0, jnp.concatenate([kv_own, kv_other], axis=1), jnp.concatenate([kv_other, kv_own], axis=1))
    own_gains = (rest + rest_other)[:, HEAD_DIM : HEAD_DIM + 2].T

    step_value = step_count[0].astype(F32)
    bias_first = 1.0 - jnp.power(BETA_ONE, step_value)
    bias_second = 1.0 - jnp.power(BETA_TWO, step_value)
    rates = jnp.stack([1.0 / bias_first, 1.0 / bias_second])
    gateup_news, down_news = unpack_adam(
        units, rates, pair_grad, single_grad, (gateup_weight, gateup_first, gateup_second),
        (down_weight.T, down_first.T, down_second.T))
    down_news = [x.T for x in down_news]

    def adam(grad, weight, first, second, decay):
        return (grad,) + adam_step(rates, grad, weight, first, second, decay)

    news = [
        adam(own_query, query_weight, query_first, query_second, DECAY_RATE),
        adam(own_keyval, keyval_weight, keyval_first, keyval_second, DECAY_RATE),
        tuple(v.T for v in adam(own_outproj, outproj_weight.T, outproj_first.T, outproj_second.T, DECAY_RATE)),
        gateup_news,
        down_news,
        adam(own_gains, norm_gains, gains_first, gains_second, 0.0),
    ]
    return (block_out, input_grad) + tuple(x[k] for k in range(4) for x in news)


def solution(mesh):
    rows, split_q, split_o = P(TOK, None), P(TOK, "mp"), P("mp", TOK)
    params = (split_q, rows, split_o, P(TOK, None, "mp"), split_o, P(None, TOK))
    in_specs = (rows, P(TOK), rows) + params * 3 + (P(),)
    out_specs = (rows, rows) + params * 4
    return jax.shard_map(
        partial(shards, dict(mesh.shape)), mesh=mesh, in_specs=in_specs, out_specs=out_specs, check_vma=False)
```
